512 devices in a mesh: ctx: 16 (over x, y_lo), table: 32 (over y_hi, z, core).
Axes of the slice: x: 4, y: 8 (y_hi: 2, y_lo: 4; y = y_hi * 4 + y_lo), z: 8, core: 2. Of those that a mesh axis runs over, the one named last changes fastest.
Arguments:
- item_inputs: bfloat16 [32, 2048, 512], P('table', 'ctx'), may hold values from -6 to 6
- attn_saved: bfloat16 [32, 2048, 512], P('table', 'ctx'), may hold values from -0.125 to 0.125
- out_grad: bfloat16 [32, 2048, 512], P('table', 'ctx'), may hold values from -6 to 6
- seq_lengths: int32 [32], P('table'), may hold values from 512 to 2048, as said below
- token_slot: int32 [32, 2048], P('table', 'ctx'), may hold values from 0 to 127, as said below
- slot_rows: int32 [32, 2048], P('table', 'ctx'), may hold values from 0 to 32767, as said below
- in_proj: bfloat16 [512, 2048], replicated, may hold values from -0.25 to 0.25
- out_proj: bfloat16 [512, 512], replicated, may hold values from -0.25 to 0.25
- norm_gain: float32 [512], replicated, may hold values from 0.5 to 1.5
Outputs:
- proj_grad: bfloat16 [32, 2048, 2048], P('table', 'ctx')
- table_grad: float32 [32768, 512], P(('ctx', 'table'))
The draws below stay inside these ranges and needn't reach their ends.
Inputs may be any that keep to these rules, and one draw needn't show every extreme that they name: `seq_lengths`: one history has length 2048. `token_slot`: position p names a slot of block p // 128. Slots o * 4 to o * 4 + 3 belong to table index o. In each block the named slots of one owner are a prefix of its 4 slots and every slot of that prefix is named. For every block index along the history there is an owner whose 4 slots are all named in that block of every history. `slot_rows`: entry c * 128 + s is the item row of slot s of block c. Its owner (row // 64) modulo the number of table indices is s // 4, and the 4 rows of one owner in one block differ.
All inputs are finite; a program needn't handle non-finite values.
Results may differ from the reference program's by a relative error of at most 0.0065.
Values may be sent and summed in bfloat16 or wider, within the bound.
No kernel may reach another device: no remote copies, remote signals or barrier semaphores. Data moves between devices by JAX's collectives and lax.ppermute only.
A program may use at most 64 MiB of HBM per device.

```python
import jax
import jax.numpy as jnp
from jax import lax

HEADS = 4
DH = 128
D = 512
TOK_DEV = 128
L = 2048
NSEQ = 32
CAP = 4
S_DEV = 128
ROWS_DEV = 64
VOCAB = 32768
N_CTX = 16
N_TABLE = 32


def slot_counts(key):
    key_count, key_pick = jax.random.split(key)
    counts = jax.random.randint(key_count, (NSEQ, N_CTX, N_TABLE), 1, CAP + 1)
    chosen = jax.random.randint(key_pick, (N_CTX,), 0, N_TABLE)
    filled = jnp.arange(N_TABLE)[None, None, :] == chosen[None, :, None]
    return jnp.where(filled, CAP, counts)


def draw_seq_lengths(key, part):
    key = jax.random.fold_in(key, 11)
    key_len, key_top = jax.random.split(key)
    lengths = jax.random.randint(key_len, (NSEQ,), L // 4, L + 1)
    longest = jax.random.randint(key_top, (), 0, NSEQ)
    return jnp.where(jnp.arange(NSEQ) == longest, L, lengths).astype(jnp.int32)


def draw_token_slot(key, part):
    counts = slot_counts(key)
    key = jax.random.fold_in(key, 7)
    key_owner, key_level, key_order = jax.random.split(key, 3)
    shape_all = (NSEQ, N_CTX, TOK_DEV)
    slot_ids = jnp.arange(TOK_DEV)
    owner_of = jnp.minimum(slot_ids // CAP, N_TABLE - 1)
    level_of = slot_ids - owner_of * CAP
    count_at = jnp.take_along_axis(counts, jnp.broadcast_to(owner_of, shape_all), axis=2)
    direct = (slot_ids < S_DEV) & (level_of < count_at)
    spare_owner = jax.random.randint(key_owner, shape_all, 0, N_TABLE)
    spare_count = jnp.take_along_axis(counts, spare_owner, axis=2)
    spare_level = jax.random.randint(key_level, shape_all, 0, 1 << 20) % spare_count
    chosen_slot = jnp.where(direct, slot_ids, spare_owner * CAP + spare_level)
    ranking = jax.random.randint(key_order, shape_all, 0, 1 << 20) * TOK_DEV + slot_ids
    shuffle = jnp.argsort(ranking, axis=2)
    mixed = jnp.take_along_axis(chosen_slot, shuffle, axis=2)
    return mixed.reshape(NSEQ, L).astype(jnp.int32)


def draw_slot_rows(key, part):
    key = jax.random.fold_in(key, 13)
    key_base, key_step = jax.random.split(key)
    pool_size = N_CTX * ROWS_DEV
    offsets = jax.random.randint(key_base, (NSEQ, N_CTX, N_TABLE, 1), 0, pool_size)
    stride = 2 * jax.random.randint(key_step, (NSEQ, N_CTX, N_TABLE, 1), 0, pool_size // 2) + 1
    levels = jnp.arange(CAP)[None, None, None, :]
    pooled = (offsets + levels * stride) % pool_size
    owners = jnp.arange(N_TABLE)[None, None, :, None]
    row_ids = (pooled // ROWS_DEV * N_TABLE + owners) * ROWS_DEV + pooled % ROWS_DEV
    return row_ids.reshape(NSEQ, N_CTX * S_DEV).astype(jnp.int32)


def block_levels(rng, extent, cuts, smallest, high):
    def one(dim, shards_of):
        heights = jax.random.uniform(jax.random.fold_in(jax.random.fold_in(rng, 6), dim), (shards_of,), jnp.float32, smallest / len(cuts), high / len(cuts))
        return jnp.repeat(jnp.exp(heights), extent[dim] // shards_of).reshape((-1,) + (1,) * (len(extent) - dim - 1))

    factor_of = one(*cuts[0])
    for cut in cuts[1:]:
        factor_of = factor_of * one(*cut)
    return factor_of


def normal_values(own_key, dims, spread, most, cuts=(), kind=jnp.bfloat16):
    array = spread * jax.random.normal(own_key, dims, jnp.float32)
    if cuts:
        array = array * block_levels(own_key, dims, cuts, -0.22, 0.18)
    return jnp.clip(array, -most, most).astype(kind)


def setup_inputs(seed: int = 0) -> dict:
    seeds = jax.random.split(jax.random.key(seed), 10)
    item_inputs = normal_values(seeds[0], (NSEQ, L, D), 1.0, 6.0, ((0, 32), (1, 16)))
    attn_saved = normal_values(seeds[1], (NSEQ, L, D), 0.02, 0.125, ((0, 32), (1, 16)))
    out_grad = normal_values(seeds[2], (NSEQ, L, D), 1.0, 6.0, ((0, 32), (1, 16)))
    seq_lengths = draw_seq_lengths(jax.random.fold_in(seeds[9], 71), 0)
    token_slot = draw_token_slot(jax.random.fold_in(seeds[9], 71), 0)
    slot_rows = draw_slot_rows(jax.random.fold_in(seeds[9], 71), 0)
    in_proj = normal_values(seeds[6], (D, 4 * D), D ** -0.5, 0.25)
    out_proj = normal_values(seeds[7], (D, D), D ** -0.5, 0.25)
    norm_gain = jnp.clip(1.0 + 0.1 * jax.random.normal(seeds[8], (D,), jnp.float32), 0.5, 1.5)
    return dict(item_inputs=item_inputs, attn_saved=attn_saved, out_grad=out_grad, seq_lengths=seq_lengths, token_slot=token_slot, slot_rows=slot_rows, in_proj=in_proj, out_proj=out_proj, norm_gain=norm_gain)


def silu_slope(value):
    squash = jax.nn.sigmoid(value)
    return squash * (1.0 + value * (1.0 - squash))

def reference(item_inputs, attn_saved, out_grad, seq_lengths, token_slot, slot_rows, in_proj, out_proj, norm_gain):
    scale = DH ** (-0.5)

    def one_sequence(packed):
        inputs_one, saved_one, grad_one, length = packed
        length_f = length.astype(jnp.float32)
        pre_act = jnp.dot(inputs_one, in_proj, preferred_element_type=jnp.float32)
        hidden = jax.nn.silu(pre_act).astype(jnp.bfloat16)
        gating = hidden[:, :D].astype(jnp.float32)
        values = hidden[:, D:2 * D].astype(jnp.float32).reshape(L, HEADS, DH)
        queries = hidden[:, 2 * D:3 * D].astype(jnp.float32).reshape(L, HEADS, DH)
        key_rows = hidden[:, 3 * D:].astype(jnp.float32).reshape(L, HEADS, DH)
        back = jnp.dot(grad_one, out_proj.T, preferred_element_type=jnp.float32)
        saved = saved_one.astype(jnp.float32)
        row_mean = lax.optimization_barrier(jnp.mean(saved, axis=1, keepdims=True))
        centred = saved - row_mean
        inv_std = lax.rsqrt(lax.optimization_barrier(jnp.mean(centred * centred, axis=1, keepdims=True)) + 1e-05)
        normed = centred * inv_std
        gating_grad = back * (normed * norm_gain)
        carried = back * gating * norm_gain
        out_attn = inv_std * (carried - lax.optimization_barrier(jnp.mean(carried, axis=1, keepdims=True)) - normed * lax.optimization_barrier(jnp.mean(carried * normed, axis=1, keepdims=True)))
        out_attn = out_attn.astype(jnp.bfloat16).astype(jnp.float32).reshape(L, HEADS, DH)
        scores = jnp.einsum('ihd,jhd->hij', queries, key_rows) * scale
        positions = jnp.arange(L, dtype=jnp.int32)
        live = (positions[None, :] <= positions[:, None]) & (positions[:, None] < length) & (positions[None, :] < length)
        weight = jnp.where(live, 1.0 / length_f, 0.0)
        squash = jax.nn.sigmoid(scores)
        attend = (scores * squash * weight).astype(jnp.bfloat16).astype(jnp.float32)
        attn_grad = jnp.einsum('ihd,jhd->hij', out_attn, values)
        score_grad = (attn_grad * squash * (1.0 + scores * (1.0 - squash)) * weight).astype(jnp.bfloat16).astype(jnp.float32)
        value_grad = jnp.einsum('hij,ihd->jhd', attend, out_attn).reshape(L, D)
        query_grad = (jnp.einsum('hij,jhd->ihd', score_grad, key_rows) * scale).reshape(L, D)
        key_grad = (jnp.einsum('hij,ihd->jhd', score_grad, queries) * scale).reshape(L, D)
        joined = jnp.concatenate([gating_grad, value_grad, query_grad, key_grad], axis=1)
        proj_one = (joined * silu_slope(pre_act)).astype(jnp.bfloat16)
        input_grad = grad_one.astype(jnp.float32) + jnp.dot(proj_one, in_proj.T, preferred_element_type=jnp.float32)
        return (proj_one, input_grad)
    proj_grad, input_grad = lax.map(one_sequence, (item_inputs, attn_saved, out_grad, seq_lengths))
    item_row = jnp.take_along_axis(slot_rows.reshape(NSEQ, N_CTX, S_DEV), token_slot.reshape(NSEQ, N_CTX, TOK_DEV), axis=2)
    table_grad = jax.ops.segment_sum(input_grad.reshape(NSEQ * L, D), item_row.reshape(NSEQ * L).astype(jnp.int32), num_segments=VOCAB)
    return (proj_grad, table_grad)
```

```python
import functools

import jax
import jax.numpy as jnp
from jax import lax
from jax.experimental import pallas as pl
from jax.experimental.pallas import tpu as pltpu
from jax.sharding import PartitionSpec as P

HEADS = 4
HEAD_DIM = 128
WIDTH = 512
TOKENS = 128
ROWS_DEV = 64
TABLES = 32
CAP = 4
SUM_ROWS = CAP * WIDTH // 128
SEND_ROWS = SUM_ROWS + 8
X_COUNT = 4
Y_COUNT = 4
VMEM_LIMIT = 48 * 1024 * 1024
ALL_VMEM = 63 * 1024 * 1024
BF16 = jnp.bfloat16
F32 = jnp.float32

X_GROUPS = [[x * Y_COUNT + y for x in range(X_COUNT)] for y in range(Y_COUNT)]
Y_GROUPS = [[x * Y_COUNT + y for y in range(Y_COUNT)] for x in range(X_COUNT)]
SWAP_QUERY = [(c, c ^ 2) for c in range(X_COUNT * Y_COUNT)]
SWAP_KEY = [(c, c ^ 1) for c in range(X_COUNT * Y_COUNT)]

MATMUL = (((1,), (0,)), ((), ()))
MATMUL_NT = (((1,), (1,)), ((), ()))
MATMUL_TN = (((0,), (0,)), ((), ()))


def dot(lhs, rhs, dims):
    return lax.dot_general(lhs, rhs, dims, preferred_element_type=F32)


def in_vmem(count):
    return [pl.BlockSpec(memory_space=pltpu.VMEM)] * count


def in_smem():
    return pl.BlockSpec(memory_space=pltpu.SMEM)


def in_hbm(count):
    return [pl.BlockSpec(memory_space=pltpu.HBM)] * count


def params(limit=VMEM_LIMIT):
    return pltpu.CompilerParams(vmem_limit_bytes=limit)


def project_kernel(
    length_ref,
    inputs_hbm,
    saved_hbm,
    grad_hbm,
    in_proj_hbm,
    out_proj_hbm,
    gain_hbm,
    parts_ref,
    slope_ref,
    gate_ref,
    base_ref,
    inputs_ref,
    saved_ref,
    grad_ref,
    in_proj_ref,
    out_proj_ref,
    gain_ref,
    sems,
):
    def copy_of(place, source, target):
        copy = pltpu.make_async_copy(source, target, sems.at[place])
        copy.start()
        return copy

    saved_copy = copy_of(0, saved_hbm, saved_ref)
    grad_copy = copy_of(1, grad_hbm, grad_ref)
    gain_copy = copy_of(2, gain_hbm, gain_ref)
    out_copy = copy_of(3, out_proj_hbm, out_proj_ref)
    inputs_copy = copy_of(4, inputs_hbm, inputs_ref)
    in_copies = [
        copy_of(
            5 + block,
            in_proj_hbm.at[:, block * WIDTH : (block + 1) * WIDTH],
            in_proj_ref.at[block],
        )
        for block in range(4)
    ]
    first = lax.axis_index("ctx") * TOKENS
    length = length_ref[0]
    saved_copy.wait()
    saved = saved_ref[...].astype(F32)
    row_mean = jnp.mean(saved, axis=1, keepdims=True)
    centred = saved - row_mean
    inv_std = lax.rsqrt(jnp.mean(centred * centred, axis=1, keepdims=True) + 1e-05)
    normed = centred * inv_std
    grad_copy.wait()
    gain_copy.wait()
    out_copy.wait()
    gain = gain_ref[...]
    grad = grad_ref[...]
    back = dot(grad, out_proj_ref[...], MATMUL_NT)

    inputs_copy.wait()
    in_copies[0].wait()
    inputs = inputs_ref[...]
    pre = dot(inputs, in_proj_ref[0], MATMUL)
    squash = jax.nn.sigmoid(pre)
    gating = (pre * squash).astype(BF16).astype(F32)
    gate = (back * (normed * gain) * (squash * (1.0 + pre * (1.0 - squash)))).astype(BF16)
    gate_ref[...] = gate
    base_ref[...] = grad.astype(F32) + dot(gate, in_proj_ref[0], MATMUL_NT)

    carried = back * gating * gain
    out_attn = inv_std * (
        carried
        - jnp.mean(carried, axis=1, keepdims=True)
        - normed * jnp.mean(carried * normed, axis=1, keepdims=True)
    )
    position = first + lax.broadcasted_iota(jnp.int32, (TOKENS, 1), 0)
    out_attn = jnp.where(position < length, out_attn, 0.0).astype(BF16)
    for head in range(HEADS):
        cols = slice(head * HEAD_DIM, (head + 1) * HEAD_DIM)
        parts_ref[head, :, HEAD_DIM : 2 * HEAD_DIM] = out_attn[:, cols]
    for block, place in ((1, 3), (2, 0), (3, 2)):
        in_copies[block].wait()
        pre = dot(inputs, in_proj_ref[block], MATMUL)
        squash = jax.nn.sigmoid(pre)
        slope_ref[:, (block - 1) * WIDTH : block * WIDTH] = squash * (1.0 + pre * (1.0 - squash))
        hidden = (pre * squash).astype(BF16)
        for head in range(HEADS):
            cols = slice(head * HEAD_DIM, (head + 1) * HEAD_DIM)
            parts_ref[head, :, place * HEAD_DIM : (place + 1) * HEAD_DIM] = hidden[:, cols]


def project(length, inputs, saved, grad, in_proj, out_proj, gain):
    return pl.pallas_call(
        project_kernel,
        out_shape=(
            jax.ShapeDtypeStruct((HEADS, TOKENS, 4 * HEAD_DIM), BF16),
            jax.ShapeDtypeStruct((TOKENS, 3 * WIDTH), F32),
            jax.ShapeDtypeStruct((TOKENS, WIDTH), BF16),
            jax.ShapeDtypeStruct((TOKENS, WIDTH), F32),
        ),
        in_specs=[in_smem()] + in_hbm(6),
        out_specs=tuple(in_vmem(4)),
        scratch_shapes=[
            pltpu.VMEM((TOKENS, WIDTH), BF16),
            pltpu.VMEM((TOKENS, WIDTH), BF16),
            pltpu.VMEM((TOKENS, WIDTH), BF16),
            pltpu.VMEM((4, WIDTH, WIDTH), BF16),
            pltpu.VMEM((WIDTH, WIDTH), BF16),
            pltpu.VMEM((1, WIDTH), F32),
            pltpu.SemaphoreType.DMA((9,)),
        ],
        compiler_params=params(ALL_VMEM),
        name="project",
    )(length, inputs, saved, grad, in_proj, out_proj, gain)


def tile_grads(queries, outs, keys, values, weight, live):
    scale = HEAD_DIM ** (-0.5)
    scores = dot(queries, keys, MATMUL_NT) * scale
    attn_grad = dot(outs, values, MATMUL_NT)
    squash = jax.nn.sigmoid(scores)
    weighted = squash * weight
    if live is not None:
        weighted = jnp.where(live, weighted, 0.0)
    attend = (scores * weighted).astype(BF16)
    score_grad = (attn_grad * weighted * (1.0 + scores * (1.0 - squash))).astype(BF16)
    return (
        dot(score_grad, keys, MATMUL) * scale,
        dot(score_grad, queries, MATMUL_TN) * scale,
        dot(attend, outs, MATMUL_TN),
    )


def attend_rows(length_ref, query_of, out_of, own_ref, key_far_ref, query_class, take_query, take_key):
    lane = lax.rem(lax.axis_index("ctx"), Y_COUNT)
    weight = jnp.full((1, 1), 1.0, F32) / jnp.full((1, 1), length_ref[0].astype(F32), F32)
    rows = lax.broadcasted_iota(jnp.int32, (TOKENS, 1), 0)
    columns = lax.broadcasted_iota(jnp.int32, (1, 2 * TOKENS), 1)
    row_pos = (lane ^ query_class) * TOKENS + rows
    column_pos = jnp.where(
        columns < TOKENS, lane * TOKENS + columns, (lane ^ 1) * TOKENS + columns - TOKENS
    )
    live = column_pos <= row_pos
    keys, values = [], []
    for x in range(X_COUNT):
        keys.append(
            jnp.concatenate(
                [own_ref[x, :, 2 * HEAD_DIM : 3 * HEAD_DIM], key_far_ref[x, :, :HEAD_DIM]], axis=0
            )
        )
        values.append(
            jnp.concatenate([own_ref[x, :, 3 * HEAD_DIM :], key_far_ref[x, :, HEAD_DIM:]], axis=0)
        )
    for query_x in range(X_COUNT):
        queries, outs = query_of(query_x), out_of(query_x)
        query_acc = None
        for key_x in range(query_x + 1):
            query_part, key_part, value_part = tile_grads(
                queries, outs, keys[key_x], values[key_x], weight, live if query_x == key_x else None
            )
            query_acc = query_part if query_acc is None else query_acc + query_part
            take_key(query_x, key_x, key_part, value_part)
        take_query(query_x, query_acc)


def attend_own_kernel(length_ref, own_ref, key_far_ref, query_ref, key_ref):
    def take_query(x, part):
        query_ref[x] = part

    def take_key(query_x, x, key_part, value_part):
        if query_x == x:
            key_ref[x, :, :HEAD_DIM] = key_part
            key_ref[x, :, HEAD_DIM:] = value_part
        else:
            key_ref[x, :, :HEAD_DIM] += key_part
            key_ref[x, :, HEAD_DIM:] += value_part

    attend_rows(
        length_ref,
        lambda x: own_ref[x, :, :HEAD_DIM],
        lambda x: own_ref[x, :, HEAD_DIM : 2 * HEAD_DIM],
        own_ref,
        key_far_ref,
        0,
        take_query,
        take_key,
    )


def attend_far_kernel(
    length_ref, own_ref, query_far_ref, key_far_ref, sums_ref, query_ref, key_own_ref, key_send_ref, acc_ref
):
    def take_query(x, part):
        query_ref[x] = part.astype(BF16)

    def take_key(query_x, x, key_part, value_part):
        source = sums_ref if query_x == x else acc_ref
        acc_ref[x, :, :HEAD_DIM] = source[x, :, :HEAD_DIM] + key_part
        acc_ref[x, :, HEAD_DIM:] = source[x, :, HEAD_DIM:] + value_part

    attend_rows(
        length_ref,
        lambda x: query_far_ref[x, :, :HEAD_DIM],
        lambda x: query_far_ref[x, :, HEAD_DIM:],
        own_ref,
        key_far_ref,
        2,
        take_query,
        take_key,
    )
    key_own_ref[...] = acc_ref[:, :TOKENS, :]
    key_send_ref[...] = acc_ref[:, TOKENS:, :].astype(BF16)


ATTEND_COST = pl.CostEstimate(
    flops=10 * 5 * 2 * 128 * 256 * 128, bytes_accessed=2 << 20, transcendentals=10 * 128 * 256
)


def attend_own(length, own, key_far):
    return pl.pallas_call(
        attend_own_kernel,
        out_shape=(
            jax.ShapeDtypeStruct((X_COUNT, TOKENS, HEAD_DIM), F32),
            jax.ShapeDtypeStruct((X_COUNT, 2 * TOKENS, 2 * HEAD_DIM), F32),
        ),
        in_specs=[in_smem()] + in_vmem(2),
        out_specs=tuple(in_vmem(2)),
        compiler_params=params(),
        cost_estimate=ATTEND_COST,
        name="attend_own",
    )(length, own, key_far)


def attend_far(length, own, query_far, key_far, sums):
    return pl.pallas_call(
        attend_far_kernel,
        out_shape=(
            jax.ShapeDtypeStruct((X_COUNT, TOKENS, HEAD_DIM), BF16),
            jax.ShapeDtypeStruct((X_COUNT, TOKENS, 2 * HEAD_DIM), F32),
            jax.ShapeDtypeStruct((X_COUNT, TOKENS, 2 * HEAD_DIM), BF16),
        ),
        in_specs=[in_smem()] + in_vmem(4),
        out_specs=tuple(in_vmem(3)),
        scratch_shapes=[pltpu.VMEM((X_COUNT, 2 * TOKENS, 2 * HEAD_DIM), F32)],
        compiler_params=params(),
        cost_estimate=ATTEND_COST,
        name="attend_far",
    )(length, own, query_far, key_far, sums)


def join_kernel(query_own_ref, query_got_ref, key_own_ref, key_got_ref, out_ref):
    out_ref[:, :, :HEAD_DIM] = (
        key_own_ref[:, :, HEAD_DIM:] + key_got_ref[:, :, HEAD_DIM:].astype(F32)
    ).astype(BF16)
    out_ref[:, :, HEAD_DIM : 2 * HEAD_DIM] = (
        query_own_ref[...] + query_got_ref[...].astype(F32)
    ).astype(BF16)
    out_ref[:, :, 2 * HEAD_DIM :] = (
        key_own_ref[:, :, :HEAD_DIM] + key_got_ref[:, :, :HEAD_DIM].astype(F32)
    ).astype(BF16)


def join_parts(query_own, query_got, key_own, key_got):
    return pl.pallas_call(
        join_kernel,
        out_shape=jax.ShapeDtypeStruct((X_COUNT, TOKENS, 3 * HEAD_DIM), BF16),
        in_specs=in_vmem(4),
        out_specs=in_vmem(1)[0],
        compiler_params=params(),
        name="join_parts",
    )(query_own, query_got, key_own, key_got)


def finish_kernel(
    grads_ref,
    slope_ref,
    gate_ref,
    base_ref,
    in_proj_ref,
    slot_ref,
    item_ref,
    proj_ref,
    rows_ref,
    wide_ref,
):
    proj_ref[:, :WIDTH] = gate_ref[...]
    for block in range(3):
        joined = jnp.concatenate(
            [
                grads_ref[head, :, block * HEAD_DIM : (block + 1) * HEAD_DIM].astype(F32)
                for head in range(HEADS)
            ],
            axis=1,
        )
        cols = slice((block + 1) * WIDTH, (block + 2) * WIDTH)
        proj_ref[:, cols] = (joined * slope_ref[:, block * WIDTH : (block + 1) * WIDTH]).astype(
            BF16
        )
    input_grad = base_ref[...] + dot(proj_ref[:, WIDTH:], in_proj_ref[:, WIDTH:], MATMUL_NT)
    high = input_grad.astype(BF16)
    low = (input_grad - high.astype(F32)).astype(BF16)
    order = lax.broadcasted_iota(jnp.int32, (TABLES * CAP, 1), 0)
    slot_of = (order % TABLES) * CAP + order // TABLES
    picks = (slot_ref[...] == slot_of).astype(F32).astype(BF16)
    summed = dot(picks, high, MATMUL) + dot(picks, low, MATMUL)
    for level in range(CAP):
        for chunk in range(WIDTH // 128):
            wide_ref[pl.ds(level * 4 + chunk, TABLES, stride=SEND_ROWS), :] = summed[
                level * TABLES : (level + 1) * TABLES, chunk * 128 : (chunk + 1) * 128
            ]
    items = item_ref[...]
    owner_of = (items // (ROWS_DEV * TABLES)).astype(F32)
    place_of = (items % ROWS_DEV).astype(F32)
    slot = lax.broadcasted_iota(jnp.int32, (TABLES, TABLES * CAP), 1)
    owner = lax.broadcasted_iota(jnp.int32, (TABLES, TABLES * CAP), 0)
    coded = jnp.zeros((TABLES, 128), F32)
    for level in range(CAP):
        match = slot == owner * CAP + level
        for value, lane in ((owner_of, level), (place_of, CAP + level)):
            column = jnp.sum(jnp.where(match, value, 0.0), axis=1, keepdims=True)
            coded = jnp.where(slot == lane, column, coded)
    wide_ref[pl.ds(SUM_ROWS, TABLES, stride=SEND_ROWS), :] = coded
    for row in range(SUM_ROWS + 1, SEND_ROWS):
        wide_ref[pl.ds(row, TABLES, stride=SEND_ROWS), :] = jnp.zeros((TABLES, 128), F32)
    rows_ref[...] = wide_ref[...].astype(BF16)


def finish(grads, slope, gate, base, in_proj, slots, items):
    return pl.pallas_call(
        finish_kernel,
        out_shape=(
            jax.ShapeDtypeStruct((TOKENS, 4 * WIDTH), BF16),
            jax.ShapeDtypeStruct((TABLES * SEND_ROWS, 128), BF16),
        ),
        in_specs=in_vmem(7),
        out_specs=tuple(in_vmem(2)),
        scratch_shapes=[pltpu.VMEM((TABLES * SEND_ROWS, 128), F32)],
        compiler_params=params(),
        name="finish",
    )(grads, slope, gate, base, in_proj, slots, items)


def scatter_kernel(rows_ref, out_ref, wide_ref):
    targets = Y_COUNT * ROWS_DEV
    count = X_COUNT * TABLES
    first = lax.div(lax.axis_index("ctx"), Y_COUNT) * targets
    wide_ref[...] = rows_ref[...].astype(F32)
    coded = wide_ref[pl.ds(SUM_ROWS, count, stride=SEND_ROWS), :].T
    ids = (coded[:CAP] * ROWS_DEV + coded[CAP : 2 * CAP]).astype(jnp.int32)
    target = first + lax.broadcasted_iota(jnp.int32, (targets, 1), 0)
    hots = [(ids[level : level + 1, :] == target).astype(F32).astype(BF16) for level in range(CAP)]
    for chunk in range(WIDTH // 128):
        total = None
        for level in range(CAP):
            rows = wide_ref[pl.ds(level * 4 + chunk, count, stride=SEND_ROWS), :].astype(BF16)
            part = dot(hots[level], rows, MATMUL)
            total = part if total is None else total + part
        out_ref[:, chunk * 128 : (chunk + 1) * 128] = total.astype(BF16)


def scatter_rows(rows):
    return pl.pallas_call(
        scatter_kernel,
        out_shape=jax.ShapeDtypeStruct((Y_COUNT * ROWS_DEV, WIDTH), BF16),
        in_specs=in_vmem(1),
        out_specs=in_vmem(1)[0],
        scratch_shapes=[pltpu.VMEM((X_COUNT * TABLES * SEND_ROWS, 128), F32)],
        compiler_params=params(),
        name="scatter_rows",
    )(rows)


def per_device(
    item_inputs,
    attn_saved,
    out_grad,
    seq_lengths,
    token_slot,
    slot_rows,
    in_proj,
    out_proj,
    norm_gain,
):
    parts, slope, gate, base = project(
        seq_lengths, item_inputs[0], attn_saved[0], out_grad[0], in_proj, out_proj, norm_gain[None]
    )
    own = lax.all_to_all(parts, "ctx", 0, 0, axis_index_groups=X_GROUPS)
    key_far = lax.ppermute(own[:, :, 2 * HEAD_DIM :], "ctx", SWAP_KEY)
    query_far = lax.ppermute(own[:, :, : 2 * HEAD_DIM], "ctx", SWAP_QUERY)
    query_own, sums = attend_own(seq_lengths, own, key_far)
    query_send, key_own, key_send = attend_far(seq_lengths, own, query_far, key_far, sums)
    key_got = lax.ppermute(key_send, "ctx", SWAP_KEY)
    query_got = lax.ppermute(query_send, "ctx", SWAP_QUERY)
    joined = join_parts(query_own, query_got, key_own, key_got)
    grads = lax.all_to_all(joined, "ctx", 0, 0, axis_index_groups=X_GROUPS)
    proj_grad, rows = finish(grads, slope, gate, base, in_proj, token_slot, slot_rows)
    rows = lax.all_to_all(rows.reshape(TABLES, SEND_ROWS, 128), "table", 0, 0)
    rows = lax.all_gather(rows, "ctx", axis_index_groups=X_GROUPS)
    dense = scatter_rows(rows.reshape(X_COUNT * TABLES * SEND_ROWS, 128))
    pieces = lax.all_to_all(
        dense.reshape(Y_COUNT, ROWS_DEV, WIDTH), "ctx", 0, 0, axis_index_groups=Y_GROUPS
    )
    table_grad = jnp.sum(pieces.astype(F32), axis=0)
    return (proj_grad[None], table_grad)


def solution(mesh):
    return jax.shard_map(
        per_device,
        mesh=mesh,
        in_specs=(
            P("table", "ctx", None),
            P("table", "ctx", None),
            P("table", "ctx", None),
            P("table"),
            P("table", "ctx"),
            P("table", "ctx"),
            P(),
            P(),
            P(),
        ),
        out_specs=(P("table", "ctx", None), P(("ctx", "table"), None)),
        check_vma=False,
    )
```

```python
import functools

import jax
import jax.numpy as jnp
from jax import lax
from jax.experimental import pallas as pl
from jax.experimental.pallas import tpu as pltpu
from jax.sharding import PartitionSpec as P

HEADS = 4
HEAD_DIM = 128
WIDTH = 512
TOKENS = 128
ROWS_DEV = 64
TABLES = 32
CAP = 4
SUM_ROWS = CAP * WIDTH // 128
SEND_ROWS = SUM_ROWS + 8
GIVE_SUMS = TABLES * SUM_ROWS
GIVE_ROWS = GIVE_SUMS + 16
X_COUNT = 4
Y_COUNT = 4
TILE = 2 * TOKENS
VMEM_LIMIT = 48 * 1024 * 1024
BF16 = jnp.bfloat16
F32 = jnp.float32

X_PAIRS = ((0, 3), (1, 2))
HEAD_GROUPS = [
    [X_PAIRS[pair][place] * Y_COUNT + upper * 2 + parity for place in range(2) for parity in range(2)]
    for pair in range(2)
    for upper in range(2)
]
X_GROUPS = [[x * Y_COUNT + y for x in range(X_COUNT)] for y in range(Y_COUNT)]
Y_GROUPS = [[x * Y_COUNT + y for y in range(Y_COUNT)] for x in range(X_COUNT)]
SWAP_QUERY = [(c, c ^ 2) for c in range(X_COUNT * Y_COUNT)]
SWAP_KEY = [(c, c ^ Y_COUNT) for c in range(X_COUNT * Y_COUNT)]

MATMUL = (((1,), (0,)), ((), ()))
MATMUL_NT = (((1,), (1,)), ((), ()))
MATMUL_TN = (((0,), (0,)), ((), ()))


def dot(lhs, rhs, dims):
    return lax.dot_general(lhs, rhs, dims, preferred_element_type=F32)


def in_vmem(count):
    return [pl.BlockSpec(memory_space=pltpu.VMEM)] * count


def in_smem():
    return pl.BlockSpec(memory_space=pltpu.SMEM)


def in_hbm(count):
    return [pl.BlockSpec(memory_space=pltpu.HBM)] * count


def params(limit=VMEM_LIMIT):
    return pltpu.CompilerParams(vmem_limit_bytes=limit)


def project_kernel(
    length_ref,
    inputs_hbm,
    saved_hbm,
    grad_hbm,
    in_proj_hbm,
    out_proj_hbm,
    gain_hbm,
    parts_ref,
    slope_ref,
    gate_ref,
    base_ref,
    inputs_ref,
    saved_ref,
    grad_ref,
    in_proj_ref,
    out_proj_ref,
    gain_ref,
    sems,
):
    def copy_of(place, source, target):
        copy = pltpu.make_async_copy(source, target, sems.at[place])
        copy.start()
        return copy

    saved_copy = copy_of(0, saved_hbm, saved_ref)
    grad_copy = copy_of(1, grad_hbm, grad_ref)
    gain_copy = copy_of(2, gain_hbm, gain_ref)
    out_copy = copy_of(3, out_proj_hbm, out_proj_ref)
    inputs_copy = copy_of(4, inputs_hbm, inputs_ref)
    in_copies = [
        copy_of(
            5 + block,
            in_proj_hbm.at[:, block * WIDTH : (block + 1) * WIDTH],
            in_proj_ref.at[block],
        )
        for block in range(4)
    ]
    first = lax.axis_index("ctx") * TOKENS
    length = length_ref[0]
    saved_copy.wait()
    saved = saved_ref[...].astype(F32)
    row_mean = jnp.mean(saved, axis=1, keepdims=True)
    centred = saved - row_mean
    inv_std = lax.rsqrt(jnp.mean(centred * centred, axis=1, keepdims=True) + 1e-05)
    normed = centred * inv_std
    grad_copy.wait()
    gain_copy.wait()
    out_copy.wait()
    gain = gain_ref[...]
    grad = grad_ref[...]
    back = dot(grad, out_proj_ref[...], MATMUL_NT)

    inputs_copy.wait()
    in_copies[0].wait()
    inputs = inputs_ref[...]
    pre = dot(inputs, in_proj_ref[0], MATMUL)
    squash = jax.nn.sigmoid(pre)
    gating = (pre * squash).astype(BF16).astype(F32)
    gate = (back * (normed * gain) * (squash * (1.0 + pre * (1.0 - squash)))).astype(BF16)
    gate_ref[...] = gate
    base_ref[...] = grad.astype(F32) + dot(gate, in_proj_ref[0], MATMUL_NT)

    carried = back * gating * gain
    out_attn = inv_std * (
        carried
        - jnp.mean(carried, axis=1, keepdims=True)
        - normed * jnp.mean(carried * normed, axis=1, keepdims=True)
    )
    position = first + lax.broadcasted_iota(jnp.int32, (TOKENS, 1), 0)
    out_attn = jnp.where(position < length, out_attn, 0.0).astype(BF16)
    for head in range(HEADS):
        cols = slice(head * HEAD_DIM, (head + 1) * HEAD_DIM)
        parts_ref[head, :, HEAD_DIM : 2 * HEAD_DIM] = out_attn[:, cols]
    for block, place in ((1, 3), (2, 0), (3, 2)):
        in_copies[block].wait()
        pre = dot(inputs, in_proj_ref[block], MATMUL)
        squash = jax.nn.sigmoid(pre)
        slope_ref[:, (block - 1) * WIDTH : block * WIDTH] = squash * (1.0 + pre * (1.0 - squash))
        hidden = (pre * squash).astype(BF16)
        for head in range(HEADS):
            cols = slice(head * HEAD_DIM, (head + 1) * HEAD_DIM)
            parts_ref[head, :, place * HEAD_DIM : (place + 1) * HEAD_DIM] = hidden[:, cols]


def project(length, *arrays):
    return pl.pallas_call(
        project_kernel,
        out_shape=(
            jax.ShapeDtypeStruct((HEADS, TOKENS, 4 * HEAD_DIM), BF16),
            jax.ShapeDtypeStruct((TOKENS, 3 * WIDTH), F32),
            jax.ShapeDtypeStruct((TOKENS, WIDTH), BF16),
            jax.ShapeDtypeStruct((TOKENS, WIDTH), F32),
        ),
        in_specs=[in_smem()] + in_hbm(6),
        out_specs=tuple(in_vmem(4)),
        scratch_shapes=[
            pltpu.VMEM((TOKENS, WIDTH), BF16),
            pltpu.VMEM((TOKENS, WIDTH), BF16),
            pltpu.VMEM((TOKENS, WIDTH), BF16),
            pltpu.VMEM((4, WIDTH, WIDTH), BF16),
            pltpu.VMEM((WIDTH, WIDTH), BF16),
            pltpu.VMEM((1, WIDTH), F32),
            pltpu.SemaphoreType.DMA((9,)),
        ],
        compiler_params=params(),
        name="project",
    )(length, *(pltpu.with_memory_space_constraint(array, pltpu.HBM) for array in arrays))


def tile_grads(query_ref, query_place, key_ref, key_place, key_column, weight, live):
    scale = HEAD_DIM ** (-0.5)
    queries = query_ref[query_place, :, :HEAD_DIM]
    outs = query_ref[query_place, :, HEAD_DIM : 2 * HEAD_DIM]
    keys = key_ref[key_place, :, key_column : key_column + HEAD_DIM]
    values = key_ref[key_place, :, key_column + HEAD_DIM : key_column + 2 * HEAD_DIM]
    scores = dot(keys, queries, MATMUL_NT) * scale
    attn_grad = dot(values, outs, MATMUL_NT)
    squash = 0.5 + 0.5 * jnp.tanh(scores * 0.5)
    weighted = squash * weight
    if live is not None:
        weighted = jnp.where(live, weighted, 0.0)
    gated = scores * weighted
    attend = gated.astype(BF16)
    score_grad = (attn_grad * (weighted + gated * (1.0 - squash))).astype(BF16)
    return (
        dot(score_grad, keys, MATMUL_TN) * scale,
        dot(score_grad, queries, MATMUL) * scale,
        dot(attend, outs, MATMUL),
    )


def place_of_device():
    ctx = lax.axis_index("ctx")
    x = lax.div(ctx, Y_COUNT)
    return (x ^ lax.div(x, 2)) & 1, lax.div(lax.rem(ctx, Y_COUNT), 2)


def weight_of(length_ref):
    return jnp.full((1, 1), 1.0, F32) / jnp.full((1, 1), length_ref[0].astype(F32), F32)


def attend_near(length_ref, query_ref, own_ref, flip):
    _, upper = place_of_device()
    weight = weight_of(length_ref)
    rows = lax.broadcasted_iota(jnp.int32, (TILE, 1), 0) + upper * TILE
    columns = lax.broadcasted_iota(jnp.int32, (1, TILE), 1) + (upper ^ flip) * TILE
    live = rows <= columns
    column = 2 * HEAD_DIM
    low = tile_grads(query_ref, 0, own_ref, 0, column, weight, live)
    whole = tile_grads(query_ref, 1, own_ref, 0, column, weight, None)
    high = tile_grads(query_ref, 1, own_ref, 1, column, weight, live)
    return low, whole, high


def attend_own_kernel(length_ref, own_ref, query_ref, key_ref):
    low, whole, high = attend_near(length_ref, own_ref, own_ref, 0)
    query_ref[0] = low[0]
    query_ref[1] = whole[0] + high[0]
    key_ref[0, :, :HEAD_DIM] = low[1] + whole[1]
    key_ref[0, :, HEAD_DIM:] = low[2] + whole[2]
    key_ref[1, :, :HEAD_DIM] = high[1]
    key_ref[1, :, HEAD_DIM:] = high[2]


def attend_queries_kernel(length_ref, own_ref, query_far_ref, sums_ref, query_ref, key_ref):
    low, whole, high = attend_near(length_ref, query_far_ref, own_ref, 1)
    query_ref[0] = low[0]
    query_ref[1] = whole[0] + high[0]
    key_ref[0, :, :HEAD_DIM] = sums_ref[0, :, :HEAD_DIM] + (low[1] + whole[1])
    key_ref[0, :, HEAD_DIM:] = sums_ref[0, :, HEAD_DIM:] + (low[2] + whole[2])
    key_ref[1, :, :HEAD_DIM] = sums_ref[1, :, :HEAD_DIM] + high[1]
    key_ref[1, :, HEAD_DIM:] = sums_ref[1, :, HEAD_DIM:] + high[2]


def attend_keys_kernel(
    length_ref,
    own_ref,
    query_far_ref,
    key_far_ref,
    near_own_ref,
    near_far_ref,
    query_own_ref,
    query_send_ref,
    key_send_ref,
    query_acc,
    key_acc,
):
    pair, _ = place_of_device()
    weight = weight_of(length_ref)
    last = 1 - pair
    for place, (query_ref, near_ref) in enumerate(
        ((own_ref, near_own_ref), (query_far_ref, near_far_ref))
    ):
        query_acc[...] = near_ref[...]
        first = tile_grads(query_ref, 1, key_far_ref, 0, 0, weight, None)
        query_acc[1] += first[0]
        if place == 0:
            key_acc[0, :, :HEAD_DIM] = first[1]
            key_acc[0, :, HEAD_DIM:] = first[2]
            key_acc[1] = jnp.zeros_like(key_acc[1])
        else:
            key_acc[0, :, :HEAD_DIM] += first[1]
            key_acc[0, :, HEAD_DIM:] += first[2]
        second = tile_grads(query_ref, last, key_far_ref, last, 0, weight, None)
        query_acc[last] += second[0]
        key_acc[last, :, :HEAD_DIM] += second[1]
        key_acc[last, :, HEAD_DIM:] += second[2]
        if place == 0:
            query_own_ref[...] = query_acc[...]
        else:
            query_send_ref[...] = query_acc[...].astype(BF16)
    key_send_ref[...] = key_acc[...].astype(BF16)


def attend_cost(tiles):
    return pl.CostEstimate(
        flops=tiles * 5 * 2 * TILE * TILE * HEAD_DIM,
        bytes_accessed=2 << 20,
        transcendentals=tiles * TILE * TILE,
    )


QUERY_SUMS = jax.ShapeDtypeStruct((2, TILE, HEAD_DIM), F32)
KEY_SUMS = jax.ShapeDtypeStruct((2, TILE, 2 * HEAD_DIM), F32)


def attend_own(length, own):
    return pl.pallas_call(
        attend_own_kernel,
        out_shape=(QUERY_SUMS, KEY_SUMS),
        in_specs=[in_smem()] + in_vmem(1),
        out_specs=tuple(in_vmem(2)),
        compiler_params=params(),
        cost_estimate=attend_cost(3),
        name="attend_own",
    )(length, own)


def attend_queries(length, own, query_far, sums):
    return pl.pallas_call(
        attend_queries_kernel,
        out_shape=(QUERY_SUMS, KEY_SUMS),
        in_specs=[in_smem()] + in_vmem(3),
        out_specs=tuple(in_vmem(2)),
        compiler_params=params(),
        cost_estimate=attend_cost(3),
        name="attend_queries",
    )(length, own, query_far, sums)


def attend_keys(length, own, query_far, key_far, near_own, near_far):
    return pl.pallas_call(
        attend_keys_kernel,
        out_shape=(
            QUERY_SUMS,
            jax.ShapeDtypeStruct((2, TILE, HEAD_DIM), BF16),
            jax.ShapeDtypeStruct((2, TILE, 2 * HEAD_DIM), BF16),
        ),
        in_specs=[in_smem()] + in_vmem(5),
        out_specs=tuple(in_vmem(3)),
        scratch_shapes=[
            pltpu.VMEM((2, TILE, HEAD_DIM), F32),
            pltpu.VMEM((2, TILE, 2 * HEAD_DIM), F32),
        ],
        compiler_params=params(),
        cost_estimate=attend_cost(4),
        name="attend_keys",
    )(length, own, query_far, key_far, near_own, near_far)


def join_kernel(query_own_ref, query_got_ref, key_own_ref, key_got_ref, out_ref):
    out_ref[:, :, :HEAD_DIM] = (
        key_own_ref[:, :, HEAD_DIM:] + key_got_ref[:, :, HEAD_DIM:].astype(F32)
    ).astype(BF16)
    out_ref[:, :, HEAD_DIM : 2 * HEAD_DIM] = (
        query_own_ref[...] + query_got_ref[...].astype(F32)
    ).astype(BF16)
    out_ref[:, :, 2 * HEAD_DIM :] = (
        key_own_ref[:, :, :HEAD_DIM] + key_got_ref[:, :, :HEAD_DIM].astype(F32)
    ).astype(BF16)


def join_parts(query_own, query_got, key_own, key_got):
    return pl.pallas_call(
        join_kernel,
        out_shape=jax.ShapeDtypeStruct((2, TILE, 3 * HEAD_DIM), BF16),
        in_specs=in_vmem(4),
        out_specs=in_vmem(1)[0],
        compiler_params=params(),
        name="join_parts",
    )(query_own, query_got, key_own, key_got)


def finish_kernel(
    grads_ref,
    slope_ref,
    gate_ref,
    base_ref,
    in_proj_ref,
    slot_ref,
    item_ref,
    proj_ref,
    rows_ref,
    wide_ref,
):
    proj_ref[:, :WIDTH] = gate_ref[...]
    for block in range(3):
        joined = jnp.concatenate(
            [
                grads_ref[head, :, block * HEAD_DIM : (block + 1) * HEAD_DIM].astype(F32)
                for head in range(HEADS)
            ],
            axis=1,
        )
        cols = slice((block + 1) * WIDTH, (block + 2) * WIDTH)
        proj_ref[:, cols] = (joined * slope_ref[:, block * WIDTH : (block + 1) * WIDTH]).astype(
            BF16
        )
    input_grad = base_ref[...] + dot(proj_ref[:, WIDTH:], in_proj_ref[:, WIDTH:], MATMUL_NT)
    high = input_grad.astype(BF16)
    low = (input_grad - high.astype(F32)).astype(BF16)
    order = lax.broadcasted_iota(jnp.int32, (TABLES * CAP, 1), 0)
    slot_of = (order % TABLES) * CAP + order // TABLES
    picks = (slot_ref[...] == slot_of).astype(F32).astype(BF16)
    summed = dot(picks, high, MATMUL) + dot(picks, low, MATMUL)
    for level in range(CAP):
        for chunk in range(WIDTH // 128):
            wide_ref[pl.ds(level * 4 + chunk, TABLES, stride=SEND_ROWS), :] = summed[
                level * TABLES : (level + 1) * TABLES, chunk * 128 : (chunk + 1) * 128
            ]
    items = item_ref[...]
    owner_of = (items // (ROWS_DEV * TABLES)).astype(F32)
    place_of = (items % ROWS_DEV).astype(F32)
    slot = lax.broadcasted_iota(jnp.int32, (TABLES, TABLES * CAP), 1)
    owner = lax.broadcasted_iota(jnp.int32, (TABLES, TABLES * CAP), 0)
    coded = jnp.zeros((TABLES, 128), F32)
    for level in range(CAP):
        match = slot == owner * CAP + level
        for value, lane in ((owner_of, level), (place_of, CAP + level)):
            column = jnp.sum(jnp.where(match, value, 0.0), axis=1, keepdims=True)
            coded = jnp.where(slot == lane, column, coded)
    wide_ref[pl.ds(SUM_ROWS, TABLES, stride=SEND_ROWS), :] = coded
    for row in range(SUM_ROWS + 1, SEND_ROWS):
        wide_ref[pl.ds(row, TABLES, stride=SEND_ROWS), :] = jnp.zeros((TABLES, 128), F32)
    rows_ref[...] = wide_ref[...].astype(BF16)


def finish(grads, slope, gate, base, in_proj, slots, items):
    return pl.pallas_call(
        finish_kernel,
        out_shape=(
            jax.ShapeDtypeStruct((TOKENS, 4 * WIDTH), BF16),
            jax.ShapeDtypeStruct((TABLES * SEND_ROWS, 128), BF16),
        ),
        in_specs=in_vmem(7),
        out_specs=tuple(in_vmem(2)),
        scratch_shapes=[pltpu.VMEM((TABLES * SEND_ROWS, 128), F32)],
        compiler_params=params(),
        name="finish",
    )(grads, slope, gate, base, in_proj, slots, items)


def compact_kernel(rows_ref, out_ref, wide_ref, packed_ref):
    x = lax.div(lax.axis_index("ctx"), Y_COUNT)
    wide_ref[...] = rows_ref[...].astype(F32)
    for owner in range(TABLES):
        packed_ref[owner * SUM_ROWS : (owner + 1) * SUM_ROWS, :] = wide_ref[
            owner * SEND_ROWS : owner * SEND_ROWS + SUM_ROWS, :
        ]
    coded = wide_ref[pl.ds(SUM_ROWS, TABLES, stride=SEND_ROWS), :].T[: 2 * CAP]
    lane = lax.broadcasted_iota(jnp.int32, (2 * CAP, 128), 1)
    spaced = jnp.where(lane // TABLES == x, jnp.concatenate([coded] * X_COUNT, axis=1), 0.0)
    packed_ref[GIVE_SUMS : GIVE_SUMS + 2 * CAP, :] = spaced
    packed_ref[GIVE_SUMS + 2 * CAP :, :] = jnp.zeros((GIVE_ROWS - GIVE_SUMS - 2 * CAP, 128), F32)
    out_ref[...] = packed_ref[...].astype(BF16)


def compact_rows(rows):
    return pl.pallas_call(
        compact_kernel,
        out_shape=jax.ShapeDtypeStruct((GIVE_ROWS, 128), BF16),
        in_specs=in_vmem(1),
        out_specs=in_vmem(1)[0],
        scratch_shapes=[
            pltpu.VMEM((TABLES * SEND_ROWS, 128), F32),
            pltpu.VMEM((GIVE_ROWS, 128), F32),
        ],
        compiler_params=params(),
        name="compact_rows",
    )(rows)


def scatter_kernel(rows_ref, out_ref, wide_ref):
    targets = Y_COUNT * ROWS_DEV
    first = lax.div(lax.axis_index("ctx"), Y_COUNT) * targets
    wide_ref[...] = rows_ref[...].astype(F32)
    coded = sum(wide_ref[x, GIVE_SUMS : GIVE_SUMS + 2 * CAP, :] for x in range(X_COUNT))
    ids = (coded[:CAP] * ROWS_DEV + coded[CAP:]).astype(jnp.int32)
    target = first + lax.broadcasted_iota(jnp.int32, (targets, 1), 0)
    hots = [(ids[level : level + 1, :] == target).astype(F32).astype(BF16) for level in range(CAP)]
    for chunk in range(WIDTH // 128):
        total = None
        for level in range(CAP):
            rows = jnp.concatenate(
                [
                    wide_ref[x, pl.ds(level * 4 + chunk, TABLES, stride=SUM_ROWS), :]
                    for x in range(X_COUNT)
                ],
                axis=0,
            ).astype(BF16)
            part = dot(hots[level], rows, MATMUL)
            total = part if total is None else total + part
        out_ref[:, chunk * 128 : (chunk + 1) * 128] = total.astype(BF16)


def scatter_rows(rows):
    return pl.pallas_call(
        scatter_kernel,
        out_shape=jax.ShapeDtypeStruct((Y_COUNT * ROWS_DEV, WIDTH), BF16),
        in_specs=in_vmem(1),
        out_specs=in_vmem(1)[0],
        scratch_shapes=[pltpu.VMEM((X_COUNT, GIVE_ROWS, 128), F32)],
        compiler_params=params(),
        name="scatter_rows",
    )(rows)


def per_device(
    item_inputs,
    attn_saved,
    out_grad,
    seq_lengths,
    token_slot,
    slot_rows,
    in_proj,
    out_proj,
    norm_gain,
):
    parts, slope, gate, base = project(
        seq_lengths, item_inputs[0], attn_saved[0], out_grad[0], in_proj, out_proj, norm_gain[None]
    )
    own = lax.all_to_all(parts, "ctx", 0, 0, axis_index_groups=HEAD_GROUPS)
    own = own.reshape(2, TILE, 4 * HEAD_DIM)
    query_far = lax.ppermute(own[:, :, : 2 * HEAD_DIM], "ctx", SWAP_QUERY)
    key_far = lax.ppermute(own[:, :, 2 * HEAD_DIM :], "ctx", SWAP_KEY)
    near_own, sums = attend_own(seq_lengths, own)
    near_far, key_own = attend_queries(seq_lengths, own, query_far, sums)
    query_own, query_send, key_send = attend_keys(
        seq_lengths, own, query_far, key_far, near_own, near_far
    )
    query_got = lax.ppermute(query_send, "ctx", SWAP_QUERY)
    key_got = lax.ppermute(key_send, "ctx", SWAP_KEY)
    joined = join_parts(query_own, query_got, key_own, key_got)
    grads = lax.all_to_all(
        joined.reshape(HEADS, TOKENS, 3 * HEAD_DIM), "ctx", 0, 0, axis_index_groups=HEAD_GROUPS
    )
    proj_grad, rows = finish(grads, slope, gate, base, in_proj, token_slot, slot_rows)
    rows = lax.all_to_all(rows.reshape(TABLES, SEND_ROWS, 128), "table", 0, 0)
    rows = compact_rows(rows.reshape(TABLES * SEND_ROWS, 128))
    rows = lax.all_gather(rows, "ctx", axis_index_groups=X_GROUPS)
    dense = scatter_rows(rows)
    pieces = lax.all_to_all(
        dense.reshape(Y_COUNT, ROWS_DEV, WIDTH), "ctx", 0, 0, axis_index_groups=Y_GROUPS
    )
    table_grad = jnp.sum(pieces.astype(F32), axis=0)
    return (proj_grad[None], table_grad)


def solution(mesh):
    return jax.shard_map(
        per_device,
        mesh=mesh,
        in_specs=(
            P("table", "ctx", None),
            P("table", "ctx", None),
            P("table", "ctx", None),
            P("table"),
            P("table", "ctx"),
            P("table", "ctx"),
            P(),
            P(),
            P(),
        ),
        out_specs=(P("table", "ctx", None), P(("ctx", "table"), None)),
        check_vma=False,
    )
```

```python
import functools

import jax
import jax.numpy as jnp
from jax import lax
from jax.experimental import pallas as pl
from jax.experimental.pallas import tpu as pltpu
from jax.sharding import PartitionSpec as P

HEADS = 4
HEAD_DIM = 128
WIDTH = 512
TOKENS = 128
ROWS_DEV = 64
TABLES = 32
CAP = 4
SUM_ROWS = CAP * WIDTH // 128
SEND_ROWS = SUM_ROWS + 8
GIVE_SUMS = TABLES * SUM_ROWS
GIVE_ROWS = GIVE_SUMS + 16
X_COUNT = 4
Y_COUNT = 4
TILE = 2 * TOKENS
VMEM_LIMIT = 48 * 1024 * 1024
BF16 = jnp.bfloat16
F32 = jnp.float32

X_PAIRS = ((0, 3), (1, 2))
HEAD_GROUPS = [
    [X_PAIRS[pair][place] * Y_COUNT + upper * 2 + parity for place in range(2) for parity in range(2)]
    for pair in range(2)
    for upper in range(2)
]
X_GROUPS = [[x * Y_COUNT + y for x in range(X_COUNT)] for y in range(Y_COUNT)]
Y_GROUPS = [[x * Y_COUNT + y for y in range(Y_COUNT)] for x in range(X_COUNT)]
SWAP_QUERY = [(c, c ^ 2) for c in range(X_COUNT * Y_COUNT)]
SWAP_KEY = [(c, c ^ Y_COUNT) for c in range(X_COUNT * Y_COUNT)]

MATMUL = (((1,), (0,)), ((), ()))
MATMUL_NT = (((1,), (1,)), ((), ()))
MATMUL_TN = (((0,), (0,)), ((), ()))


def dot(lhs, rhs, dims):
    return lax.dot_general(lhs, rhs, dims, preferred_element_type=F32)


def in_vmem(count):
    return [pl.BlockSpec(memory_space=pltpu.VMEM)] * count


def in_smem():
    return pl.BlockSpec(memory_space=pltpu.SMEM)


def in_hbm(count):
    return [pl.BlockSpec(memory_space=pltpu.HBM)] * count


def params(limit=VMEM_LIMIT):
    return pltpu.CompilerParams(vmem_limit_bytes=limit)


def project_kernel(
    length_ref,
    inputs_hbm,
    saved_hbm,
    grad_hbm,
    in_proj_hbm,
    out_proj_hbm,
    gain_hbm,
    parts_ref,
    pre_ref,
    gain_grad_ref,
    inputs_ref,
    saved_ref,
    grad_ref,
    in_proj_ref,
    out_proj_ref,
    gain_ref,
    sems,
):
    def copy_of(place, source, target):
        copy = pltpu.make_async_copy(source, target, sems.at[place])
        copy.start()
        return copy

    saved_copy = copy_of(0, saved_hbm, saved_ref)
    grad_copy = copy_of(1, grad_hbm, grad_ref)
    gain_copy = copy_of(2, gain_hbm, gain_ref)
    out_copy = copy_of(3, out_proj_hbm, out_proj_ref)
    inputs_copy = copy_of(4, inputs_hbm, inputs_ref)
    in_copies = [
        copy_of(
            5 + block,
            in_proj_hbm.at[:, block * WIDTH : (block + 1) * WIDTH],
            in_proj_ref.at[block],
        )
        for block in range(4)
    ]
    first = lax.axis_index("ctx") * TOKENS
    length = length_ref[0]
    saved_copy.wait()
    saved = saved_ref[...].astype(F32)
    row_mean = jnp.mean(saved, axis=1, keepdims=True)
    centred = saved - row_mean
    inv_std = lax.rsqrt(jnp.mean(centred * centred, axis=1, keepdims=True) + 1e-05)
    normed = centred * inv_std
    grad_copy.wait()
    gain_copy.wait()
    out_copy.wait()
    gain = gain_ref[...]
    grad = grad_ref[...]
    back = dot(grad, out_proj_ref[...], MATMUL_NT)

    inputs_copy.wait()
    in_copies[0].wait()
    inputs = inputs_ref[...]
    pre = dot(inputs, in_proj_ref[0], MATMUL)
    pre_ref[:, :WIDTH] = pre
    gating = (pre * jax.nn.sigmoid(pre)).astype(BF16).astype(F32)
    gain_grad_ref[...] = back * (normed * gain)
    carried = back * gating * gain
    out_attn = inv_std * (
        carried
        - jnp.mean(carried, axis=1, keepdims=True)
        - normed * jnp.mean(carried * normed, axis=1, keepdims=True)
    )
    position = first + lax.broadcasted_iota(jnp.int32, (TOKENS, 1), 0)
    out_attn = jnp.where(position < length, out_attn, 0.0).astype(BF16)
    for head in range(HEADS):
        cols = slice(head * HEAD_DIM, (head + 1) * HEAD_DIM)
        parts_ref[head, :, HEAD_DIM : 2 * HEAD_DIM] = out_attn[:, cols]
    for block, place in ((1, 3), (2, 0), (3, 2)):
        in_copies[block].wait()
        pre = dot(inputs, in_proj_ref[block], MATMUL)
        pre_ref[:, block * WIDTH : (block + 1) * WIDTH] = pre
        hidden = (pre * jax.nn.sigmoid(pre)).astype(BF16)
        for head in range(HEADS):
            cols = slice(head * HEAD_DIM, (head + 1) * HEAD_DIM)
            parts_ref[head, :, place * HEAD_DIM : (place + 1) * HEAD_DIM] = hidden[:, cols]


def project(length, *arrays):
    return pl.pallas_call(
        project_kernel,
        out_shape=(
            jax.ShapeDtypeStruct((HEADS, TOKENS, 4 * HEAD_DIM), BF16),
            jax.ShapeDtypeStruct((TOKENS, 4 * WIDTH), F32),
            jax.ShapeDtypeStruct((TOKENS, WIDTH), F32),
        ),
        in_specs=[in_smem()] + in_hbm(6),
        out_specs=tuple(in_vmem(3)),
        scratch_shapes=[
            pltpu.VMEM((TOKENS, WIDTH), BF16),
            pltpu.VMEM((TOKENS, WIDTH), BF16),
            pltpu.VMEM((TOKENS, WIDTH), BF16),
            pltpu.VMEM((4, WIDTH, WIDTH), BF16),
            pltpu.VMEM((WIDTH, WIDTH), BF16),
            pltpu.VMEM((1, WIDTH), F32),
            pltpu.SemaphoreType.DMA((9,)),
        ],
        compiler_params=params(),
        name="project",
    )(length, *(pltpu.with_memory_space_constraint(array, pltpu.HBM) for array in arrays))


def local_kernel(
    pre_ref, gain_grad_ref, grad_ref, in_proj_ref, item_ref, slope_ref, gate_ref, base_ref, code_ref
):
    pre = pre_ref[...]
    squash = jax.nn.sigmoid(pre)
    slope = squash * (1.0 + pre * (1.0 - squash))
    slope_ref[...] = slope[:, WIDTH:]
    gate = (gain_grad_ref[...] * slope[:, :WIDTH]).astype(BF16)
    gate_ref[...] = gate
    base_ref[...] = grad_ref[...].astype(F32) + dot(gate, in_proj_ref[:, :WIDTH], MATMUL_NT)
    items = item_ref[...]
    owner_of = (items // (ROWS_DEV * TABLES)).astype(F32)
    place_of = (items % ROWS_DEV).astype(F32)
    slot = lax.broadcasted_iota(jnp.int32, (TABLES, TABLES * CAP), 1)
    owner = lax.broadcasted_iota(jnp.int32, (TABLES, TABLES * CAP), 0)
    coded = jnp.zeros((TABLES, 128), F32)
    for level in range(CAP):
        match = slot == owner * CAP + level
        for value, lane in ((owner_of, level), (place_of, CAP + level)):
            column = jnp.sum(jnp.where(match, value, 0.0), axis=1, keepdims=True)
            coded = jnp.where(slot == lane, column, coded)
    code_ref[...] = coded


def local_terms(pre, gain_grad, grad, in_proj, items):
    return pl.pallas_call(
        local_kernel,
        out_shape=(
            jax.ShapeDtypeStruct((TOKENS, 3 * WIDTH), F32),
            jax.ShapeDtypeStruct((TOKENS, WIDTH), BF16),
            jax.ShapeDtypeStruct((TOKENS, WIDTH), F32),
            jax.ShapeDtypeStruct((TABLES, 128), F32),
        ),
        in_specs=in_vmem(5),
        out_specs=tuple(in_vmem(4)),
        compiler_params=params(),
        cost_estimate=pl.CostEstimate(
            flops=2 * TOKENS * WIDTH * WIDTH,
            bytes_accessed=3 << 20,
            transcendentals=TOKENS * 4 * WIDTH,
        ),
        name="local_terms",
    )(pre, gain_grad, grad, in_proj, items)


def tile_grads(query_ref, query_place, key_ref, key_place, key_column, weight, live):
    scale = HEAD_DIM ** (-0.5)
    queries = query_ref[query_place, :, :HEAD_DIM]
    outs = query_ref[query_place, :, HEAD_DIM : 2 * HEAD_DIM]
    if key_place is None:
        keys, values = (
            key_ref[:, :, column : column + HEAD_DIM].reshape(2 * TILE, HEAD_DIM)
            for column in (key_column, key_column + HEAD_DIM)
        )
    else:
        keys = key_ref[key_place, :, key_column : key_column + HEAD_DIM]
        values = key_ref[key_place, :, key_column + HEAD_DIM : key_column + 2 * HEAD_DIM]
    scores = dot(keys, queries, MATMUL_NT) * scale
    attn_grad = dot(values, outs, MATMUL_NT)
    squash = 0.5 + 0.5 * jnp.tanh(scores * 0.5)
    weighted = squash * weight
    if live is not None:
        weighted = jnp.where(live, weighted, 0.0)
    gated = scores * weighted
    attend = gated.astype(BF16)
    score_grad = (attn_grad * (weighted + gated * (1.0 - squash))).astype(BF16)
    return (
        dot(score_grad, keys, MATMUL_TN) * scale,
        dot(score_grad, queries, MATMUL) * scale,
        dot(attend, outs, MATMUL),
    )


def place_of_device():
    ctx = lax.axis_index("ctx")
    x = lax.div(ctx, Y_COUNT)
    return (x ^ lax.div(x, 2)) & 1, lax.div(lax.rem(ctx, Y_COUNT), 2)


def weight_of(length_ref):
    return jnp.full((1, 1), 1.0, F32) / jnp.full((1, 1), length_ref[0].astype(F32), F32)


def attend_near(length_ref, query_ref, own_ref, flip):
    _, upper = place_of_device()
    weight = weight_of(length_ref)
    rows = lax.broadcasted_iota(jnp.int32, (2 * TILE, 1), 0)
    rows = jnp.where(rows < TILE, -1, rows - TILE + upper * TILE)
    columns = lax.broadcasted_iota(jnp.int32, (1, TILE), 1) + (upper ^ flip) * TILE
    live = rows <= columns
    column = 2 * HEAD_DIM
    low = tile_grads(query_ref, 0, own_ref, 0, column, weight, live[TILE:])
    high = tile_grads(query_ref, 1, own_ref, None, column, weight, live)
    return low, high


def attend_own_kernel(length_ref, own_ref, query_ref, key_ref):
    low, high = attend_near(length_ref, own_ref, own_ref, 0)
    query_ref[0] = low[0]
    query_ref[1] = high[0]
    key_ref[0, :, :HEAD_DIM] = low[1] + high[1][:TILE]
    key_ref[0, :, HEAD_DIM:] = low[2] + high[2][:TILE]
    key_ref[1, :, :HEAD_DIM] = high[1][TILE:]
    key_ref[1, :, HEAD_DIM:] = high[2][TILE:]


def attend_queries_kernel(
    length_ref, own_ref, query_far_ref, sums_ref, _, query_ref, key_ref
):
    low, high = attend_near(length_ref, query_far_ref, own_ref, 1)
    query_ref[0] = low[0]
    query_ref[1] = high[0]
    key_ref[0, :, :HEAD_DIM] = sums_ref[0, :, :HEAD_DIM] + (low[1] + high[1][:TILE])
    key_ref[0, :, HEAD_DIM:] = sums_ref[0, :, HEAD_DIM:] + (low[2] + high[2][:TILE])
    key_ref[1, :, :HEAD_DIM] = sums_ref[1, :, :HEAD_DIM] + high[1][TILE:]
    key_ref[1, :, HEAD_DIM:] = sums_ref[1, :, HEAD_DIM:] + high[2][TILE:]


def attend_keys_kernel(
    length_ref,
    own_ref,
    query_far_ref,
    key_far_ref,
    near_own_ref,
    near_far_ref,
    query_own_ref,
    query_send_ref,
    key_send_ref,
    query_acc,
    key_acc,
):
    pair, _ = place_of_device()
    weight = weight_of(length_ref)
    last = 1 - pair
    for place, (query_ref, near_ref) in enumerate(
        ((own_ref, near_own_ref), (query_far_ref, near_far_ref))
    ):
        query_acc[...] = near_ref[...]
        first = tile_grads(query_ref, 1, key_far_ref, 0, 0, weight, None)
        query_acc[1] += first[0]
        if place == 0:
            key_acc[0, :, :HEAD_DIM] = first[1]
            key_acc[0, :, HEAD_DIM:] = first[2]
            key_acc[1] = jnp.zeros_like(key_acc[1])
        else:
            key_acc[0, :, :HEAD_DIM] += first[1]
            key_acc[0, :, HEAD_DIM:] += first[2]
        second = tile_grads(query_ref, last, key_far_ref, last, 0, weight, None)
        query_acc[last] += second[0]
        key_acc[last, :, :HEAD_DIM] += second[1]
        key_acc[last, :, HEAD_DIM:] += second[2]
        if place == 0:
            query_own_ref[...] = query_acc[...]
        else:
            query_send_ref[...] = query_acc[...].astype(BF16)
    key_send_ref[...] = key_acc[...].astype(BF16)


def attend_cost(tiles):
    return pl.CostEstimate(
        flops=tiles * 5 * 2 * TILE * TILE * HEAD_DIM,
        bytes_accessed=2 << 20,
        transcendentals=tiles * TILE * TILE,
    )


QUERY_SUMS = jax.ShapeDtypeStruct((2, TILE, HEAD_DIM), F32)
KEY_SUMS = jax.ShapeDtypeStruct((2, TILE, 2 * HEAD_DIM), F32)


def attend_own(length, own):
    return pl.pallas_call(
        attend_own_kernel,
        out_shape=(QUERY_SUMS, KEY_SUMS),
        in_specs=[in_smem()] + in_vmem(1),
        out_specs=tuple(in_vmem(2)),
        compiler_params=params(),
        cost_estimate=attend_cost(3),
        name="attend_own",
    )(length, own)


def attend_queries(length, own, query_far, sums, codes):
    return pl.pallas_call(
        attend_queries_kernel,
        out_shape=(QUERY_SUMS, KEY_SUMS),
        in_specs=[in_smem()] + in_vmem(3) + [pl.BlockSpec(memory_space=pl.ANY)],
        out_specs=tuple(in_vmem(2)),
        compiler_params=params(),
        cost_estimate=attend_cost(3),
        name="attend_queries",
    )(length, own, query_far, sums, codes)


def attend_keys(length, own, query_far, key_far, near_own, near_far):
    return pl.pallas_call(
        attend_keys_kernel,
        out_shape=(
            QUERY_SUMS,
            jax.ShapeDtypeStruct((2, TILE, HEAD_DIM), BF16),
            jax.ShapeDtypeStruct((2, TILE, 2 * HEAD_DIM), BF16),
        ),
        in_specs=[in_smem()] + in_vmem(5),
        out_specs=tuple(in_vmem(3)),
        scratch_shapes=[
            pltpu.VMEM((2, TILE, HEAD_DIM), F32),
            pltpu.VMEM((2, TILE, 2 * HEAD_DIM), F32),
        ],
        compiler_params=params(),
        cost_estimate=attend_cost(4),
        name="attend_keys",
    )(length, own, query_far, key_far, near_own, near_far)


def join_kernel(query_own_ref, query_got_ref, key_own_ref, key_got_ref, out_ref):
    out_ref[:, :, :HEAD_DIM] = (
        key_own_ref[:, :, HEAD_DIM:] + key_got_ref[:, :, HEAD_DIM:].astype(F32)
    ).astype(BF16)
    out_ref[:, :, HEAD_DIM : 2 * HEAD_DIM] = (
        query_own_ref[...] + query_got_ref[...].astype(F32)
    ).astype(BF16)
    out_ref[:, :, 2 * HEAD_DIM :] = (
        key_own_ref[:, :, :HEAD_DIM] + key_got_ref[:, :, :HEAD_DIM].astype(F32)
    ).astype(BF16)


def join_parts(query_own, query_got, key_own, key_got):
    return pl.pallas_call(
        join_kernel,
        out_shape=jax.ShapeDtypeStruct((2, TILE, 3 * HEAD_DIM), BF16),
        in_specs=in_vmem(4),
        out_specs=in_vmem(1)[0],
        compiler_params=params(),
        name="join_parts",
    )(query_own, query_got, key_own, key_got)


def finish_kernel(
    grads_ref,
    slope_ref,
    gate_ref,
    base_ref,
    in_proj_ref,
    slot_ref,
    code_ref,
    proj_ref,
    rows_ref,
    wide_ref,
):
    proj_ref[:, :WIDTH] = gate_ref[...]
    for block in range(3):
        joined = jnp.concatenate(
            [
                grads_ref[head, :, block * HEAD_DIM : (block + 1) * HEAD_DIM].astype(F32)
                for head in range(HEADS)
            ],
            axis=1,
        )
        cols = slice((block + 1) * WIDTH, (block + 2) * WIDTH)
        proj_ref[:, cols] = (joined * slope_ref[:, block * WIDTH : (block + 1) * WIDTH]).astype(
            BF16
        )
    input_grad = base_ref[...] + dot(proj_ref[:, WIDTH:], in_proj_ref[:, WIDTH:], MATMUL_NT)
    high = input_grad.astype(BF16)
    low = (input_grad - high.astype(F32)).astype(BF16)
    order = lax.broadcasted_iota(jnp.int32, (TABLES * CAP, 1), 0)
    slot_of = (order % TABLES) * CAP + order // TABLES
    picks = (slot_ref[...] == slot_of).astype(F32).astype(BF16)
    summed = dot(picks, high, MATMUL) + dot(picks, low, MATMUL)
    for level in range(CAP):
        for chunk in range(WIDTH // 128):
            wide_ref[pl.ds(level * 4 + chunk, TABLES, stride=SEND_ROWS), :] = summed[
                level * TABLES : (level + 1) * TABLES, chunk * 128 : (chunk + 1) * 128
            ]
    wide_ref[pl.ds(SUM_ROWS, TABLES, stride=SEND_ROWS), :] = code_ref[...]
    for row in range(SUM_ROWS + 1, SEND_ROWS):
        wide_ref[pl.ds(row, TABLES, stride=SEND_ROWS), :] = jnp.zeros((TABLES, 128), F32)
    rows_ref[...] = wide_ref[...].astype(BF16)


def finish(grads, slope, gate, base, in_proj, slots, codes):
    return pl.pallas_call(
        finish_kernel,
        out_shape=(
            pltpu.VMEM((TOKENS, 4 * WIDTH), BF16),
            jax.ShapeDtypeStruct((TABLES * SEND_ROWS, 128), BF16),
        ),
        in_specs=in_vmem(7),
        out_specs=tuple(in_vmem(2)),
        scratch_shapes=[pltpu.VMEM((TABLES * SEND_ROWS, 128), F32)],
        compiler_params=params(),
        name="finish",
    )(grads, slope, gate, base, in_proj, slots, codes)


def compact_kernel(rows_ref, out_ref, wide_ref, packed_ref):
    x = lax.div(lax.axis_index("ctx"), Y_COUNT)
    wide_ref[...] = rows_ref[...].astype(F32)
    for owner in range(TABLES):
        packed_ref[owner * SUM_ROWS : (owner + 1) * SUM_ROWS, :] = wide_ref[
            owner * SEND_ROWS : owner * SEND_ROWS + SUM_ROWS, :
        ]
    coded = wide_ref[pl.ds(SUM_ROWS, TABLES, stride=SEND_ROWS), :].T[: 2 * CAP]
    lane = lax.broadcasted_iota(jnp.int32, (2 * CAP, 128), 1)
    spaced = jnp.where(lane // TABLES == x, jnp.concatenate([coded] * X_COUNT, axis=1), 0.0)
    packed_ref[GIVE_SUMS : GIVE_SUMS + 2 * CAP, :] = spaced
    packed_ref[GIVE_SUMS + 2 * CAP :, :] = jnp.zeros((GIVE_ROWS - GIVE_SUMS - 2 * CAP, 128), F32)
    packed = packed_ref[...].astype(BF16)
    for x_to in range(X_COUNT):
        out_ref[x_to] = packed


def compact_rows(rows):
    return pl.pallas_call(
        compact_kernel,
        out_shape=jax.ShapeDtypeStruct((X_COUNT, GIVE_ROWS, 128), BF16),
        in_specs=in_vmem(1),
        out_specs=in_vmem(1)[0],
        scratch_shapes=[
            pltpu.VMEM((TABLES * SEND_ROWS, 128), F32),
            pltpu.VMEM((GIVE_ROWS, 128), F32),
        ],
        compiler_params=params(),
        name="compact_rows",
    )(rows)


def scatter_kernel(rows_ref, proj_ref, out_ref, proj_out, wide_ref, sem):
    copy = pltpu.make_async_copy(proj_ref, proj_out, sem)
    copy.start()
    targets = Y_COUNT * ROWS_DEV
    first = lax.div(lax.axis_index("ctx"), Y_COUNT) * targets
    wide_ref[...] = rows_ref[...].astype(F32)
    coded = sum(wide_ref[x, GIVE_SUMS : GIVE_SUMS + 2 * CAP, :] for x in range(X_COUNT))
    ids = (coded[:CAP] * ROWS_DEV + coded[CAP:]).astype(jnp.int32)
    target = first + lax.broadcasted_iota(jnp.int32, (targets, 1), 0)
    hots = [(ids[level : level + 1, :] == target).astype(F32).astype(BF16) for level in range(CAP)]
    for chunk in range(WIDTH // 128):
        total = None
        for level in range(CAP):
            rows = jnp.concatenate(
                [
                    wide_ref[x, pl.ds(level * 4 + chunk, TABLES, stride=SUM_ROWS), :]
                    for x in range(X_COUNT)
                ],
                axis=0,
            ).astype(BF16)
            part = dot(hots[level], rows, MATMUL)
            total = part if total is None else total + part
        out_ref[:, chunk * 128 : (chunk + 1) * 128] = total.astype(BF16)
    copy.wait()


def scatter_rows(rows, proj):
    return pl.pallas_call(
        scatter_kernel,
        out_shape=(
            jax.ShapeDtypeStruct((Y_COUNT * ROWS_DEV, WIDTH), BF16),
            jax.ShapeDtypeStruct((TOKENS, 4 * WIDTH), BF16),
        ),
        in_specs=in_vmem(2),
        out_specs=tuple(in_vmem(1) + in_hbm(1)),
        scratch_shapes=[
            pltpu.VMEM((X_COUNT, GIVE_ROWS, 128), F32),
            pltpu.SemaphoreType.DMA(()),
        ],
        compiler_params=params(),
        name="scatter_rows",
    )(rows, proj)


def per_device(
    item_inputs,
    attn_saved,
    out_grad,
    seq_lengths,
    token_slot,
    slot_rows,
    in_proj,
    out_proj,
    norm_gain,
):
    parts, pre, gain_grad = project(
        seq_lengths, item_inputs[0], attn_saved[0], out_grad[0], in_proj, out_proj, norm_gain[None]
    )
    own = lax.all_to_all(parts, "ctx", 0, 0, axis_index_groups=HEAD_GROUPS)
    own = own.reshape(2, TILE, 4 * HEAD_DIM)
    query_far = lax.ppermute(own[:, :, : 2 * HEAD_DIM], "ctx", SWAP_QUERY)
    key_far = lax.ppermute(own[:, :, 2 * HEAD_DIM :], "ctx", SWAP_KEY)
    near_own, sums = attend_own(seq_lengths, own)
    slope, gate, base, codes = local_terms(pre, gain_grad, out_grad[0], in_proj, slot_rows)
    near_far, key_own = attend_queries(seq_lengths, own, query_far, sums, codes)
    query_own, query_send, key_send = attend_keys(
        seq_lengths, own, query_far, key_far, near_own, near_far
    )
    query_got = lax.ppermute(query_send, "ctx", SWAP_QUERY)
    key_got = lax.ppermute(key_send, "ctx", SWAP_KEY)
    joined = join_parts(query_own, query_got, key_own, key_got)
    grads = lax.all_to_all(
        joined.reshape(HEADS, TOKENS, 3 * HEAD_DIM), "ctx", 0, 0, axis_index_groups=HEAD_GROUPS
    )
    proj_grad, rows = finish(grads, slope, gate, base, in_proj, token_slot, codes)
    rows = lax.all_to_all(rows.reshape(TABLES, SEND_ROWS, 128), "table", 0, 0)
    rows = compact_rows(rows.reshape(TABLES * SEND_ROWS, 128))
    rows = lax.all_to_all(rows, "ctx", 0, 0, axis_index_groups=X_GROUPS)
    dense, proj_grad = scatter_rows(rows, proj_grad)
    pieces = lax.all_to_all(
        dense.reshape(Y_COUNT, ROWS_DEV, WIDTH), "ctx", 0, 0, axis_index_groups=Y_GROUPS
    )
    table_grad = jnp.sum(pieces.astype(F32), axis=0)
    return (proj_grad[None], table_grad)


def solution(mesh):
    return jax.shard_map(
        per_device,
        mesh=mesh,
        in_specs=(
            P("table", "ctx", None),
            P("table", "ctx", None),
            P("table", "ctx", None),
            P("table"),
            P("table", "ctx"),
            P("table", "ctx"),
            P(),
            P(),
            P(),
        ),
        out_specs=(P("table", "ctx", None), P(("ctx", "table"), None)),
        check_vma=False,
    )
```

```python
import functools

import jax
import jax.numpy as jnp
from jax import lax
from jax.experimental import pallas as pl
from jax.experimental.pallas import tpu as pltpu
from jax.sharding import PartitionSpec as P

HEADS = 4
HEAD_DIM = 128
WIDTH = 512
TOKENS = 128
ROWS_DEV = 64
TABLES = 32
CAP = 4
CORES = 2
FARS = TABLES // CORES
QUARTER = 128
HALF_SLOTS = FARS * CAP
NEAR_ROWS = HALF_SLOTS + 8
FAR_SUMS = 4 * CORES * CAP
FAR_ROWS = FAR_SUMS + 8
X_COUNT = 4
Y_COUNT = 4
CTX_COUNT = X_COUNT * Y_COUNT
TILE = 2 * TOKENS
VMEM_LIMIT = 48 * 1024 * 1024
BF16 = jnp.bfloat16
F32 = jnp.float32

X_PAIRS = ((0, 3), (1, 2))
HEAD_GROUPS = [
    [X_PAIRS[pair][place] * Y_COUNT + upper * 2 + parity for place in range(2) for parity in range(2)]
    for pair in range(2)
    for upper in range(2)
]
X_CORE_GROUPS = [
    [
        (x * Y_COUNT + y) * TABLES + far * CORES + core
        for x in range(X_COUNT)
        for core in range(CORES)
    ]
    for y in range(Y_COUNT)
    for far in range(FARS)
]
FAR_GROUPS = [[far * CORES + core for far in range(FARS)] for core in range(CORES)]
SWAP_QUERY = [(c, c ^ 2) for c in range(X_COUNT * Y_COUNT)]
SWAP_KEY = [(c, c ^ Y_COUNT) for c in range(X_COUNT * Y_COUNT)]

MATMUL = (((1,), (0,)), ((), ()))
MATMUL_NT = (((1,), (1,)), ((), ()))
MATMUL_TN = (((0,), (0,)), ((), ()))


def dot(lhs, rhs, dims):
    return lax.dot_general(lhs, rhs, dims, preferred_element_type=F32)


def in_vmem(count):
    return [pl.BlockSpec(memory_space=pltpu.VMEM)] * count


def in_smem():
    return pl.BlockSpec(memory_space=pltpu.SMEM)


def in_hbm(count):
    return [pl.BlockSpec(memory_space=pltpu.HBM)] * count


def params(limit=VMEM_LIMIT):
    return pltpu.CompilerParams(vmem_limit_bytes=limit)


def project_kernel(
    length_ref,
    inputs_hbm,
    saved_hbm,
    grad_hbm,
    in_proj_hbm,
    out_proj_hbm,
    gain_hbm,
    parts_ref,
    pre_ref,
    gain_grad_ref,
    inputs_ref,
    saved_ref,
    grad_ref,
    in_proj_ref,
    out_proj_ref,
    gain_ref,
    sems,
):
    def copy_of(place, source, target):
        copy = pltpu.make_async_copy(source, target, sems.at[place])
        copy.start()
        return copy

    saved_copy = copy_of(0, saved_hbm, saved_ref)
    grad_copy = copy_of(1, grad_hbm, grad_ref)
    gain_copy = copy_of(2, gain_hbm, gain_ref)
    out_copy = copy_of(3, out_proj_hbm, out_proj_ref)
    inputs_copy = copy_of(4, inputs_hbm, inputs_ref)
    in_copies = [
        copy_of(
            5 + block,
            in_proj_hbm.at[:, block * WIDTH : (block + 1) * WIDTH],
            in_proj_ref.at[block],
        )
        for block in range(4)
    ]
    first = lax.axis_index("ctx") * TOKENS
    length = length_ref[0]
    saved_copy.wait()
    saved = saved_ref[...].astype(F32)
    row_mean = jnp.mean(saved, axis=1, keepdims=True)
    centred = saved - row_mean
    inv_std = lax.rsqrt(jnp.mean(centred * centred, axis=1, keepdims=True) + 1e-05)
    normed = centred * inv_std
    grad_copy.wait()
    gain_copy.wait()
    out_copy.wait()
    gain = gain_ref[...]
    grad = grad_ref[...]
    back = dot(grad, out_proj_ref[...], MATMUL_NT)

    inputs_copy.wait()
    in_copies[0].wait()
    inputs = inputs_ref[...]
    pre = dot(inputs, in_proj_ref[0], MATMUL)
    pre_ref[:, :WIDTH] = pre
    gating = (pre * jax.nn.sigmoid(pre)).astype(BF16).astype(F32)
    gain_grad_ref[...] = back * (normed * gain)
    carried = back * gating * gain
    out_attn = inv_std * (
        carried
        - jnp.mean(carried, axis=1, keepdims=True)
        - normed * jnp.mean(carried * normed, axis=1, keepdims=True)
    )
    position = first + lax.broadcasted_iota(jnp.int32, (TOKENS, 1), 0)
    out_attn = jnp.where(position < length, out_attn, 0.0).astype(BF16)
    for head in range(HEADS):
        cols = slice(head * HEAD_DIM, (head + 1) * HEAD_DIM)
        parts_ref[head, :, HEAD_DIM : 2 * HEAD_DIM] = out_attn[:, cols]
    for block, place in ((1, 3), (2, 0), (3, 2)):
        in_copies[block].wait()
        pre = dot(inputs, in_proj_ref[block], MATMUL)
        pre_ref[:, block * WIDTH : (block + 1) * WIDTH] = pre
        hidden = (pre * jax.nn.sigmoid(pre)).astype(BF16)
        for head in range(HEADS):
            cols = slice(head * HEAD_DIM, (head + 1) * HEAD_DIM)
            parts_ref[head, :, place * HEAD_DIM : (place + 1) * HEAD_DIM] = hidden[:, cols]


def project(length, *arrays):
    return pl.pallas_call(
        project_kernel,
        out_shape=(
            jax.ShapeDtypeStruct((HEADS, TOKENS, 4 * HEAD_DIM), BF16),
            jax.ShapeDtypeStruct((TOKENS, 4 * WIDTH), F32),
            jax.ShapeDtypeStruct((TOKENS, WIDTH), F32),
        ),
        in_specs=[in_smem()] + in_hbm(6),
        out_specs=tuple(in_vmem(3)),
        scratch_shapes=[
            pltpu.VMEM((TOKENS, WIDTH), BF16),
            pltpu.VMEM((TOKENS, WIDTH), BF16),
            pltpu.VMEM((TOKENS, WIDTH), BF16),
            pltpu.VMEM((4, WIDTH, WIDTH), BF16),
            pltpu.VMEM((WIDTH, WIDTH), BF16),
            pltpu.VMEM((1, WIDTH), F32),
            pltpu.SemaphoreType.DMA((9,)),
        ],
        compiler_params=params(),
        name="project",
    )(length, *(pltpu.with_memory_space_constraint(array, pltpu.HBM) for array in arrays))


def local_kernel(
    pre_ref, gain_grad_ref, grad_ref, in_proj_ref, item_ref, slope_ref, gate_ref, base_ref, code_ref
):
    pre = pre_ref[...]
    squash = jax.nn.sigmoid(pre)
    slope = squash * (1.0 + pre * (1.0 - squash))
    slope_ref[...] = slope[:, WIDTH:]
    gate = (gain_grad_ref[...] * slope[:, :WIDTH]).astype(BF16)
    gate_ref[...] = gate
    base_ref[...] = grad_ref[...].astype(F32) + dot(gate, in_proj_ref[:, :WIDTH], MATMUL_NT)
    items = item_ref[...]
    owner_of = (items // (ROWS_DEV * TABLES)).astype(F32)
    place_of = (items % ROWS_DEV).astype(F32)
    slot = lax.broadcasted_iota(jnp.int32, (TABLES * CAP, 128), 0)
    lane = lax.broadcasted_iota(jnp.int32, (TABLES * CAP, 128), 1)
    wanted = lane % HALF_SLOTS
    wanted = (wanted % FARS) * (CORES * CAP) + wanted // FARS
    for core in range(CORES):
        match = slot == wanted + core * CAP
        row = sum(
            dot(
                jnp.broadcast_to(values, (8, 128)).astype(BF16),
                (match & (lane // HALF_SLOTS == part)).astype(F32).astype(BF16),
                MATMUL,
            )
            for part, values in enumerate((owner_of, place_of))
        )
        first = lax.broadcasted_iota(jnp.int32, (8, 128), 0) == 0
        code_ref[core] = jnp.where(first, row, 0.0)


def local_terms(pre, gain_grad, grad, in_proj, items):
    return pl.pallas_call(
        local_kernel,
        out_shape=(
            jax.ShapeDtypeStruct((TOKENS, 3 * WIDTH), F32),
            jax.ShapeDtypeStruct((TOKENS, WIDTH), BF16),
            jax.ShapeDtypeStruct((TOKENS, WIDTH), F32),
            jax.ShapeDtypeStruct((CORES, 8, 128), F32),
        ),
        in_specs=in_vmem(5),
        out_specs=tuple(in_vmem(4)),
        compiler_params=params(),
        cost_estimate=pl.CostEstimate(
            flops=2 * TOKENS * WIDTH * WIDTH,
            bytes_accessed=3 << 20,
            transcendentals=TOKENS * 4 * WIDTH,
        ),
        name="local_terms",
    )(pre, gain_grad, grad, in_proj, items)


def tile_grads(query_ref, query_place, key_ref, key_place, key_column, weight, live):
    scale = HEAD_DIM ** (-0.5)
    queries = query_ref[query_place, :, :HEAD_DIM]
    outs = query_ref[query_place, :, HEAD_DIM : 2 * HEAD_DIM]
    if key_place is None:
        keys, values = (
            key_ref[:, :, column : column + HEAD_DIM].reshape(2 * TILE, HEAD_DIM)
            for column in (key_column, key_column + HEAD_DIM)
        )
    else:
        keys = key_ref[key_place, :, key_column : key_column + HEAD_DIM]
        values = key_ref[key_place, :, key_column + HEAD_DIM : key_column + 2 * HEAD_DIM]
    scores = dot(keys, queries, MATMUL_NT) * scale
    attn_grad = dot(values, outs, MATMUL_NT)
    squash = 0.5 + 0.5 * jnp.tanh(scores * 0.5)
    weighted = squash * weight
    if live is not None:
        weighted = jnp.where(live, weighted, 0.0)
    gated = scores * weighted
    attend = gated.astype(BF16)
    score_grad = (attn_grad * (weighted + gated * (1.0 - squash))).astype(BF16)
    return (
        dot(score_grad, keys, MATMUL_TN) * scale,
        dot(score_grad, queries, MATMUL) * scale,
        dot(attend, outs, MATMUL),
    )


def place_of_device():
    ctx = lax.axis_index("ctx")
    x = lax.div(ctx, Y_COUNT)
    return (x ^ lax.div(x, 2)) & 1, lax.div(lax.rem(ctx, Y_COUNT), 2)


def weight_of(length_ref):
    return jnp.full((1, 1), 1.0, F32) / jnp.full((1, 1), length_ref[0].astype(F32), F32)


def attend_near(length_ref, query_ref, own_ref, flip):
    _, upper = place_of_device()
    weight = weight_of(length_ref)
    rows = lax.broadcasted_iota(jnp.int32, (2 * TILE, 1), 0)
    rows = jnp.where(rows < TILE, -1, rows - TILE + upper * TILE)
    columns = lax.broadcasted_iota(jnp.int32, (1, TILE), 1) + (upper ^ flip) * TILE
    live = rows <= columns
    column = 2 * HEAD_DIM
    low = tile_grads(query_ref, 0, own_ref, 0, column, weight, live[TILE:])
    high = tile_grads(query_ref, 1, own_ref, None, column, weight, live)
    return low, high


def attend_own_kernel(length_ref, own_ref, query_ref, key_ref):
    low, high = attend_near(length_ref, own_ref, own_ref, 0)
    query_ref[0] = low[0]
    query_ref[1] = high[0]
    key_ref[0, :, :HEAD_DIM] = low[1] + high[1][:TILE]
    key_ref[0, :, HEAD_DIM:] = low[2] + high[2][:TILE]
    key_ref[1, :, :HEAD_DIM] = high[1][TILE:]
    key_ref[1, :, HEAD_DIM:] = high[2][TILE:]


def attend_queries_kernel(
    length_ref, own_ref, query_far_ref, sums_ref, _, query_ref, key_ref
):
    low, high = attend_near(length_ref, query_far_ref, own_ref, 1)
    query_ref[0] = low[0]
    query_ref[1] = high[0]
    key_ref[0, :, :HEAD_DIM] = sums_ref[0, :, :HEAD_DIM] + (low[1] + high[1][:TILE])
    key_ref[0, :, HEAD_DIM:] = sums_ref[0, :, HEAD_DIM:] + (low[2] + high[2][:TILE])
    key_ref[1, :, :HEAD_DIM] = sums_ref[1, :, :HEAD_DIM] + high[1][TILE:]
    key_ref[1, :, HEAD_DIM:] = sums_ref[1, :, HEAD_DIM:] + high[2][TILE:]


def attend_keys_kernel(
    length_ref,
    own_ref,
    query_far_ref,
    key_far_ref,
    near_own_ref,
    near_far_ref,
    query_own_ref,
    query_send_ref,
    key_send_ref,
    query_acc,
    key_acc,
):
    pair, _ = place_of_device()
    weight = weight_of(length_ref)
    last = 1 - pair
    for place, (query_ref, near_ref) in enumerate(
        ((own_ref, near_own_ref), (query_far_ref, near_far_ref))
    ):
        query_acc[...] = near_ref[...]
        first = tile_grads(query_ref, 1, key_far_ref, 0, 0, weight, None)
        query_acc[1] += first[0]
        if place == 0:
            key_acc[0, :, :HEAD_DIM] = first[1]
            key_acc[0, :, HEAD_DIM:] = first[2]
            key_acc[1] = jnp.zeros_like(key_acc[1])
        else:
            key_acc[0, :, :HEAD_DIM] += first[1]
            key_acc[0, :, HEAD_DIM:] += first[2]
        second = tile_grads(query_ref, last, key_far_ref, last, 0, weight, None)
        query_acc[last] += second[0]
        key_acc[last, :, :HEAD_DIM] += second[1]
        key_acc[last, :, HEAD_DIM:] += second[2]
        if place == 0:
            query_own_ref[...] = query_acc[...]
        else:
            query_send_ref[...] = query_acc[...].astype(BF16)
    key_send_ref[...] = key_acc[...].astype(BF16)


def attend_cost(tiles):
    return pl.CostEstimate(
        flops=tiles * 5 * 2 * TILE * TILE * HEAD_DIM,
        bytes_accessed=2 << 20,
        transcendentals=tiles * TILE * TILE,
    )


QUERY_SUMS = jax.ShapeDtypeStruct((2, TILE, HEAD_DIM), F32)
KEY_SUMS = jax.ShapeDtypeStruct((2, TILE, 2 * HEAD_DIM), F32)


def attend_own(length, own):
    return pl.pallas_call(
        attend_own_kernel,
        out_shape=(QUERY_SUMS, KEY_SUMS),
        in_specs=[in_smem()] + in_vmem(1),
        out_specs=tuple(in_vmem(2)),
        compiler_params=params(),
        cost_estimate=attend_cost(3),
        name="attend_own",
    )(length, own)


def attend_queries(length, own, query_far, sums, codes):
    return pl.pallas_call(
        attend_queries_kernel,
        out_shape=(QUERY_SUMS, KEY_SUMS),
        in_specs=[in_smem()] + in_vmem(3) + [pl.BlockSpec(memory_space=pl.ANY)],
        out_specs=tuple(in_vmem(2)),
        compiler_params=params(),
        cost_estimate=attend_cost(3),
        name="attend_queries",
    )(length, own, query_far, sums, codes)


def attend_keys(length, own, query_far, key_far, near_own, near_far):
    return pl.pallas_call(
        attend_keys_kernel,
        out_shape=(
            QUERY_SUMS,
            jax.ShapeDtypeStruct((2, TILE, HEAD_DIM), BF16),
            jax.ShapeDtypeStruct((2, TILE, 2 * HEAD_DIM), BF16),
        ),
        in_specs=[in_smem()] + in_vmem(5),
        out_specs=tuple(in_vmem(3)),
        scratch_shapes=[
            pltpu.VMEM((2, TILE, HEAD_DIM), F32),
            pltpu.VMEM((2, TILE, 2 * HEAD_DIM), F32),
        ],
        compiler_params=params(),
        cost_estimate=attend_cost(4),
        name="attend_keys",
    )(length, own, query_far, key_far, near_own, near_far)


def join_kernel(query_own_ref, query_got_ref, key_own_ref, key_got_ref, out_ref):
    out_ref[:, :, :HEAD_DIM] = (
        key_own_ref[:, :, HEAD_DIM:] + key_got_ref[:, :, HEAD_DIM:].astype(F32)
    ).astype(BF16)
    out_ref[:, :, HEAD_DIM : 2 * HEAD_DIM] = (
        query_own_ref[...] + query_got_ref[...].astype(F32)
    ).astype(BF16)
    out_ref[:, :, 2 * HEAD_DIM :] = (
        key_own_ref[:, :, :HEAD_DIM] + key_got_ref[:, :, :HEAD_DIM].astype(F32)
    ).astype(BF16)


def join_parts(query_own, query_got, key_own, key_got):
    return pl.pallas_call(
        join_kernel,
        out_shape=jax.ShapeDtypeStruct((2, TILE, 3 * HEAD_DIM), BF16),
        in_specs=in_vmem(4),
        out_specs=in_vmem(1)[0],
        compiler_params=params(),
        name="join_parts",
    )(query_own, query_got, key_own, key_got)


def finish_kernel(
    grads_ref,
    slope_ref,
    gate_ref,
    base_ref,
    in_proj_ref,
    slot_ref,
    code_ref,
    proj_ref,
    rows_ref,
    wide_ref,
):
    proj_ref[:, :WIDTH] = gate_ref[...]
    for block in range(3):
        joined = jnp.concatenate(
            [
                grads_ref[head, :, block * HEAD_DIM : (block + 1) * HEAD_DIM].astype(F32)
                for head in range(HEADS)
            ],
            axis=1,
        )
        cols = slice((block + 1) * WIDTH, (block + 2) * WIDTH)
        proj_ref[:, cols] = (joined * slope_ref[:, block * WIDTH : (block + 1) * WIDTH]).astype(
            BF16
        )
    input_grad = base_ref[...] + dot(proj_ref[:, WIDTH:], in_proj_ref[:, WIDTH:], MATMUL_NT)
    high = input_grad.astype(BF16)
    low = (input_grad - high.astype(F32)).astype(BF16)
    order = lax.broadcasted_iota(jnp.int32, (TABLES * CAP, 1), 0)
    within = order % HALF_SLOTS
    slot_of = ((within % FARS) * CORES + order // HALF_SLOTS) * CAP + within // FARS
    picks = (slot_ref[...] == slot_of).astype(F32).astype(BF16)
    summed = dot(picks, high, MATMUL) + dot(picks, low, MATMUL)
    for x in range(X_COUNT):
        for core in range(CORES):
            target = x * CORES + core
            wide_ref[target, :HALF_SLOTS] = summed[
                core * HALF_SLOTS : (core + 1) * HALF_SLOTS, x * QUARTER : (x + 1) * QUARTER
            ]
            wide_ref[target, HALF_SLOTS:] = code_ref[core]
    rows_ref[...] = wide_ref[...].astype(BF16)


def finish(grads, slope, gate, base, in_proj, slots, codes):
    return pl.pallas_call(
        finish_kernel,
        out_shape=(
            pltpu.VMEM((TOKENS, 4 * WIDTH), BF16),
            jax.ShapeDtypeStruct((X_COUNT * CORES, NEAR_ROWS, QUARTER), BF16),
        ),
        in_specs=in_vmem(7),
        out_specs=tuple(in_vmem(2)),
        scratch_shapes=[pltpu.VMEM((X_COUNT * CORES, NEAR_ROWS, QUARTER), F32)],
        compiler_params=params(),
        name="finish",
    )(grads, slope, gate, base, in_proj, slots, codes)


def arrange_kernel(rows_ref, out_ref, wide_ref, packed_ref):
    givers = X_COUNT * CORES
    wide_ref[...] = rows_ref[...].astype(F32)
    for giver in range(givers):
        for level in range(CAP):
            packed_ref[pl.ds(giver * CAP + level, FARS, stride=FAR_ROWS), :] = wide_ref[
                giver, level * FARS : (level + 1) * FARS
            ]
    own = lax.rem(lax.div(lax.axis_index("table"), CORES), 4)
    coded = jnp.concatenate(
        [wide_ref[giver, HALF_SLOTS : HALF_SLOTS + 1] for giver in range(givers)], axis=0
    ).T
    giver = lax.broadcasted_iota(jnp.int32, (givers, 128), 0)
    lane = lax.broadcasted_iota(jnp.int32, (givers, 128), 1)
    for part in range(2):
        row = sum(
            dot(
                coded[
                    part * HALF_SLOTS + level * FARS : part * HALF_SLOTS + (level + 1) * FARS
                ].astype(BF16),
                (lane == own * FAR_SUMS + giver * CAP + level).astype(F32).astype(BF16),
                MATMUL,
            )
            for level in range(CAP)
        )
        packed_ref[pl.ds(FAR_SUMS + part, FARS, stride=FAR_ROWS), :] = row
    for row in range(FAR_SUMS + 2, FAR_ROWS):
        packed_ref[pl.ds(row, FARS, stride=FAR_ROWS), :] = jnp.zeros((FARS, 128), F32)
    out_ref[...] = packed_ref[...].astype(BF16)


def arrange_rows(rows):
    return pl.pallas_call(
        arrange_kernel,
        out_shape=jax.ShapeDtypeStruct((FARS * FAR_ROWS, QUARTER), BF16),
        in_specs=in_vmem(1),
        out_specs=in_vmem(1)[0],
        scratch_shapes=[
            pltpu.VMEM((X_COUNT * CORES, NEAR_ROWS, QUARTER), F32),
            pltpu.VMEM((FARS * FAR_ROWS, QUARTER), F32),
        ],
        compiler_params=params(),
        name="arrange_rows",
    )(rows)


def scatter_kernel(rows_ref, proj_ref, out_ref, proj_out, wide_ref, sem):
    copy = pltpu.make_async_copy(proj_ref, proj_out, sem)
    copy.start()
    targets = CTX_COUNT * ROWS_DEV
    wide_ref[...] = rows_ref[...].astype(F32)
    rows = wide_ref[:, :FAR_SUMS].reshape(FARS * FAR_SUMS, QUARTER).astype(BF16)
    ids = []
    for first in range(0, FARS, 4):
        coded = sum(wide_ref[far, FAR_SUMS : FAR_SUMS + 8] for far in range(first, first + 4))
        ids.append(coded[:1] * ROWS_DEV + coded[1:2])
    ids = jnp.concatenate(ids, axis=1).astype(jnp.int32)
    target = lax.broadcasted_iota(jnp.int32, (targets, 1), 0)
    hots = (ids == target).astype(F32).astype(BF16)
    out_ref[...] = dot(hots, rows, MATMUL).astype(BF16)
    copy.wait()


def scatter_rows(rows, proj):
    return pl.pallas_call(
        scatter_kernel,
        out_shape=(
            jax.ShapeDtypeStruct((CTX_COUNT * ROWS_DEV, QUARTER), BF16),
            jax.ShapeDtypeStruct((TOKENS, 4 * WIDTH), BF16),
        ),
        in_specs=in_vmem(2),
        out_specs=tuple(in_vmem(1) + in_hbm(1)),
        scratch_shapes=[
            pltpu.VMEM((FARS, FAR_ROWS, QUARTER), F32),
            pltpu.SemaphoreType.DMA(()),
        ],
        compiler_params=params(),
        name="scatter_rows",
    )(rows, proj)


def total_kernel(pieces_ref, out_ref):
    for x in range(X_COUNT):
        out_ref[:, x * QUARTER : (x + 1) * QUARTER] = sum(
            pieces_ref[x * Y_COUNT + y].astype(F32) for y in range(Y_COUNT)
        )


def total_rows(pieces):
    return pl.pallas_call(
        total_kernel,
        out_shape=jax.ShapeDtypeStruct((ROWS_DEV, WIDTH), F32),
        in_specs=in_vmem(1),
        out_specs=in_vmem(1)[0],
        compiler_params=params(),
        name="total_rows",
    )(pieces)


def per_device(
    item_inputs,
    attn_saved,
    out_grad,
    seq_lengths,
    token_slot,
    slot_rows,
    in_proj,
    out_proj,
    norm_gain,
):
    parts, pre, gain_grad = project(
        seq_lengths, item_inputs[0], attn_saved[0], out_grad[0], in_proj, out_proj, norm_gain[None]
    )
    own = lax.all_to_all(parts, "ctx", 0, 0, axis_index_groups=HEAD_GROUPS)
    own = own.reshape(2, TILE, 4 * HEAD_DIM)
    query_far = lax.ppermute(own[:, :, : 2 * HEAD_DIM], "ctx", SWAP_QUERY)
    key_far = lax.ppermute(own[:, :, 2 * HEAD_DIM :], "ctx", SWAP_KEY)
    near_own, sums = attend_own(seq_lengths, own)
    slope, gate, base, codes = local_terms(pre, gain_grad, out_grad[0], in_proj, slot_rows)
    near_far, key_own = attend_queries(seq_lengths, own, query_far, sums, codes)
    query_own, query_send, key_send = attend_keys(
        seq_lengths, own, query_far, key_far, near_own, near_far
    )
    query_got = lax.ppermute(query_send, "ctx", SWAP_QUERY)
    key_got = lax.ppermute(key_send, "ctx", SWAP_KEY)
    joined = join_parts(query_own, query_got, key_own, key_got)
    grads = lax.all_to_all(
        joined.reshape(HEADS, TOKENS, 3 * HEAD_DIM), "ctx", 0, 0, axis_index_groups=HEAD_GROUPS
    )
    proj_grad, rows = finish(grads, slope, gate, base, in_proj, token_slot, codes)
    rows = lax.all_to_all(rows, ("ctx", "table"), 0, 0, axis_index_groups=X_CORE_GROUPS)
    rows = arrange_rows(rows).reshape(FARS, FAR_ROWS, QUARTER)
    rows = lax.all_to_all(rows, "table", 0, 0, axis_index_groups=FAR_GROUPS)
    dense, proj_grad = scatter_rows(rows, proj_grad)
    pieces = lax.all_to_all(dense.reshape(CTX_COUNT, ROWS_DEV, QUARTER), "ctx", 0, 0)
    table_grad = total_rows(pieces)
    return (proj_grad[None], table_grad)


def solution(mesh):
    return jax.shard_map(
        per_device,
        mesh=mesh,
        in_specs=(
            P("table", "ctx", None),
            P("table", "ctx", None),
            P("table", "ctx", None),
            P("table"),
            P("table", "ctx"),
            P("table", "ctx"),
            P(),
            P(),
            P(),
        ),
        out_specs=(P("table", "ctx", None), P(("ctx", "table"), None)),
        check_vma=False,
    )
```

```python
import functools

import jax
import jax.numpy as jnp
from jax import lax
from jax.experimental import pallas as pl
from jax.experimental.pallas import tpu as pltpu
from jax.sharding import PartitionSpec as P

HEADS = 4
HEAD_DIM = 128
WIDTH = 512
TOKENS = 128
ROWS_DEV = 64
TABLES = 32
CAP = 4
CORES = 2
FARS = TABLES // CORES
QUARTER = 128
HALF_SLOTS = FARS * CAP
NEAR_ROWS = HALF_SLOTS + 8
FAR_SUMS = 4 * CORES * CAP
FAR_ROWS = FAR_SUMS + 8
X_COUNT = 4
Y_COUNT = 4
CTX_COUNT = X_COUNT * Y_COUNT
TILE = 2 * TOKENS
VMEM_LIMIT = 48 * 1024 * 1024
BF16 = jnp.bfloat16
F32 = jnp.float32

def device(x, y, table):
    return (x * Y_COUNT + y) * TABLES + table


def y_of(core, part, bit):
    return part * 2 + bit if core == 0 else bit * 2 + part


X_PAIRS = ((0, 3), (1, 2))
HEAD_GROUPS = [
    [
        device(X_PAIRS[pair][place], y_of(table % CORES, part, bit), table)
        for place in range(2)
        for bit in range(2)
    ]
    for pair in range(2)
    for part in range(2)
    for table in range(TABLES)
]
X_CORE_GROUPS = [
    [
        (x * Y_COUNT + y) * TABLES + far * CORES + core
        for x in range(X_COUNT)
        for core in range(CORES)
    ]
    for y in range(Y_COUNT)
    for far in range(FARS)
]
FAR_GROUPS = [[far * CORES + core for far in range(FARS)] for core in range(CORES)]
SWAP_QUERY = [
    (c * TABLES + t, (c ^ (2 if t % CORES == 0 else 1)) * TABLES + t)
    for c in range(CTX_COUNT)
    for t in range(TABLES)
]
SWAP_KEY = [
    (c * TABLES + t, (c ^ Y_COUNT) * TABLES + t) for c in range(CTX_COUNT) for t in range(TABLES)
]
AXES = ("ctx", "table")

MATMUL = (((1,), (0,)), ((), ()))
MATMUL_NT = (((1,), (1,)), ((), ()))
MATMUL_TN = (((0,), (0,)), ((), ()))


def dot(lhs, rhs, dims):
    return lax.dot_general(lhs, rhs, dims, preferred_element_type=F32)


def in_vmem(count):
    return [pl.BlockSpec(memory_space=pltpu.VMEM)] * count


def in_smem():
    return pl.BlockSpec(memory_space=pltpu.SMEM)


def in_hbm(count):
    return [pl.BlockSpec(memory_space=pltpu.HBM)] * count


def params(limit=VMEM_LIMIT):
    return pltpu.CompilerParams(vmem_limit_bytes=limit)


def project_kernel(
    length_ref,
    inputs_hbm,
    saved_hbm,
    grad_hbm,
    in_proj_hbm,
    out_proj_hbm,
    gain_hbm,
    parts_ref,
    pre_ref,
    gain_grad_ref,
    inputs_ref,
    saved_ref,
    grad_ref,
    in_proj_ref,
    out_proj_ref,
    gain_ref,
    sems,
):
    def copy_of(place, source, target):
        copy = pltpu.make_async_copy(source, target, sems.at[place])
        copy.start()
        return copy

    saved_copy = copy_of(0, saved_hbm, saved_ref)
    grad_copy = copy_of(1, grad_hbm, grad_ref)
    gain_copy = copy_of(2, gain_hbm, gain_ref)
    out_copy = copy_of(3, out_proj_hbm, out_proj_ref)
    inputs_copy = copy_of(4, inputs_hbm, inputs_ref)
    in_copies = [
        copy_of(
            5 + block,
            in_proj_hbm.at[:, block * WIDTH : (block + 1) * WIDTH],
            in_proj_ref.at[block],
        )
        for block in range(4)
    ]
    first = lax.axis_index("ctx") * TOKENS
    length = length_ref[0]
    saved_copy.wait()
    saved = saved_ref[...].astype(F32)
    row_mean = jnp.mean(saved, axis=1, keepdims=True)
    centred = saved - row_mean
    inv_std = lax.rsqrt(jnp.mean(centred * centred, axis=1, keepdims=True) + 1e-05)
    normed = centred * inv_std
    grad_copy.wait()
    gain_copy.wait()
    out_copy.wait()
    gain = gain_ref[...]
    grad = grad_ref[...]
    back = dot(grad, out_proj_ref[...], MATMUL_NT)

    inputs_copy.wait()
    in_copies[0].wait()
    inputs = inputs_ref[...]
    pre = dot(inputs, in_proj_ref[0], MATMUL)
    pre_ref[:, :WIDTH] = pre
    gating = (pre * jax.nn.sigmoid(pre)).astype(BF16).astype(F32)
    gain_grad_ref[...] = back * (normed * gain)
    carried = back * gating * gain
    out_attn = inv_std * (
        carried
        - jnp.mean(carried, axis=1, keepdims=True)
        - normed * jnp.mean(carried * normed, axis=1, keepdims=True)
    )
    position = first + lax.broadcasted_iota(jnp.int32, (TOKENS, 1), 0)
    out_attn = jnp.where(position < length, out_attn, 0.0).astype(BF16)
    for head in range(HEADS):
        cols = slice(head * HEAD_DIM, (head + 1) * HEAD_DIM)
        parts_ref[head, :, HEAD_DIM : 2 * HEAD_DIM] = out_attn[:, cols]
    for block, place in ((1, 3), (2, 0), (3, 2)):
        in_copies[block].wait()
        pre = dot(inputs, in_proj_ref[block], MATMUL)
        pre_ref[:, block * WIDTH : (block + 1) * WIDTH] = pre
        hidden = (pre * jax.nn.sigmoid(pre)).astype(BF16)
        for head in range(HEADS):
            cols = slice(head * HEAD_DIM, (head + 1) * HEAD_DIM)
            parts_ref[head, :, place * HEAD_DIM : (place + 1) * HEAD_DIM] = hidden[:, cols]


def project(length, *arrays):
    return pl.pallas_call(
        project_kernel,
        out_shape=(
            jax.ShapeDtypeStruct((HEADS, TOKENS, 4 * HEAD_DIM), BF16),
            jax.ShapeDtypeStruct((TOKENS, 4 * WIDTH), F32),
            jax.ShapeDtypeStruct((TOKENS, WIDTH), F32),
        ),
        in_specs=[in_smem()] + in_hbm(6),
        out_specs=tuple(in_vmem(3)),
        scratch_shapes=[
            pltpu.VMEM((TOKENS, WIDTH), BF16),
            pltpu.VMEM((TOKENS, WIDTH), BF16),
            pltpu.VMEM((TOKENS, WIDTH), BF16),
            pltpu.VMEM((4, WIDTH, WIDTH), BF16),
            pltpu.VMEM((WIDTH, WIDTH), BF16),
            pltpu.VMEM((1, WIDTH), F32),
            pltpu.SemaphoreType.DMA((9,)),
        ],
        compiler_params=params(),
        name="project",
    )(length, *(pltpu.with_memory_space_constraint(array, pltpu.HBM) for array in arrays))


def local_kernel(
    pre_ref, gain_grad_ref, grad_ref, in_proj_ref, item_ref, slope_ref, gate_ref, base_ref, code_ref
):
    pre = pre_ref[...]
    squash = jax.nn.sigmoid(pre)
    slope = squash * (1.0 + pre * (1.0 - squash))
    slope_ref[...] = slope[:, WIDTH:]
    gate = (gain_grad_ref[...] * slope[:, :WIDTH]).astype(BF16)
    gate_ref[...] = gate
    base_ref[...] = grad_ref[...].astype(F32) + dot(gate, in_proj_ref[:, :WIDTH], MATMUL_NT)
    items = item_ref[...]
    owner_of = (items // (ROWS_DEV * TABLES)).astype(F32)
    place_of = (items % ROWS_DEV).astype(F32)
    slot = lax.broadcasted_iota(jnp.int32, (TABLES * CAP, 128), 0)
    lane = lax.broadcasted_iota(jnp.int32, (TABLES * CAP, 128), 1)
    wanted = lane % HALF_SLOTS
    wanted = (wanted % FARS) * (CORES * CAP) + wanted // FARS
    for core in range(CORES):
        match = slot == wanted + core * CAP
        row = sum(
            dot(
                jnp.broadcast_to(values, (8, 128)).astype(BF16),
                (match & (lane // HALF_SLOTS == part)).astype(F32).astype(BF16),
                MATMUL,
            )
            for part, values in enumerate((owner_of, place_of))
        )
        first = lax.broadcasted_iota(jnp.int32, (8, 128), 0) == 0
        code_ref[core] = jnp.where(first, row, 0.0)


def local_terms(pre, gain_grad, grad, in_proj, items):
    return pl.pallas_call(
        local_kernel,
        out_shape=(
            jax.ShapeDtypeStruct((TOKENS, 3 * WIDTH), F32),
            jax.ShapeDtypeStruct((TOKENS, WIDTH), BF16),
            jax.ShapeDtypeStruct((TOKENS, WIDTH), F32),
            jax.ShapeDtypeStruct((CORES, 8, 128), F32),
        ),
        in_specs=in_vmem(5),
        out_specs=tuple(in_vmem(4)),
        compiler_params=params(),
        cost_estimate=pl.CostEstimate(
            flops=2 * TOKENS * WIDTH * WIDTH,
            bytes_accessed=3 << 20,
            transcendentals=TOKENS * 4 * WIDTH,
        ),
        name="local_terms",
    )(pre, gain_grad, grad, in_proj, items)


def tile_grads(query_ref, query_place, key_ref, key_place, key_column, weight, live):
    scale = HEAD_DIM ** (-0.5)
    queries = query_ref[query_place, :, :HEAD_DIM]
    outs = query_ref[query_place, :, HEAD_DIM : 2 * HEAD_DIM]
    if key_place is None:
        keys, values = (
            key_ref[:, :, column : column + HEAD_DIM].reshape(2 * TILE, HEAD_DIM)
            for column in (key_column, key_column + HEAD_DIM)
        )
    else:
        keys = key_ref[key_place, :, key_column : key_column + HEAD_DIM]
        values = key_ref[key_place, :, key_column + HEAD_DIM : key_column + 2 * HEAD_DIM]
    scores = dot(keys, queries, MATMUL_NT) * scale
    attn_grad = dot(values, outs, MATMUL_NT)
    squash = 0.5 + 0.5 * jnp.tanh(scores * 0.5)
    weighted = squash * weight
    if live is not None:
        weighted = jnp.where(live, weighted, 0.0)
    gated = scores * weighted
    attend = gated.astype(BF16)
    score_grad = (attn_grad * (weighted + gated * (1.0 - squash))).astype(BF16)
    return (
        dot(score_grad, keys, MATMUL_TN) * scale,
        dot(score_grad, queries, MATMUL) * scale,
        dot(attend, outs, MATMUL),
    )


def place_of_device():
    ctx = lax.axis_index("ctx")
    x = lax.div(ctx, Y_COUNT)
    y = lax.rem(ctx, Y_COUNT)
    core = lax.rem(lax.axis_index("table"), CORES)
    part = jnp.where(core == 0, lax.div(y, 2), lax.rem(y, 2))
    return (x ^ lax.div(x, 2)) & 1, part, core


def position(index, part, core):
    halves = part * TILE + index
    parities = (index // TOKENS) * TILE + part * TOKENS + index % TOKENS
    return jnp.where(core == 0, halves, parities)


def weight_of(length_ref):
    return jnp.full((1, 1), 1.0, F32) / jnp.full((1, 1), length_ref[0].astype(F32), F32)


def attend_near(length_ref, query_ref, own_ref, flip):
    _, part, core = place_of_device()
    weight = weight_of(length_ref)
    rows = lax.broadcasted_iota(jnp.int32, (2 * TILE, 1), 0)
    rows = jnp.where(rows < TILE, -1, position(rows - TILE, part, core))
    columns = position(lax.broadcasted_iota(jnp.int32, (1, TILE), 1), part ^ flip, core)
    live = rows <= columns
    column = 2 * HEAD_DIM
    low = tile_grads(query_ref, 0, own_ref, 0, column, weight, live[TILE:])
    high = tile_grads(query_ref, 1, own_ref, None, column, weight, live)
    return low, high


def attend_own_kernel(length_ref, own_ref, query_ref, key_ref):
    low, high = attend_near(length_ref, own_ref, own_ref, 0)
    query_ref[0] = low[0]
    query_ref[1] = high[0]
    key_ref[0, :, :HEAD_DIM] = low[1] + high[1][:TILE]
    key_ref[0, :, HEAD_DIM:] = low[2] + high[2][:TILE]
    key_ref[1, :, :HEAD_DIM] = high[1][TILE:]
    key_ref[1, :, HEAD_DIM:] = high[2][TILE:]


def attend_queries_kernel(
    length_ref, own_ref, query_far_ref, sums_ref, _, query_ref, key_ref
):
    low, high = attend_near(length_ref, query_far_ref, own_ref, 1)
    query_ref[0] = low[0]
    query_ref[1] = high[0]
    key_ref[0, :, :HEAD_DIM] = sums_ref[0, :, :HEAD_DIM] + (low[1] + high[1][:TILE])
    key_ref[0, :, HEAD_DIM:] = sums_ref[0, :, HEAD_DIM:] + (low[2] + high[2][:TILE])
    key_ref[1, :, :HEAD_DIM] = sums_ref[1, :, :HEAD_DIM] + high[1][TILE:]
    key_ref[1, :, HEAD_DIM:] = sums_ref[1, :, HEAD_DIM:] + high[2][TILE:]


def attend_keys_kernel(
    length_ref,
    own_ref,
    query_far_ref,
    key_far_ref,
    near_own_ref,
    near_far_ref,
    query_own_ref,
    query_send_ref,
    key_send_ref,
    query_acc,
    key_acc,
):
    pair, _, _ = place_of_device()
    weight = weight_of(length_ref)
    last = 1 - pair
    for place, (query_ref, near_ref) in enumerate(
        ((own_ref, near_own_ref), (query_far_ref, near_far_ref))
    ):
        query_acc[...] = near_ref[...]
        first = tile_grads(query_ref, 1, key_far_ref, 0, 0, weight, None)
        query_acc[1] += first[0]
        if place == 0:
            key_acc[0, :, :HEAD_DIM] = first[1]
            key_acc[0, :, HEAD_DIM:] = first[2]
            key_acc[1] = jnp.zeros_like(key_acc[1])
        else:
            key_acc[0, :, :HEAD_DIM] += first[1]
            key_acc[0, :, HEAD_DIM:] += first[2]
        second = tile_grads(query_ref, last, key_far_ref, last, 0, weight, None)
        query_acc[last] += second[0]
        key_acc[last, :, :HEAD_DIM] += second[1]
        key_acc[last, :, HEAD_DIM:] += second[2]
        if place == 0:
            query_own_ref[...] = query_acc[...]
        else:
            query_send_ref[...] = query_acc[...].astype(BF16)
    key_send_ref[...] = key_acc[...].astype(BF16)


def attend_cost(tiles):
    return pl.CostEstimate(
        flops=tiles * 5 * 2 * TILE * TILE * HEAD_DIM,
        bytes_accessed=2 << 20,
        transcendentals=tiles * TILE * TILE,
    )


QUERY_SUMS = jax.ShapeDtypeStruct((2, TILE, HEAD_DIM), F32)
KEY_SUMS = jax.ShapeDtypeStruct((2, TILE, 2 * HEAD_DIM), F32)


def attend_own(length, own):
    return pl.pallas_call(
        attend_own_kernel,
        out_shape=(QUERY_SUMS, KEY_SUMS),
        in_specs=[in_smem()] + in_vmem(1),
        out_specs=tuple(in_vmem(2)),
        compiler_params=params(),
        cost_estimate=attend_cost(3),
        name="attend_own",
    )(length, own)


def attend_queries(length, own, query_far, sums, codes):
    return pl.pallas_call(
        attend_queries_kernel,
        out_shape=(QUERY_SUMS, KEY_SUMS),
        in_specs=[in_smem()] + in_vmem(3) + [pl.BlockSpec(memory_space=pl.ANY)],
        out_specs=tuple(in_vmem(2)),
        compiler_params=params(),
        cost_estimate=attend_cost(3),
        name="attend_queries",
    )(length, own, query_far, sums, codes)


def attend_keys(length, own, query_far, key_far, near_own, near_far):
    return pl.pallas_call(
        attend_keys_kernel,
        out_shape=(
            QUERY_SUMS,
            jax.ShapeDtypeStruct((2, TILE, HEAD_DIM), BF16),
            jax.ShapeDtypeStruct((2, TILE, 2 * HEAD_DIM), BF16),
        ),
        in_specs=[in_smem()] + in_vmem(5),
        out_specs=tuple(in_vmem(3)),
        scratch_shapes=[
            pltpu.VMEM((2, TILE, HEAD_DIM), F32),
            pltpu.VMEM((2, TILE, 2 * HEAD_DIM), F32),
        ],
        compiler_params=params(),
        cost_estimate=attend_cost(4),
        name="attend_keys",
    )(length, own, query_far, key_far, near_own, near_far)


def join_kernel(query_own_ref, query_got_ref, key_own_ref, key_got_ref, out_ref):
    out_ref[:, :, :HEAD_DIM] = (
        key_own_ref[:, :, HEAD_DIM:] + key_got_ref[:, :, HEAD_DIM:].astype(F32)
    ).astype(BF16)
    out_ref[:, :, HEAD_DIM : 2 * HEAD_DIM] = (
        query_own_ref[...] + query_got_ref[...].astype(F32)
    ).astype(BF16)
    out_ref[:, :, 2 * HEAD_DIM :] = (
        key_own_ref[:, :, :HEAD_DIM] + key_got_ref[:, :, :HEAD_DIM].astype(F32)
    ).astype(BF16)


def join_parts(query_own, query_got, key_own, key_got):
    return pl.pallas_call(
        join_kernel,
        out_shape=jax.ShapeDtypeStruct((2, TILE, 3 * HEAD_DIM), BF16),
        in_specs=in_vmem(4),
        out_specs=in_vmem(1)[0],
        compiler_params=params(),
        name="join_parts",
    )(query_own, query_got, key_own, key_got)


def finish_kernel(
    grads_ref,
    slope_ref,
    gate_ref,
    base_ref,
    in_proj_ref,
    slot_ref,
    code_ref,
    proj_ref,
    rows_ref,
    wide_ref,
):
    proj_ref[:, :WIDTH] = gate_ref[...]
    for block in range(3):
        joined = jnp.concatenate(
            [
                grads_ref[head, :, block * HEAD_DIM : (block + 1) * HEAD_DIM].astype(F32)
                for head in range(HEADS)
            ],
            axis=1,
        )
        cols = slice((block + 1) * WIDTH, (block + 2) * WIDTH)
        proj_ref[:, cols] = (joined * slope_ref[:, block * WIDTH : (block + 1) * WIDTH]).astype(
            BF16
        )
    input_grad = base_ref[...] + dot(proj_ref[:, WIDTH:], in_proj_ref[:, WIDTH:], MATMUL_NT)
    high = input_grad.astype(BF16)
    low = (input_grad - high.astype(F32)).astype(BF16)
    order = lax.broadcasted_iota(jnp.int32, (TABLES * CAP, 1), 0)
    within = order % HALF_SLOTS
    slot_of = ((within % FARS) * CORES + order // HALF_SLOTS) * CAP + within // FARS
    picks = (slot_ref[...] == slot_of).astype(F32).astype(BF16)
    summed = dot(picks, high, MATMUL) + dot(picks, low, MATMUL)
    for x in range(X_COUNT):
        for core in range(CORES):
            target = x * CORES + core
            wide_ref[target, :HALF_SLOTS] = summed[
                core * HALF_SLOTS : (core + 1) * HALF_SLOTS, x * QUARTER : (x + 1) * QUARTER
            ]
            wide_ref[target, HALF_SLOTS:] = code_ref[core]
    rows_ref[...] = wide_ref[...].astype(BF16)


def finish(grads, slope, gate, base, in_proj, slots, codes):
    return pl.pallas_call(
        finish_kernel,
        out_shape=(
            pltpu.VMEM((TOKENS, 4 * WIDTH), BF16),
            jax.ShapeDtypeStruct((X_COUNT * CORES, NEAR_ROWS, QUARTER), BF16),
        ),
        in_specs=in_vmem(7),
        out_specs=tuple(in_vmem(2)),
        scratch_shapes=[pltpu.VMEM((X_COUNT * CORES, NEAR_ROWS, QUARTER), F32)],
        compiler_params=params(),
        name="finish",
    )(grads, slope, gate, base, in_proj, slots, codes)


def arrange_kernel(rows_ref, out_ref, wide_ref, packed_ref):
    givers = X_COUNT * CORES
    wide_ref[...] = rows_ref[...].astype(F32)
    for giver in range(givers):
        for level in range(CAP):
            packed_ref[pl.ds(giver * CAP + level, FARS, stride=FAR_ROWS), :] = wide_ref[
                giver, level * FARS : (level + 1) * FARS
            ]
    own = lax.rem(lax.div(lax.axis_index("table"), CORES), 4)
    coded = jnp.concatenate(
        [wide_ref[giver, HALF_SLOTS : HALF_SLOTS + 1] for giver in range(givers)], axis=0
    ).T
    giver = lax.broadcasted_iota(jnp.int32, (givers, 128), 0)
    lane = lax.broadcasted_iota(jnp.int32, (givers, 128), 1)
    for part in range(2):
        row = sum(
            dot(
                coded[
                    part * HALF_SLOTS + level * FARS : part * HALF_SLOTS + (level + 1) * FARS
                ].astype(BF16),
                (lane == own * FAR_SUMS + giver * CAP + level).astype(F32).astype(BF16),
                MATMUL,
            )
            for level in range(CAP)
        )
        packed_ref[pl.ds(FAR_SUMS + part, FARS, stride=FAR_ROWS), :] = row
    for row in range(FAR_SUMS + 2, FAR_ROWS):
        packed_ref[pl.ds(row, FARS, stride=FAR_ROWS), :] = jnp.zeros((FARS, 128), F32)
    out_ref[...] = packed_ref[...].astype(BF16)


def arrange_rows(rows):
    return pl.pallas_call(
        arrange_kernel,
        out_shape=jax.ShapeDtypeStruct((FARS * FAR_ROWS, QUARTER), BF16),
        in_specs=in_vmem(1),
        out_specs=in_vmem(1)[0],
        scratch_shapes=[
            pltpu.VMEM((X_COUNT * CORES, NEAR_ROWS, QUARTER), F32),
            pltpu.VMEM((FARS * FAR_ROWS, QUARTER), F32),
        ],
        compiler_params=params(),
        name="arrange_rows",
    )(rows)


def scatter_kernel(rows_ref, proj_ref, out_ref, proj_out, wide_ref, sem):
    copy = pltpu.make_async_copy(proj_ref, proj_out, sem)
    copy.start()
    targets = CTX_COUNT * ROWS_DEV
    wide_ref[...] = rows_ref[...].astype(F32)
    rows = wide_ref[:, :FAR_SUMS].reshape(FARS * FAR_SUMS, QUARTER).astype(BF16)
    ids = []
    for first in range(0, FARS, 4):
        coded = sum(wide_ref[far, FAR_SUMS : FAR_SUMS + 8] for far in range(first, first + 4))
        ids.append(coded[:1] * ROWS_DEV + coded[1:2])
    ids = jnp.concatenate(ids, axis=1).astype(jnp.int32)
    target = lax.broadcasted_iota(jnp.int32, (targets, 1), 0)
    hots = (ids == target).astype(F32).astype(BF16)
    out_ref[...] = dot(hots, rows, MATMUL).astype(BF16)
    copy.wait()


def scatter_rows(rows, proj):
    return pl.pallas_call(
        scatter_kernel,
        out_shape=(
            jax.ShapeDtypeStruct((CTX_COUNT * ROWS_DEV, QUARTER), BF16),
            jax.ShapeDtypeStruct((TOKENS, 4 * WIDTH), BF16),
        ),
        in_specs=in_vmem(2),
        out_specs=tuple(in_vmem(1) + in_hbm(1)),
        scratch_shapes=[
            pltpu.VMEM((FARS, FAR_ROWS, QUARTER), F32),
            pltpu.SemaphoreType.DMA(()),
        ],
        compiler_params=params(),
        name="scatter_rows",
    )(rows, proj)


def total_kernel(pieces_ref, out_ref):
    for x in range(X_COUNT):
        out_ref[:, x * QUARTER : (x + 1) * QUARTER] = sum(
            pieces_ref[x * Y_COUNT + y].astype(F32) for y in range(Y_COUNT)
        )


def total_rows(pieces):
    return pl.pallas_call(
        total_kernel,
        out_shape=jax.ShapeDtypeStruct((ROWS_DEV, WIDTH), F32),
        in_specs=in_vmem(1),
        out_specs=in_vmem(1)[0],
        compiler_params=params(),
        name="total_rows",
    )(pieces)


def per_device(
    item_inputs,
    attn_saved,
    out_grad,
    seq_lengths,
    token_slot,
    slot_rows,
    in_proj,
    out_proj,
    norm_gain,
):
    parts, pre, gain_grad = project(
        seq_lengths, item_inputs[0], attn_saved[0], out_grad[0], in_proj, out_proj, norm_gain[None]
    )
    own = lax.all_to_all(parts, AXES, 0, 0, axis_index_groups=HEAD_GROUPS)
    own = own.reshape(2, TILE, 4 * HEAD_DIM)
    query_far = lax.ppermute(own[:, :, : 2 * HEAD_DIM], AXES, SWAP_QUERY)
    key_far = lax.ppermute(own[:, :, 2 * HEAD_DIM :], AXES, SWAP_KEY)
    near_own, sums = attend_own(seq_lengths, own)
    slope, gate, base, codes = local_terms(pre, gain_grad, out_grad[0], in_proj, slot_rows)
    near_far, key_own = attend_queries(seq_lengths, own, query_far, sums, codes)
    query_own, query_send, key_send = attend_keys(
        seq_lengths, own, query_far, key_far, near_own, near_far
    )
    query_got = lax.ppermute(query_send, AXES, SWAP_QUERY)
    key_got = lax.ppermute(key_send, AXES, SWAP_KEY)
    joined = join_parts(query_own, query_got, key_own, key_got)
    grads = lax.all_to_all(
        joined.reshape(HEADS, TOKENS, 3 * HEAD_DIM), AXES, 0, 0, axis_index_groups=HEAD_GROUPS
    )
    proj_grad, rows = finish(grads, slope, gate, base, in_proj, token_slot, codes)
    rows = lax.all_to_all(rows, AXES, 0, 0, axis_index_groups=X_CORE_GROUPS)
    rows = arrange_rows(rows).reshape(FARS, FAR_ROWS, QUARTER)
    rows = lax.all_to_all(rows, "table", 0, 0, axis_index_groups=FAR_GROUPS)
    dense, proj_grad = scatter_rows(rows, proj_grad)
    pieces = lax.all_to_all(dense.reshape(CTX_COUNT, ROWS_DEV, QUARTER), "ctx", 0, 0)
    table_grad = total_rows(pieces)
    return (proj_grad[None], table_grad)


def solution(mesh):
    return jax.shard_map(
        per_device,
        mesh=mesh,
        in_specs=(
            P("table", "ctx", None),
            P("table", "ctx", None),
            P("table", "ctx", None),
            P("table"),
            P("table", "ctx"),
            P("table", "ctx"),
            P(),
            P(),
            P(),
        ),
        out_specs=(P("table", "ctx", None), P(("ctx", "table"), None)),
        check_vma=False,
    )
```

```python
import functools

import jax
import jax.numpy as jnp
from jax import lax
from jax.experimental import pallas as pl
from jax.experimental.pallas import tpu as pltpu
from jax.sharding import PartitionSpec as P

HEADS = 4
HEAD_DIM = 128
WIDTH = 512
TOKENS = 128
ROWS_DEV = 64
TABLES = 32
CAP = 4
CORES = 2
FARS = TABLES // CORES
QUARTER = 128
HALF_SLOTS = FARS * CAP
NEAR_ROWS = HALF_SLOTS + 8
FAR_SUMS = 4 * CORES * CAP
FAR_ROWS = FAR_SUMS + 8
X_COUNT = 4
Y_COUNT = 4
CTX_COUNT = X_COUNT * Y_COUNT
TILE = 2 * TOKENS
VMEM_LIMIT = 48 * 1024 * 1024
BF16 = jnp.bfloat16
F32 = jnp.float32

def device(x, y, table):
    return (x * Y_COUNT + y) * TABLES + table


def y_of(core, part, bit):
    return part * 2 + bit if core == 0 else bit * 2 + part


X_PAIRS = ((0, 3), (1, 2))
HEAD_GROUPS = [
    [
        device(X_PAIRS[pair][place], y_of(table % CORES, part, bit), table)
        for place in range(2)
        for bit in range(2)
    ]
    for pair in range(2)
    for part in range(2)
    for table in range(TABLES)
]
X_CORE_GROUPS = [
    [
        (x * Y_COUNT + y) * TABLES + far * CORES + core
        for x in range(X_COUNT)
        for core in range(CORES)
    ]
    for y in range(Y_COUNT)
    for far in range(FARS)
]
FAR_GROUPS = [[far * CORES + core for far in range(FARS)] for core in range(CORES)]
SWAP_QUERY = [
    (c * TABLES + t, (c ^ (2 if t % CORES == 0 else 1)) * TABLES + t)
    for c in range(CTX_COUNT)
    for t in range(TABLES)
]
SWAP_KEY = [
    (c * TABLES + t, (c ^ Y_COUNT) * TABLES + t) for c in range(CTX_COUNT) for t in range(TABLES)
]
AXES = ("ctx", "table")

MATMUL = (((1,), (0,)), ((), ()))
MATMUL_NT = (((1,), (1,)), ((), ()))
MATMUL_TN = (((0,), (0,)), ((), ()))


def dot(lhs, rhs, dims):
    return lax.dot_general(lhs, rhs, dims, preferred_element_type=F32)


def in_vmem(count):
    return [pl.BlockSpec(memory_space=pltpu.VMEM)] * count


def in_smem():
    return pl.BlockSpec(memory_space=pltpu.SMEM)


def in_hbm(count):
    return [pl.BlockSpec(memory_space=pltpu.HBM)] * count


def params(limit=VMEM_LIMIT):
    return pltpu.CompilerParams(vmem_limit_bytes=limit)


def project_kernel(
    length_ref,
    inputs_hbm,
    saved_hbm,
    grad_hbm,
    in_proj_hbm,
    out_proj_hbm,
    gain_hbm,
    parts_ref,
    pre_ref,
    gain_grad_ref,
    inputs_ref,
    saved_ref,
    grad_ref,
    in_proj_ref,
    out_proj_ref,
    gain_ref,
    sems,
):
    def copy_of(place, source, target):
        copy = pltpu.make_async_copy(source, target, sems.at[place])
        copy.start()
        return copy

    saved_copy = copy_of(0, saved_hbm, saved_ref)
    grad_copy = copy_of(1, grad_hbm, grad_ref)
    gain_copy = copy_of(2, gain_hbm, gain_ref)
    out_copy = copy_of(3, out_proj_hbm, out_proj_ref)
    inputs_copy = copy_of(4, inputs_hbm, inputs_ref)
    in_copies = [
        copy_of(
            5 + block,
            in_proj_hbm.at[:, block * WIDTH : (block + 1) * WIDTH],
            in_proj_ref.at[block],
        )
        for block in range(4)
    ]
    first = lax.axis_index("ctx") * TOKENS
    length = length_ref[0]
    saved_copy.wait()
    saved = saved_ref[...].astype(F32)
    row_mean = jnp.mean(saved, axis=1, keepdims=True)
    centred = saved - row_mean
    inv_std = lax.rsqrt(jnp.mean(centred * centred, axis=1, keepdims=True) + 1e-05)
    normed = centred * inv_std
    grad_copy.wait()
    gain_copy.wait()
    out_copy.wait()
    gain = gain_ref[...]
    grad = grad_ref[...]
    back = dot(grad, out_proj_ref[...], MATMUL_NT)

    inputs_copy.wait()
    in_copies[0].wait()
    inputs = inputs_ref[...]
    pre = dot(inputs, in_proj_ref[0], MATMUL)
    pre_ref[:, :WIDTH] = pre
    gating = (pre * jax.nn.sigmoid(pre)).astype(BF16).astype(F32)
    gain_grad_ref[...] = back * (normed * gain)
    carried = back * gating * gain
    out_attn = inv_std * (
        carried
        - jnp.mean(carried, axis=1, keepdims=True)
        - normed * jnp.mean(carried * normed, axis=1, keepdims=True)
    )
    position = first + lax.broadcasted_iota(jnp.int32, (TOKENS, 1), 0)
    out_attn = jnp.where(position < length, out_attn, 0.0).astype(BF16)
    for head in range(HEADS):
        cols = slice(head * HEAD_DIM, (head + 1) * HEAD_DIM)
        parts_ref[head, :, HEAD_DIM : 2 * HEAD_DIM] = out_attn[:, cols]
    for block, place in ((1, 3), (2, 0), (3, 2)):
        in_copies[block].wait()
        pre = dot(inputs, in_proj_ref[block], MATMUL)
        pre_ref[:, block * WIDTH : (block + 1) * WIDTH] = pre
        hidden = (pre * jax.nn.sigmoid(pre)).astype(BF16)
        for head in range(HEADS):
            cols = slice(head * HEAD_DIM, (head + 1) * HEAD_DIM)
            parts_ref[head, :, place * HEAD_DIM : (place + 1) * HEAD_DIM] = hidden[:, cols]


def project(length, *arrays):
    return pl.pallas_call(
        project_kernel,
        out_shape=(
            jax.ShapeDtypeStruct((HEADS, TOKENS, 4 * HEAD_DIM), BF16),
            jax.ShapeDtypeStruct((TOKENS, 4 * WIDTH), F32),
            jax.ShapeDtypeStruct((TOKENS, WIDTH), F32),
        ),
        in_specs=[in_smem()] + in_hbm(6),
        out_specs=tuple(in_vmem(3)),
        scratch_shapes=[
            pltpu.VMEM((TOKENS, WIDTH), BF16),
            pltpu.VMEM((TOKENS, WIDTH), BF16),
            pltpu.VMEM((TOKENS, WIDTH), BF16),
            pltpu.VMEM((4, WIDTH, WIDTH), BF16),
            pltpu.VMEM((WIDTH, WIDTH), BF16),
            pltpu.VMEM((1, WIDTH), F32),
            pltpu.SemaphoreType.DMA((9,)),
        ],
        compiler_params=params(),
        name="project",
    )(length, *(pltpu.with_memory_space_constraint(array, pltpu.HBM) for array in arrays))


def local_kernel(
    pre_ref, gain_grad_ref, grad_ref, in_proj_ref, item_ref, slope_ref, gate_ref, base_ref, code_ref
):
    pre = pre_ref[...]
    squash = jax.nn.sigmoid(pre)
    slope = squash * (1.0 + pre * (1.0 - squash))
    slope_ref[...] = slope[:, WIDTH:]
    gate = (gain_grad_ref[...] * slope[:, :WIDTH]).astype(BF16)
    gate_ref[...] = gate
    base_ref[...] = grad_ref[...].astype(F32) + dot(gate, in_proj_ref[:, :WIDTH], MATMUL_NT)
    items = item_ref[...]
    owner_of = (items // (ROWS_DEV * TABLES)).astype(F32)
    place_of = (items % ROWS_DEV).astype(F32)
    slot = lax.broadcasted_iota(jnp.int32, (TABLES * CAP, 128), 0)
    lane = lax.broadcasted_iota(jnp.int32, (TABLES * CAP, 128), 1)
    wanted = lane % HALF_SLOTS
    wanted = (wanted % FARS) * (CORES * CAP) + wanted // FARS
    for core in range(CORES):
        match = slot == wanted + core * CAP
        row = sum(
            dot(
                jnp.broadcast_to(values, (8, 128)).astype(BF16),
                (match & (lane // HALF_SLOTS == part)).astype(F32).astype(BF16),
                MATMUL,
            )
            for part, values in enumerate((owner_of, place_of))
        )
        first = lax.broadcasted_iota(jnp.int32, (8, 128), 0) == 0
        code_ref[core] = jnp.where(first, row, 0.0)


def local_terms(pre, gain_grad, grad, in_proj, items):
    return pl.pallas_call(
        local_kernel,
        out_shape=(
            jax.ShapeDtypeStruct((TOKENS, 3 * WIDTH), F32),
            jax.ShapeDtypeStruct((TOKENS, WIDTH), BF16),
            jax.ShapeDtypeStruct((TOKENS, WIDTH), F32),
            jax.ShapeDtypeStruct((CORES, 8, 128), F32),
        ),
        in_specs=in_vmem(5),
        out_specs=tuple(in_vmem(4)),
        compiler_params=params(),
        cost_estimate=pl.CostEstimate(
            flops=2 * TOKENS * WIDTH * WIDTH,
            bytes_accessed=3 << 20,
            transcendentals=TOKENS * 4 * WIDTH,
        ),
        name="local_terms",
    )(pre, gain_grad, grad, in_proj, items)


def tile_grads(queries, outs, keys, values, weight, live):
    scale = HEAD_DIM ** (-0.5)
    scores = dot(keys, queries, MATMUL_NT) * scale
    attn_grad = dot(values, outs, MATMUL_NT)
    squash = 0.5 + 0.5 * jnp.tanh(scores * 0.5)
    weighted = squash * weight
    if live is not None:
        weighted = jnp.where(live, weighted, 0.0)
    gated = scores * weighted
    attend = gated.astype(BF16)
    score_grad = (attn_grad * (weighted + gated * (1.0 - squash))).astype(BF16)
    return (
        dot(score_grad, keys, MATMUL_TN) * scale,
        dot(score_grad, queries, MATMUL) * scale,
        dot(attend, outs, MATMUL),
    )


def two_of(ref, place, column):
    blocks = (slice(column, column + HEAD_DIM), slice(column + HEAD_DIM, column + 2 * HEAD_DIM))
    if place is None:
        return [ref[:, :, block].reshape(2 * TILE, HEAD_DIM) for block in blocks]
    return [ref[place, :, block] for block in blocks]


def place_of_device():
    ctx = lax.axis_index("ctx")
    x = lax.div(ctx, Y_COUNT)
    y = lax.rem(ctx, Y_COUNT)
    core = lax.rem(lax.axis_index("table"), CORES)
    part = jnp.where(core == 0, lax.div(y, 2), lax.rem(y, 2))
    return (x ^ lax.div(x, 2)) & 1, part, core


def position(index, part, core):
    halves = part * TILE + index
    parities = (index // TOKENS) * TILE + part * TOKENS + index % TOKENS
    return jnp.where(core == 0, halves, parities)


def weight_of(length_ref):
    return jnp.full((1, 1), 1.0, F32) / jnp.full((1, 1), length_ref[0].astype(F32), F32)


def attend_near(length_ref, query_ref, own_ref, flip):
    _, part, core = place_of_device()
    weight = weight_of(length_ref)
    rows = lax.broadcasted_iota(jnp.int32, (2 * TILE, 1), 0)
    rows = jnp.where(rows < TILE, -1, position(rows - TILE, part, core))
    columns = position(lax.broadcasted_iota(jnp.int32, (1, TILE), 1), part ^ flip, core)
    live = rows <= columns
    column = 2 * HEAD_DIM
    low = tile_grads(*two_of(query_ref, 0, 0), *two_of(own_ref, 0, column), weight, live[TILE:])
    high = tile_grads(*two_of(query_ref, 1, 0), *two_of(own_ref, None, column), weight, live)
    return low, high


def attend_own_kernel(length_ref, own_ref, query_ref, key_ref):
    low, high = attend_near(length_ref, own_ref, own_ref, 0)
    query_ref[0] = low[0]
    query_ref[1] = high[0]
    key_ref[0, :, :HEAD_DIM] = low[1] + high[1][:TILE]
    key_ref[0, :, HEAD_DIM:] = low[2] + high[2][:TILE]
    key_ref[1, :, :HEAD_DIM] = high[1][TILE:]
    key_ref[1, :, HEAD_DIM:] = high[2][TILE:]


def attend_queries_kernel(
    length_ref, own_ref, query_far_ref, sums_ref, _, query_ref, key_ref
):
    low, high = attend_near(length_ref, query_far_ref, own_ref, 1)
    query_ref[0] = low[0]
    query_ref[1] = high[0]
    key_ref[0, :, :HEAD_DIM] = sums_ref[0, :, :HEAD_DIM] + (low[1] + high[1][:TILE])
    key_ref[0, :, HEAD_DIM:] = sums_ref[0, :, HEAD_DIM:] + (low[2] + high[2][:TILE])
    key_ref[1, :, :HEAD_DIM] = sums_ref[1, :, :HEAD_DIM] + high[1][TILE:]
    key_ref[1, :, HEAD_DIM:] = sums_ref[1, :, HEAD_DIM:] + high[2][TILE:]


def attend_keys_kernel(
    length_ref,
    own_ref,
    query_far_ref,
    key_far_ref,
    near_own_ref,
    near_far_ref,
    query_own_ref,
    query_send_ref,
    key_send_ref,
    query_acc,
    key_acc,
):
    pair, _, _ = place_of_device()
    weight = weight_of(length_ref)
    last = 1 - pair
    query_own_ref[...] = near_own_ref[...]
    query_acc[...] = near_far_ref[...]
    key_acc[1] = jnp.zeros_like(key_acc[1])
    for query_tile, key_tile in ((1, 0), (last, last)):
        queries, outs = (
            jnp.concatenate(both, axis=0)
            for both in zip(two_of(own_ref, query_tile, 0), two_of(query_far_ref, query_tile, 0))
        )
        query_part, key_part, value_part = tile_grads(
            queries, outs, *two_of(key_far_ref, key_tile, 0), weight, None
        )
        query_own_ref[query_tile] += query_part[:TILE]
        query_acc[query_tile] += query_part[TILE:]
        if key_tile is not last:
            key_acc[0, :, :HEAD_DIM] = key_part
            key_acc[0, :, HEAD_DIM:] = value_part
        else:
            key_acc[last, :, :HEAD_DIM] += key_part
            key_acc[last, :, HEAD_DIM:] += value_part
    query_send_ref[...] = query_acc[...].astype(BF16)
    key_send_ref[...] = key_acc[...].astype(BF16)


def attend_cost(tiles):
    return pl.CostEstimate(
        flops=tiles * 5 * 2 * TILE * TILE * HEAD_DIM,
        bytes_accessed=2 << 20,
        transcendentals=tiles * TILE * TILE,
    )


QUERY_SUMS = jax.ShapeDtypeStruct((2, TILE, HEAD_DIM), F32)
KEY_SUMS = jax.ShapeDtypeStruct((2, TILE, 2 * HEAD_DIM), F32)


def attend_own(length, own):
    return pl.pallas_call(
        attend_own_kernel,
        out_shape=(QUERY_SUMS, KEY_SUMS),
        in_specs=[in_smem()] + in_vmem(1),
        out_specs=tuple(in_vmem(2)),
        compiler_params=params(),
        cost_estimate=attend_cost(3),
        name="attend_own",
    )(length, own)


def attend_queries(length, own, query_far, sums, codes):
    return pl.pallas_call(
        attend_queries_kernel,
        out_shape=(QUERY_SUMS, KEY_SUMS),
        in_specs=[in_smem()] + in_vmem(3) + [pl.BlockSpec(memory_space=pl.ANY)],
        out_specs=tuple(in_vmem(2)),
        compiler_params=params(),
        cost_estimate=attend_cost(3),
        name="attend_queries",
    )(length, own, query_far, sums, codes)


def attend_keys(length, own, query_far, key_far, near_own, near_far):
    return pl.pallas_call(
        attend_keys_kernel,
        out_shape=(
            QUERY_SUMS,
            jax.ShapeDtypeStruct((2, TILE, HEAD_DIM), BF16),
            jax.ShapeDtypeStruct((2, TILE, 2 * HEAD_DIM), BF16),
        ),
        in_specs=[in_smem()] + in_vmem(5),
        out_specs=tuple(in_vmem(3)),
        scratch_shapes=[
            pltpu.VMEM((2, TILE, HEAD_DIM), F32),
            pltpu.VMEM((2, TILE, 2 * HEAD_DIM), F32),
        ],
        compiler_params=params(),
        cost_estimate=attend_cost(4),
        name="attend_keys",
    )(length, own, query_far, key_far, near_own, near_far)


def join_kernel(query_own_ref, query_got_ref, key_own_ref, key_got_ref, out_ref):
    out_ref[:, :, :HEAD_DIM] = (
        key_own_ref[:, :, HEAD_DIM:] + key_got_ref[:, :, HEAD_DIM:].astype(F32)
    ).astype(BF16)
    out_ref[:, :, HEAD_DIM : 2 * HEAD_DIM] = (
        query_own_ref[...] + query_got_ref[...].astype(F32)
    ).astype(BF16)
    out_ref[:, :, 2 * HEAD_DIM :] = (
        key_own_ref[:, :, :HEAD_DIM] + key_got_ref[:, :, :HEAD_DIM].astype(F32)
    ).astype(BF16)


def join_parts(query_own, query_got, key_own, key_got):
    return pl.pallas_call(
        join_kernel,
        out_shape=jax.ShapeDtypeStruct((2, TILE, 3 * HEAD_DIM), BF16),
        in_specs=in_vmem(4),
        out_specs=in_vmem(1)[0],
        compiler_params=params(),
        name="join_parts",
    )(query_own, query_got, key_own, key_got)


def finish_kernel(
    grads_ref,
    slope_ref,
    gate_ref,
    base_ref,
    in_proj_ref,
    slot_ref,
    code_ref,
    proj_ref,
    rows_ref,
    wide_ref,
):
    proj_ref[:, :WIDTH] = gate_ref[...]
    for block in range(3):
        joined = jnp.concatenate(
            [
                grads_ref[head, :, block * HEAD_DIM : (block + 1) * HEAD_DIM].astype(F32)
                for head in range(HEADS)
            ],
            axis=1,
        )
        cols = slice((block + 1) * WIDTH, (block + 2) * WIDTH)
        proj_ref[:, cols] = (joined * slope_ref[:, block * WIDTH : (block + 1) * WIDTH]).astype(
            BF16
        )
    input_grad = base_ref[...] + dot(proj_ref[:, WIDTH:], in_proj_ref[:, WIDTH:], MATMUL_NT)
    high = input_grad.astype(BF16)
    low = (input_grad - high.astype(F32)).astype(BF16)
    order = lax.broadcasted_iota(jnp.int32, (TABLES * CAP, 1), 0)
    within = order % HALF_SLOTS
    slot_of = ((within % FARS) * CORES + order // HALF_SLOTS) * CAP + within // FARS
    picks = (slot_ref[...] == slot_of).astype(F32).astype(BF16)
    summed = dot(picks, high, MATMUL) + dot(picks, low, MATMUL)
    for x in range(X_COUNT):
        for core in range(CORES):
            target = x * CORES + core
            wide_ref[target, :HALF_SLOTS] = summed[
                core * HALF_SLOTS : (core + 1) * HALF_SLOTS, x * QUARTER : (x + 1) * QUARTER
            ]
            wide_ref[target, HALF_SLOTS:] = code_ref[core]
    rows_ref[...] = wide_ref[...].astype(BF16)


def finish(grads, slope, gate, base, in_proj, slots, codes):
    return pl.pallas_call(
        finish_kernel,
        out_shape=(
            pltpu.VMEM((TOKENS, 4 * WIDTH), BF16),
            jax.ShapeDtypeStruct((X_COUNT * CORES, NEAR_ROWS, QUARTER), BF16),
        ),
        in_specs=in_vmem(7),
        out_specs=tuple(in_vmem(2)),
        scratch_shapes=[pltpu.VMEM((X_COUNT * CORES, NEAR_ROWS, QUARTER), F32)],
        compiler_params=params(),
        name="finish",
    )(grads, slope, gate, base, in_proj, slots, codes)


def arrange_kernel(rows_ref, out_ref, wide_ref, packed_ref):
    givers = X_COUNT * CORES
    wide_ref[...] = rows_ref[...].astype(F32)
    for giver in range(givers):
        for level in range(CAP):
            packed_ref[pl.ds(giver * CAP + level, FARS, stride=FAR_ROWS), :] = wide_ref[
                giver, level * FARS : (level + 1) * FARS
            ]
    own = lax.rem(lax.div(lax.axis_index("table"), CORES), 4)
    coded = jnp.concatenate(
        [wide_ref[giver, HALF_SLOTS : HALF_SLOTS + 1] for giver in range(givers)], axis=0
    ).T
    giver = lax.broadcasted_iota(jnp.int32, (givers, 128), 0)
    lane = lax.broadcasted_iota(jnp.int32, (givers, 128), 1)
    for part in range(2):
        row = sum(
            dot(
                coded[
                    part * HALF_SLOTS + level * FARS : part * HALF_SLOTS + (level + 1) * FARS
                ].astype(BF16),
                (lane == own * FAR_SUMS + giver * CAP + level).astype(F32).astype(BF16),
                MATMUL,
            )
            for level in range(CAP)
        )
        packed_ref[pl.ds(FAR_SUMS + part, FARS, stride=FAR_ROWS), :] = row
    for row in range(FAR_SUMS + 2, FAR_ROWS):
        packed_ref[pl.ds(row, FARS, stride=FAR_ROWS), :] = jnp.zeros((FARS, 128), F32)
    out_ref[...] = packed_ref[: FARS * FAR_ROWS].astype(BF16)


def arrange_rows(rows):
    return pl.pallas_call(
        arrange_kernel,
        out_shape=jax.ShapeDtypeStruct((FARS * FAR_ROWS, QUARTER), BF16),
        in_specs=in_vmem(1),
        out_specs=in_vmem(1)[0],
        scratch_shapes=[
            pltpu.VMEM((X_COUNT * CORES, NEAR_ROWS, QUARTER), F32),
            pltpu.VMEM(((FARS + 1) * FAR_ROWS, QUARTER), F32),
        ],
        compiler_params=params(),
        name="arrange_rows",
    )(rows)


def scatter_kernel(rows_ref, proj_ref, out_ref, proj_out, wide_ref, sem):
    copy = pltpu.make_async_copy(proj_ref, proj_out, sem)
    copy.start()
    targets = CTX_COUNT * ROWS_DEV
    wide_ref[...] = rows_ref[...].astype(F32)
    rows = wide_ref[:, :FAR_SUMS].reshape(FARS * FAR_SUMS, QUARTER).astype(BF16)
    ids = []
    for first in range(0, FARS, 4):
        coded = sum(wide_ref[far, FAR_SUMS : FAR_SUMS + 8] for far in range(first, first + 4))
        ids.append(coded[:1] * ROWS_DEV + coded[1:2])
    ids = jnp.concatenate(ids, axis=1).astype(jnp.int32)
    target = lax.broadcasted_iota(jnp.int32, (targets, 1), 0)
    hots = (ids == target).astype(F32).astype(BF16)
    out_ref[...] = dot(hots, rows, MATMUL).astype(BF16)
    copy.wait()


def scatter_rows(rows, proj):
    return pl.pallas_call(
        scatter_kernel,
        out_shape=(
            jax.ShapeDtypeStruct((CTX_COUNT * ROWS_DEV, QUARTER), BF16),
            jax.ShapeDtypeStruct((TOKENS, 4 * WIDTH), BF16),
        ),
        in_specs=in_vmem(2),
        out_specs=tuple(in_vmem(1) + in_hbm(1)),
        scratch_shapes=[
            pltpu.VMEM((FARS, FAR_ROWS, QUARTER), F32),
            pltpu.SemaphoreType.DMA(()),
        ],
        compiler_params=params(),
        name="scatter_rows",
    )(rows, proj)


def total_kernel(pieces_ref, out_ref):
    for x in range(X_COUNT):
        out_ref[:, x * QUARTER : (x + 1) * QUARTER] = sum(
            pieces_ref[x * Y_COUNT + y].astype(F32) for y in range(Y_COUNT)
        )


def total_rows(pieces):
    return pl.pallas_call(
        total_kernel,
        out_shape=jax.ShapeDtypeStruct((ROWS_DEV, WIDTH), F32),
        in_specs=in_vmem(1),
        out_specs=in_vmem(1)[0],
        compiler_params=params(),
        name="total_rows",
    )(pieces)


def per_device(
    item_inputs,
    attn_saved,
    out_grad,
    seq_lengths,
    token_slot,
    slot_rows,
    in_proj,
    out_proj,
    norm_gain,
):
    parts, pre, gain_grad = project(
        seq_lengths, item_inputs[0], attn_saved[0], out_grad[0], in_proj, out_proj, norm_gain[None]
    )
    own = lax.all_to_all(parts, AXES, 0, 0, axis_index_groups=HEAD_GROUPS)
    own = own.reshape(2, TILE, 4 * HEAD_DIM)
    query_far = lax.ppermute(own[:, :, : 2 * HEAD_DIM], AXES, SWAP_QUERY)
    key_far = lax.ppermute(own[:, :, 2 * HEAD_DIM :], AXES, SWAP_KEY)
    near_own, sums = attend_own(seq_lengths, own)
    slope, gate, base, codes = local_terms(pre, gain_grad, out_grad[0], in_proj, slot_rows)
    near_far, key_own = attend_queries(seq_lengths, own, query_far, sums, codes)
    query_own, query_send, key_send = attend_keys(
        seq_lengths, own, query_far, key_far, near_own, near_far
    )
    query_got = lax.ppermute(query_send, AXES, SWAP_QUERY)
    key_got = lax.ppermute(key_send, AXES, SWAP_KEY)
    joined = join_parts(query_own, query_got, key_own, key_got)
    grads = lax.all_to_all(
        joined.reshape(HEADS, TOKENS, 3 * HEAD_DIM), AXES, 0, 0, axis_index_groups=HEAD_GROUPS
    )
    proj_grad, rows = finish(grads, slope, gate, base, in_proj, token_slot, codes)
    rows = lax.all_to_all(rows, AXES, 0, 0, axis_index_groups=X_CORE_GROUPS)
    rows = arrange_rows(rows).reshape(FARS, FAR_ROWS, QUARTER)
    rows = lax.all_to_all(rows, "table", 0, 0, axis_index_groups=FAR_GROUPS)
    dense, proj_grad = scatter_rows(rows, proj_grad)
    pieces = lax.all_to_all(dense.reshape(CTX_COUNT, ROWS_DEV, QUARTER), "ctx", 0, 0)
    table_grad = total_rows(pieces)
    return (proj_grad[None], table_grad)


def solution(mesh):
    return jax.shard_map(
        per_device,
        mesh=mesh,
        in_specs=(
            P("table", "ctx", None),
            P("table", "ctx", None),
            P("table", "ctx", None),
            P("table"),
            P("table", "ctx"),
            P("table", "ctx"),
            P(),
            P(),
            P(),
        ),
        out_specs=(P("table", "ctx", None), P(("ctx", "table"), None)),
        check_vma=False,
    )
```

```python
import functools

import jax
import jax.numpy as jnp
from jax import lax
from jax.experimental import pallas as pl
from jax.experimental.pallas import tpu as pltpu
from jax.sharding import PartitionSpec as P

HEADS = 4
HEAD_DIM = 128
WIDTH = 512
TOKENS = 128
ROWS_DEV = 64
TABLES = 32
CAP = 4
CORES = 2
FARS = TABLES // CORES
QUARTER = 128
HALF_SLOTS = FARS * CAP
NEAR_ROWS = HALF_SLOTS + 8
FAR_SUMS = 4 * CORES * CAP
FAR_ROWS = FAR_SUMS + 8
X_COUNT = 4
Y_COUNT = 4
HALF = TOKENS // 2
CTX_COUNT = X_COUNT * Y_COUNT
TILE = 2 * TOKENS
VMEM_LIMIT = 48 * 1024 * 1024
BF16 = jnp.bfloat16
F32 = jnp.float32

def device(x, y, table):
    return (x * Y_COUNT + y) * TABLES + table


def y_of(core, part, bit):
    return part * 2 + bit if core == 0 else bit * 2 + part


X_PAIRS = ((0, 3), (1, 2))
HEAD_GROUPS = [
    [
        device(X_PAIRS[pair][place], y_of(table % CORES, part, bit), table)
        for place in range(2)
        for bit in range(2)
    ]
    for pair in range(2)
    for part in range(2)
    for table in range(TABLES)
]
X_CORE_GROUPS = [
    [
        (x * Y_COUNT + y) * TABLES + far * CORES + core
        for x in range(X_COUNT)
        for core in range(CORES)
    ]
    for y in range(Y_COUNT)
    for far in range(FARS)
]
FAR_GROUPS = [[far * CORES + core for far in range(FARS)] for core in range(CORES)]
SWAP_QUERY = [
    (c * TABLES + t, (c ^ (2 if t % CORES == 0 else 1)) * TABLES + t)
    for c in range(CTX_COUNT)
    for t in range(TABLES)
]
SWAP_KEY = [
    (c * TABLES + t, (c ^ Y_COUNT) * TABLES + t) for c in range(CTX_COUNT) for t in range(TABLES)
]
AXES = ("ctx", "table")

MATMUL = (((1,), (0,)), ((), ()))
MATMUL_NT = (((1,), (1,)), ((), ()))
MATMUL_TN = (((0,), (0,)), ((), ()))


def dot(lhs, rhs, dims):
    return lax.dot_general(lhs, rhs, dims, preferred_element_type=F32)


def in_vmem(count):
    return [pl.BlockSpec(memory_space=pltpu.VMEM)] * count


def in_smem():
    return pl.BlockSpec(memory_space=pltpu.SMEM)


def in_hbm(count):
    return [pl.BlockSpec(memory_space=pltpu.HBM)] * count


def params(limit=VMEM_LIMIT):
    return pltpu.CompilerParams(vmem_limit_bytes=limit)


def project_kernel(
    length_ref,
    inputs_hbm,
    saved_hbm,
    grad_hbm,
    in_proj_hbm,
    out_proj_hbm,
    gain_hbm,
    parts_ref,
    pre_ref,
    gain_grad_ref,
    inputs_ref,
    saved_ref,
    grad_ref,
    in_proj_ref,
    out_proj_ref,
    gain_ref,
    sems,
):
    def copy_of(place, source, target):
        copy = pltpu.make_async_copy(source, target, sems.at[place])
        copy.start()
        return copy

    saved_copy = copy_of(0, saved_hbm, saved_ref)
    grad_copy = copy_of(1, grad_hbm, grad_ref)
    gain_copy = copy_of(2, gain_hbm, gain_ref)
    out_copy = copy_of(3, out_proj_hbm, out_proj_ref)
    inputs_copy = copy_of(4, inputs_hbm, inputs_ref)
    in_copies = [
        copy_of(
            5 + block,
            in_proj_hbm.at[:, block * WIDTH : (block + 1) * WIDTH],
            in_proj_ref.at[block],
        )
        for block in range(4)
    ]
    first = lax.axis_index("ctx") * TOKENS
    length = length_ref[0]
    saved_copy.wait()
    saved = saved_ref[...].astype(F32)
    row_mean = jnp.mean(saved, axis=1, keepdims=True)
    centred = saved - row_mean
    inv_std = lax.rsqrt(jnp.mean(centred * centred, axis=1, keepdims=True) + 1e-05)
    normed = centred * inv_std
    grad_copy.wait()
    gain_copy.wait()
    out_copy.wait()
    gain = gain_ref[...]
    grad = grad_ref[...]
    back = dot(grad, out_proj_ref[...], MATMUL_NT)

    inputs_copy.wait()
    in_copies[0].wait()
    inputs = inputs_ref[...]
    pre = dot(inputs, in_proj_ref[0], MATMUL)
    pre_ref[:, :WIDTH] = pre
    gating = (pre * jax.nn.sigmoid(pre)).astype(BF16).astype(F32)
    gain_grad_ref[...] = back * (normed * gain)
    carried = back * gating * gain
    out_attn = inv_std * (
        carried
        - jnp.mean(carried, axis=1, keepdims=True)
        - normed * jnp.mean(carried * normed, axis=1, keepdims=True)
    )
    position = first + lax.broadcasted_iota(jnp.int32, (TOKENS, 1), 0)
    out_attn = jnp.where(position < length, out_attn, 0.0).astype(BF16)
    for head in range(HEADS):
        cols = slice(head * HEAD_DIM, (head + 1) * HEAD_DIM)
        parts_ref[head, :, HEAD_DIM : 2 * HEAD_DIM] = out_attn[:, cols]
    for block, place in ((1, 3), (2, 0), (3, 2)):
        in_copies[block].wait()
        pre = dot(inputs, in_proj_ref[block], MATMUL)
        pre_ref[:, block * WIDTH : (block + 1) * WIDTH] = pre
        hidden = (pre * jax.nn.sigmoid(pre)).astype(BF16)
        for head in range(HEADS):
            cols = slice(head * HEAD_DIM, (head + 1) * HEAD_DIM)
            parts_ref[head, :, place * HEAD_DIM : (place + 1) * HEAD_DIM] = hidden[:, cols]


def project(length, *arrays):
    return pl.pallas_call(
        project_kernel,
        out_shape=(
            jax.ShapeDtypeStruct((HEADS, TOKENS, 4 * HEAD_DIM), BF16),
            jax.ShapeDtypeStruct((TOKENS, 4 * WIDTH), F32),
            jax.ShapeDtypeStruct((TOKENS, WIDTH), F32),
        ),
        in_specs=[in_smem()] + in_hbm(6),
        out_specs=tuple(in_vmem(3)),
        scratch_shapes=[
            pltpu.VMEM((TOKENS, WIDTH), BF16),
            pltpu.VMEM((TOKENS, WIDTH), BF16),
            pltpu.VMEM((TOKENS, WIDTH), BF16),
            pltpu.VMEM((4, WIDTH, WIDTH), BF16),
            pltpu.VMEM((WIDTH, WIDTH), BF16),
            pltpu.VMEM((1, WIDTH), F32),
            pltpu.SemaphoreType.DMA((9,)),
        ],
        compiler_params=params(),
        name="project",
    )(length, *(pltpu.with_memory_space_constraint(array, pltpu.HBM) for array in arrays))


def local_kernel(
    pre_ref, gain_grad_ref, grad_ref, in_proj_ref, item_ref, slope_ref, gate_ref, base_ref, code_ref
):
    pre = pre_ref[...]
    squash = jax.nn.sigmoid(pre)
    slope = squash * (1.0 + pre * (1.0 - squash))
    slope_ref[...] = slope[:, WIDTH:]
    gate = (gain_grad_ref[...] * slope[:, :WIDTH]).astype(BF16)
    gate_ref[...] = gate
    base_ref[...] = grad_ref[...].astype(F32) + dot(gate, in_proj_ref[:, :WIDTH], MATMUL_NT)
    items = item_ref[...]
    owner_of = (items // (ROWS_DEV * TABLES)).astype(F32)
    place_of = (items % ROWS_DEV).astype(F32)
    slot = lax.broadcasted_iota(jnp.int32, (TABLES * CAP, 128), 0)
    lane = lax.broadcasted_iota(jnp.int32, (TABLES * CAP, 128), 1)
    wanted = lane % HALF_SLOTS
    wanted = (wanted % FARS) * (CORES * CAP) + wanted // FARS
    for core in range(CORES):
        match = slot == wanted + core * CAP
        row = sum(
            dot(
                jnp.broadcast_to(values, (8, 128)).astype(BF16),
                (match & (lane // HALF_SLOTS == part)).astype(F32).astype(BF16),
                MATMUL,
            )
            for part, values in enumerate((owner_of, place_of))
        )
        first = lax.broadcasted_iota(jnp.int32, (8, 128), 0) == 0
        code_ref[core] = jnp.where(first, row, 0.0)


def local_terms(pre, gain_grad, grad, in_proj, items):
    return pl.pallas_call(
        local_kernel,
        out_shape=(
            jax.ShapeDtypeStruct((TOKENS, 3 * WIDTH), F32),
            jax.ShapeDtypeStruct((TOKENS, WIDTH), BF16),
            jax.ShapeDtypeStruct((TOKENS, WIDTH), F32),
            jax.ShapeDtypeStruct((CORES, 8, 128), F32),
        ),
        in_specs=in_vmem(5),
        out_specs=tuple(in_vmem(4)),
        compiler_params=params(),
        cost_estimate=pl.CostEstimate(
            flops=2 * TOKENS * WIDTH * WIDTH,
            bytes_accessed=3 << 20,
            transcendentals=TOKENS * 4 * WIDTH,
        ),
        name="local_terms",
    )(pre, gain_grad, grad, in_proj, items)


def tile_grads(queries, outs, keys, values, weight, live):
    scale = HEAD_DIM ** (-0.5)
    scores = dot(keys, queries, MATMUL_NT) * scale
    attn_grad = dot(values, outs, MATMUL_NT)
    squash = 0.5 + 0.5 * jnp.tanh(scores * 0.5)
    weighted = squash * weight
    if live is not None:
        weighted = jnp.where(live, weighted, 0.0)
    gated = scores * weighted
    attend = gated.astype(BF16)
    score_grad = (attn_grad * (weighted + gated * (1.0 - squash))).astype(BF16)
    return (
        dot(score_grad, keys, MATMUL_TN) * scale,
        dot(score_grad, queries, MATMUL) * scale,
        dot(attend, outs, MATMUL),
    )


def two_of(ref, place, column):
    blocks = (slice(column, column + HEAD_DIM), slice(column + HEAD_DIM, column + 2 * HEAD_DIM))
    if place is None:
        return [ref[:, :, block].reshape(2 * TILE, HEAD_DIM) for block in blocks]
    return [ref[place, :, block] for block in blocks]


def place_of_device():
    ctx = lax.axis_index("ctx")
    x = lax.div(ctx, Y_COUNT)
    y = lax.rem(ctx, Y_COUNT)
    core = lax.rem(lax.axis_index("table"), CORES)
    part = jnp.where(core == 0, lax.div(y, 2), lax.rem(y, 2))
    return (x ^ lax.div(x, 2)) & 1, part, core


def position(index, part, core):
    halves = part * TILE + index
    parities = (index // TOKENS) * TILE + part * TOKENS + index % TOKENS
    return jnp.where(core == 0, halves, parities)


def weight_of(length_ref):
    return jnp.full((1, 1), 1.0, F32) / jnp.full((1, 1), length_ref[0].astype(F32), F32)


def attend_near(length_ref, query_ref, own_ref, flip):
    _, part, core = place_of_device()
    weight = weight_of(length_ref)
    rows = lax.broadcasted_iota(jnp.int32, (2 * TILE, 1), 0)
    rows = jnp.where(rows < TILE, -1, position(rows - TILE, part, core))
    columns = position(lax.broadcasted_iota(jnp.int32, (1, TILE), 1), part ^ flip, core)
    live = rows <= columns
    column = 2 * HEAD_DIM
    low = tile_grads(*two_of(query_ref, 0, 0), *two_of(own_ref, 0, column), weight, live[TILE:])
    high = tile_grads(*two_of(query_ref, 1, 0), *two_of(own_ref, None, column), weight, live)
    return low, high


def attend_own_kernel(length_ref, own_ref, query_ref, key_ref):
    low, high = attend_near(length_ref, own_ref, own_ref, 0)
    query_ref[0] = low[0]
    query_ref[1] = high[0]
    key_ref[0, :, :HEAD_DIM] = low[1] + high[1][:TILE]
    key_ref[0, :, HEAD_DIM:] = low[2] + high[2][:TILE]
    key_ref[1, :, :HEAD_DIM] = high[1][TILE:]
    key_ref[1, :, HEAD_DIM:] = high[2][TILE:]


def attend_queries_kernel(
    length_ref, own_ref, query_far_ref, sums_ref, _, query_ref, key_ref
):
    low, high = attend_near(length_ref, query_far_ref, own_ref, 1)
    query_ref[0] = low[0]
    query_ref[1] = high[0]
    key_ref[0, :, :HEAD_DIM] = sums_ref[0, :, :HEAD_DIM] + (low[1] + high[1][:TILE])
    key_ref[0, :, HEAD_DIM:] = sums_ref[0, :, HEAD_DIM:] + (low[2] + high[2][:TILE])
    key_ref[1, :, :HEAD_DIM] = sums_ref[1, :, :HEAD_DIM] + high[1][TILE:]
    key_ref[1, :, HEAD_DIM:] = sums_ref[1, :, HEAD_DIM:] + high[2][TILE:]


def attend_keys_kernel(
    length_ref,
    own_ref,
    query_far_ref,
    key_far_ref,
    near_own_ref,
    near_far_ref,
    query_own_ref,
    query_send_ref,
    key_send_ref,
    query_acc,
    key_acc,
):
    pair, _, _ = place_of_device()
    weight = weight_of(length_ref)
    last = 1 - pair
    query_own_ref[...] = near_own_ref[...]
    query_acc[...] = near_far_ref[...]
    key_acc[1] = jnp.zeros_like(key_acc[1])
    for query_tile, key_tile in ((1, 0), (last, last)):
        queries, outs = (
            jnp.concatenate(both, axis=0)
            for both in zip(two_of(own_ref, query_tile, 0), two_of(query_far_ref, query_tile, 0))
        )
        query_part, key_part, value_part = tile_grads(
            queries, outs, *two_of(key_far_ref, key_tile, 0), weight, None
        )
        query_own_ref[query_tile] += query_part[:TILE]
        query_acc[query_tile] += query_part[TILE:]
        if key_tile is not last:
            key_acc[0, :, :HEAD_DIM] = key_part
            key_acc[0, :, HEAD_DIM:] = value_part
        else:
            key_acc[last, :, :HEAD_DIM] += key_part
            key_acc[last, :, HEAD_DIM:] += value_part
    query_send_ref[...] = query_acc[...].astype(BF16)
    key_send_ref[...] = key_acc[...].astype(BF16)


def attend_cost(tiles):
    return pl.CostEstimate(
        flops=tiles * 5 * 2 * TILE * TILE * HEAD_DIM,
        bytes_accessed=2 << 20,
        transcendentals=tiles * TILE * TILE,
    )


QUERY_SUMS = jax.ShapeDtypeStruct((2, TILE, HEAD_DIM), F32)
KEY_SUMS = jax.ShapeDtypeStruct((2, TILE, 2 * HEAD_DIM), F32)


def attend_own(length, own):
    return pl.pallas_call(
        attend_own_kernel,
        out_shape=(QUERY_SUMS, KEY_SUMS),
        in_specs=[in_smem()] + in_vmem(1),
        out_specs=tuple(in_vmem(2)),
        compiler_params=params(),
        cost_estimate=attend_cost(3),
        name="attend_own",
    )(length, own)


def attend_queries(length, own, query_far, sums, codes):
    return pl.pallas_call(
        attend_queries_kernel,
        out_shape=(QUERY_SUMS, KEY_SUMS),
        in_specs=[in_smem()] + in_vmem(3) + [pl.BlockSpec(memory_space=pl.ANY)],
        out_specs=tuple(in_vmem(2)),
        compiler_params=params(),
        cost_estimate=attend_cost(3),
        name="attend_queries",
    )(length, own, query_far, sums, codes)


def attend_keys(length, own, query_far, key_far, near_own, near_far):
    return pl.pallas_call(
        attend_keys_kernel,
        out_shape=(
            QUERY_SUMS,
            jax.ShapeDtypeStruct((2, TILE, HEAD_DIM), BF16),
            jax.ShapeDtypeStruct((2, TILE, 2 * HEAD_DIM), BF16),
        ),
        in_specs=[in_smem()] + in_vmem(5),
        out_specs=tuple(in_vmem(3)),
        scratch_shapes=[
            pltpu.VMEM((2, TILE, HEAD_DIM), F32),
            pltpu.VMEM((2, TILE, 2 * HEAD_DIM), F32),
        ],
        compiler_params=params(),
        cost_estimate=attend_cost(4),
        name="attend_keys",
    )(length, own, query_far, key_far, near_own, near_far)


def join_kernel(query_own_ref, query_got_ref, key_own_ref, key_got_ref, out_ref):
    out_ref[:, :, :HEAD_DIM] = (
        key_own_ref[:, :, HEAD_DIM:] + key_got_ref[:, :, HEAD_DIM:].astype(F32)
    ).astype(BF16)
    out_ref[:, :, HEAD_DIM : 2 * HEAD_DIM] = (
        query_own_ref[...] + query_got_ref[...].astype(F32)
    ).astype(BF16)
    out_ref[:, :, 2 * HEAD_DIM :] = (
        key_own_ref[:, :, :HEAD_DIM] + key_got_ref[:, :, :HEAD_DIM].astype(F32)
    ).astype(BF16)


def join_parts(query_own, query_got, key_own, key_got):
    return pl.pallas_call(
        join_kernel,
        out_shape=jax.ShapeDtypeStruct((2, TILE, 3 * HEAD_DIM), BF16),
        in_specs=in_vmem(4),
        out_specs=in_vmem(1)[0],
        compiler_params=params(),
        name="join_parts",
    )(query_own, query_got, key_own, key_got)


def finish_kernel(
    grads_ref,
    slope_ref,
    gate_ref,
    base_ref,
    in_proj_ref,
    slot_ref,
    code_ref,
    proj_ref,
    rows_ref,
    wide_ref,
):
    proj_ref[:, :WIDTH] = gate_ref[...]
    for block in range(3):
        joined = jnp.concatenate(
            [
                grads_ref[head, :, block * HEAD_DIM : (block + 1) * HEAD_DIM].astype(F32)
                for head in range(HEADS)
            ],
            axis=1,
        )
        cols = slice((block + 1) * WIDTH, (block + 2) * WIDTH)
        proj_ref[:, cols] = (joined * slope_ref[:, block * WIDTH : (block + 1) * WIDTH]).astype(
            BF16
        )
    input_grad = base_ref[...] + dot(proj_ref[:, WIDTH:], in_proj_ref[:, WIDTH:], MATMUL_NT)
    high = input_grad.astype(BF16)
    low = (input_grad - high.astype(F32)).astype(BF16)
    order = lax.broadcasted_iota(jnp.int32, (TABLES * CAP, 1), 0)
    within = order % HALF_SLOTS
    slot_of = ((within % FARS) * CORES + order // HALF_SLOTS) * CAP + within // FARS
    picks = (slot_ref[...] == slot_of).astype(F32).astype(BF16)
    summed = dot(picks, high, MATMUL) + dot(picks, low, MATMUL)
    for x in range(X_COUNT):
        for core in range(CORES):
            target = x * CORES + core
            wide_ref[target, :HALF_SLOTS] = summed[
                core * HALF_SLOTS : (core + 1) * HALF_SLOTS, x * QUARTER : (x + 1) * QUARTER
            ]
            wide_ref[target, HALF_SLOTS:] = code_ref[core]
    rows_ref[...] = wide_ref[...].astype(BF16)


def finish(grads, slope, gate, base, in_proj, slots, codes):
    return pl.pallas_call(
        finish_kernel,
        out_shape=(
            pltpu.VMEM((TOKENS, 4 * WIDTH), BF16),
            jax.ShapeDtypeStruct((X_COUNT * CORES, NEAR_ROWS, QUARTER), BF16),
        ),
        in_specs=in_vmem(7),
        out_specs=tuple(in_vmem(2)),
        scratch_shapes=[pltpu.VMEM((X_COUNT * CORES, NEAR_ROWS, QUARTER), F32)],
        compiler_params=params(),
        name="finish",
    )(grads, slope, gate, base, in_proj, slots, codes)


def arrange_kernel(rows_ref, out_ref, wide_ref, packed_ref):
    givers = X_COUNT * CORES
    wide_ref[...] = rows_ref[...].astype(F32)
    for giver in range(givers):
        for level in range(CAP):
            packed_ref[pl.ds(giver * CAP + level, FARS, stride=FAR_ROWS), :] = wide_ref[
                giver, level * FARS : (level + 1) * FARS
            ]
    own = lax.rem(lax.div(lax.axis_index("table"), CORES), 4)
    coded = jnp.concatenate(
        [wide_ref[giver, HALF_SLOTS : HALF_SLOTS + 1] for giver in range(givers)], axis=0
    ).T
    giver = lax.broadcasted_iota(jnp.int32, (givers, 128), 0)
    lane = lax.broadcasted_iota(jnp.int32, (givers, 128), 1)
    for part in range(2):
        row = sum(
            dot(
                coded[
                    part * HALF_SLOTS + level * FARS : part * HALF_SLOTS + (level + 1) * FARS
                ].astype(BF16),
                (lane == own * FAR_SUMS + giver * CAP + level).astype(F32).astype(BF16),
                MATMUL,
            )
            for level in range(CAP)
        )
        packed_ref[pl.ds(FAR_SUMS + part, FARS, stride=FAR_ROWS), :] = row
    for row in range(FAR_SUMS + 2, FAR_ROWS):
        packed_ref[pl.ds(row, FARS, stride=FAR_ROWS), :] = jnp.zeros((FARS, 128), F32)
    out_ref[...] = packed_ref[: FARS * FAR_ROWS].astype(BF16)


def arrange_rows(rows):
    return pl.pallas_call(
        arrange_kernel,
        out_shape=jax.ShapeDtypeStruct((FARS * FAR_ROWS, QUARTER), BF16),
        in_specs=in_vmem(1),
        out_specs=in_vmem(1)[0],
        scratch_shapes=[
            pltpu.VMEM((X_COUNT * CORES, NEAR_ROWS, QUARTER), F32),
            pltpu.VMEM(((FARS + 1) * FAR_ROWS, QUARTER), F32),
        ],
        compiler_params=params(),
        name="arrange_rows",
    )(rows)


def scatter_kernel(rows_ref, proj_ref, out_ref, proj_out, wide_ref, sem):
    copy = pltpu.make_async_copy(proj_ref.at[:HALF], proj_out.at[:HALF], sem)
    copy.start()
    targets = CTX_COUNT * ROWS_DEV
    wide_ref[...] = rows_ref[...].astype(F32)
    rows = wide_ref[:, :FAR_SUMS].reshape(FARS * FAR_SUMS, QUARTER).astype(BF16)
    ids = []
    for first in range(0, FARS, 4):
        coded = sum(wide_ref[far, FAR_SUMS : FAR_SUMS + 8] for far in range(first, first + 4))
        ids.append(coded[:1] * ROWS_DEV + coded[1:2])
    ids = jnp.concatenate(ids, axis=1).astype(jnp.int32)
    target = lax.broadcasted_iota(jnp.int32, (targets, 1), 0)
    hots = (ids == target).astype(F32).astype(BF16)
    out_ref[...] = dot(hots, rows, MATMUL).astype(BF16)
    copy.wait()


def scatter_rows(rows, proj):
    return pl.pallas_call(
        scatter_kernel,
        out_shape=(
            jax.ShapeDtypeStruct((CTX_COUNT * ROWS_DEV, QUARTER), BF16),
            jax.ShapeDtypeStruct((TOKENS, 4 * WIDTH), BF16),
        ),
        in_specs=in_vmem(2),
        out_specs=tuple(in_vmem(1) + in_hbm(1)),
        scratch_shapes=[
            pltpu.VMEM((FARS, FAR_ROWS, QUARTER), F32),
            pltpu.SemaphoreType.DMA(()),
        ],
        compiler_params=params(),
        name="scatter_rows",
    )(rows, proj)


def total_kernel(pieces_ref, proj_ref, _, total_out, proj_out, total_ref, sems):
    copy = pltpu.make_async_copy(proj_ref.at[HALF:], proj_out.at[HALF:], sems.at[0])
    copy.start()
    for x in range(X_COUNT):
        total_ref[:, x * QUARTER : (x + 1) * QUARTER] = sum(
            pieces_ref[x * Y_COUNT + y].astype(F32) for y in range(Y_COUNT)
        )
    total_copy = pltpu.make_async_copy(total_ref, total_out, sems.at[1])
    total_copy.start()
    copy.wait()
    total_copy.wait()


def total_rows(pieces, proj, proj_out):
    return pl.pallas_call(
        total_kernel,
        out_shape=(
            jax.ShapeDtypeStruct((ROWS_DEV, WIDTH), F32),
            jax.ShapeDtypeStruct((TOKENS, 4 * WIDTH), BF16),
        ),
        in_specs=in_vmem(2) + in_hbm(1),
        out_specs=tuple(in_hbm(2)),
        input_output_aliases={2: 1},
        scratch_shapes=[pltpu.VMEM((ROWS_DEV, WIDTH), F32), pltpu.SemaphoreType.DMA((2,))],
        compiler_params=params(),
        name="total_rows",
    )(pieces, proj, proj_out)


def per_device(
    item_inputs,
    attn_saved,
    out_grad,
    seq_lengths,
    token_slot,
    slot_rows,
    in_proj,
    out_proj,
    norm_gain,
):
    parts, pre, gain_grad = project(
        seq_lengths, item_inputs[0], attn_saved[0], out_grad[0], in_proj, out_proj, norm_gain[None]
    )
    own = lax.all_to_all(parts, AXES, 0, 0, axis_index_groups=HEAD_GROUPS)
    own = own.reshape(2, TILE, 4 * HEAD_DIM)
    query_far = lax.ppermute(own[:, :, : 2 * HEAD_DIM], AXES, SWAP_QUERY)
    key_far = lax.ppermute(own[:, :, 2 * HEAD_DIM :], AXES, SWAP_KEY)
    near_own, sums = attend_own(seq_lengths, own)
    slope, gate, base, codes = local_terms(pre, gain_grad, out_grad[0], in_proj, slot_rows)
    near_far, key_own = attend_queries(seq_lengths, own, query_far, sums, codes)
    query_own, query_send, key_send = attend_keys(
        seq_lengths, own, query_far, key_far, near_own, near_far
    )
    query_got = lax.ppermute(query_send, AXES, SWAP_QUERY)
    key_got = lax.ppermute(key_send, AXES, SWAP_KEY)
    joined = join_parts(query_own, query_got, key_own, key_got)
    grads = lax.all_to_all(
        joined.reshape(HEADS, TOKENS, 3 * HEAD_DIM), AXES, 0, 0, axis_index_groups=HEAD_GROUPS
    )
    proj, rows = finish(grads, slope, gate, base, in_proj, token_slot, codes)
    rows = lax.all_to_all(rows, AXES, 0, 0, axis_index_groups=X_CORE_GROUPS)
    rows = arrange_rows(rows).reshape(FARS, FAR_ROWS, QUARTER)
    rows = lax.all_to_all(rows, "table", 0, 0, axis_index_groups=FAR_GROUPS)
    dense, proj_out = scatter_rows(rows, proj)
    pieces = lax.all_to_all(dense.reshape(CTX_COUNT, ROWS_DEV, QUARTER), "ctx", 0, 0)
    table_grad, proj_grad = total_rows(pieces, proj, proj_out)
    return (proj_grad[None], table_grad)


def solution(mesh):
    return jax.shard_map(
        per_device,
        mesh=mesh,
        in_specs=(
            P("table", "ctx", None),
            P("table", "ctx", None),
            P("table", "ctx", None),
            P("table"),
            P("table", "ctx"),
            P("table", "ctx"),
            P(),
            P(),
            P(),
        ),
        out_specs=(P("table", "ctx", None), P(("ctx", "table"), None)),
        check_vma=False,
    )
```

```python
import functools

import jax
import jax.numpy as jnp
from jax import lax
from jax.experimental import pallas as pl
from jax.experimental.pallas import tpu as pltpu
from jax.sharding import PartitionSpec as P

HEADS = 4
HEAD_DIM = 128
WIDTH = 512
TOKENS = 128
ROWS_DEV = 64
TABLES = 32
CAP = 4
CORES = 2
FARS = TABLES // CORES
QUARTER = 128
HALF_SLOTS = FARS * CAP
NEAR_ROWS = HALF_SLOTS + 8
FAR_SUMS = 4 * CORES * CAP
FAR_ROWS = FAR_SUMS + 8
X_COUNT = 4
Y_COUNT = 4
HALF = TOKENS // 2
CTX_COUNT = X_COUNT * Y_COUNT
TILE = 2 * TOKENS
VMEM_LIMIT = 48 * 1024 * 1024
BF16 = jnp.bfloat16
F32 = jnp.float32

def device(x, y, table):
    return (x * Y_COUNT + y) * TABLES + table


def y_of(core, part, bit):
    return part * 2 + bit if core == 0 else bit * 2 + part


X_PAIRS = ((0, 3), (1, 2))
HEAD_GROUPS = [
    [
        device(X_PAIRS[pair][place], y_of(table % CORES, part, bit), table)
        for place in range(2)
        for bit in range(2)
    ]
    for pair in range(2)
    for part in range(2)
    for table in range(TABLES)
]
X_CORE_GROUPS = [
    [
        (x * Y_COUNT + y) * TABLES + far * CORES + core
        for x in range(X_COUNT)
        for core in range(CORES)
    ]
    for y in range(Y_COUNT)
    for far in range(FARS)
]
FAR_GROUPS = [[far * CORES + core for far in range(FARS)] for core in range(CORES)]
SWAP_QUERY = [
    (c * TABLES + t, (c ^ (2 if t % CORES == 0 else 1)) * TABLES + t)
    for c in range(CTX_COUNT)
    for t in range(TABLES)
]
SWAP_KEY = [
    (c * TABLES + t, (c ^ Y_COUNT) * TABLES + t) for c in range(CTX_COUNT) for t in range(TABLES)
]
AXES = ("ctx", "table")

MATMUL = (((1,), (0,)), ((), ()))
MATMUL_NT = (((1,), (1,)), ((), ()))
MATMUL_TN = (((0,), (0,)), ((), ()))


def dot(lhs, rhs, dims):
    return lax.dot_general(lhs, rhs, dims, preferred_element_type=F32)


def in_vmem(count):
    return [pl.BlockSpec(memory_space=pltpu.VMEM)] * count


def in_smem():
    return pl.BlockSpec(memory_space=pltpu.SMEM)


def in_hbm(count):
    return [pl.BlockSpec(memory_space=pltpu.HBM)] * count


def params(limit=VMEM_LIMIT):
    return pltpu.CompilerParams(vmem_limit_bytes=limit)


def silu(value):
    half = 0.5 * value
    return half + half * jnp.tanh(half)


def project_kernel(
    length_ref,
    inputs_hbm,
    saved_hbm,
    grad_hbm,
    in_proj_hbm,
    out_proj_hbm,
    gain_hbm,
    parts_ref,
    pre_ref,
    gain_grad_ref,
    inputs_ref,
    saved_ref,
    grad_ref,
    in_proj_ref,
    out_proj_ref,
    gain_ref,
    sems,
):
    def copy_of(place, source, target):
        copy = pltpu.make_async_copy(source, target, sems.at[place])
        copy.start()
        return copy

    saved_copy = copy_of(0, saved_hbm, saved_ref)
    grad_copy = copy_of(1, grad_hbm, grad_ref)
    gain_copy = copy_of(2, gain_hbm, gain_ref)
    out_copy = copy_of(3, out_proj_hbm, out_proj_ref)
    inputs_copy = copy_of(4, inputs_hbm, inputs_ref)
    in_copies = [
        copy_of(
            5 + block,
            in_proj_hbm.at[:, block * WIDTH : (block + 1) * WIDTH],
            in_proj_ref.at[block],
        )
        for block in range(4)
    ]
    first = lax.axis_index("ctx") * TOKENS
    length = length_ref[0]
    saved_copy.wait()
    saved = saved_ref[...].astype(F32)
    row_mean = jnp.mean(saved, axis=1, keepdims=True)
    centred = saved - row_mean
    inv_std = lax.rsqrt(jnp.mean(centred * centred, axis=1, keepdims=True) + 1e-05)
    normed = centred * inv_std
    grad_copy.wait()
    gain_copy.wait()
    out_copy.wait()
    gain = gain_ref[...]
    grad = grad_ref[...]
    back = dot(grad, out_proj_ref[...], MATMUL_NT)

    inputs_copy.wait()
    in_copies[0].wait()
    inputs = inputs_ref[...]
    pre = dot(inputs, in_proj_ref[0], MATMUL)
    pre_ref[:, :WIDTH] = pre
    gating = silu(pre).astype(BF16).astype(F32)
    gain_grad_ref[...] = back * (normed * gain)
    carried = back * gating * gain
    out_attn = inv_std * (
        carried
        - jnp.mean(carried, axis=1, keepdims=True)
        - normed * jnp.mean(carried * normed, axis=1, keepdims=True)
    )
    position = first + lax.broadcasted_iota(jnp.int32, (TOKENS, 1), 0)
    out_attn = jnp.where(position < length, out_attn, 0.0).astype(BF16)
    for head in range(HEADS):
        cols = slice(head * HEAD_DIM, (head + 1) * HEAD_DIM)
        parts_ref[head, :, HEAD_DIM : 2 * HEAD_DIM] = out_attn[:, cols]
    for block, place in ((1, 3), (2, 0), (3, 2)):
        in_copies[block].wait()
        pre = dot(inputs, in_proj_ref[block], MATMUL)
        pre_ref[:, block * WIDTH : (block + 1) * WIDTH] = pre
        hidden = silu(pre).astype(BF16)
        for head in range(HEADS):
            cols = slice(head * HEAD_DIM, (head + 1) * HEAD_DIM)
            parts_ref[head, :, place * HEAD_DIM : (place + 1) * HEAD_DIM] = hidden[:, cols]


def project(length, *arrays):
    return pl.pallas_call(
        project_kernel,
        out_shape=(
            jax.ShapeDtypeStruct((HEADS, TOKENS, 4 * HEAD_DIM), BF16),
            jax.ShapeDtypeStruct((TOKENS, 4 * WIDTH), F32),
            jax.ShapeDtypeStruct((TOKENS, WIDTH), F32),
        ),
        in_specs=[in_smem()] + in_hbm(6),
        out_specs=tuple(in_vmem(3)),
        scratch_shapes=[
            pltpu.VMEM((TOKENS, WIDTH), BF16),
            pltpu.VMEM((TOKENS, WIDTH), BF16),
            pltpu.VMEM((TOKENS, WIDTH), BF16),
            pltpu.VMEM((4, WIDTH, WIDTH), BF16),
            pltpu.VMEM((WIDTH, WIDTH), BF16),
            pltpu.VMEM((1, WIDTH), F32),
            pltpu.SemaphoreType.DMA((9,)),
        ],
        compiler_params=params(),
        name="project",
    )(length, *(pltpu.with_memory_space_constraint(array, pltpu.HBM) for array in arrays))


def local_kernel(
    pre_ref, gain_grad_ref, grad_ref, in_proj_ref, item_ref, slope_ref, gate_ref, base_ref, code_ref
):
    pre = pre_ref[...]
    squash = jax.nn.sigmoid(pre)
    slope = squash * (1.0 + pre * (1.0 - squash))
    slope_ref[...] = slope[:, WIDTH:]
    gate = (gain_grad_ref[...] * slope[:, :WIDTH]).astype(BF16)
    gate_ref[...] = gate
    base_ref[...] = grad_ref[...].astype(F32) + dot(gate, in_proj_ref[:, :WIDTH], MATMUL_NT)
    items = item_ref[...]
    owner_of = (items // (ROWS_DEV * TABLES)).astype(F32)
    place_of = (items % ROWS_DEV).astype(F32)
    slot = lax.broadcasted_iota(jnp.int32, (TABLES * CAP, 128), 0)
    lane = lax.broadcasted_iota(jnp.int32, (TABLES * CAP, 128), 1)
    wanted = lane % HALF_SLOTS
    wanted = (wanted % FARS) * (CORES * CAP) + wanted // FARS
    for core in range(CORES):
        match = slot == wanted + core * CAP
        row = sum(
            dot(
                jnp.broadcast_to(values, (8, 128)).astype(BF16),
                (match & (lane // HALF_SLOTS == part)).astype(F32).astype(BF16),
                MATMUL,
            )
            for part, values in enumerate((owner_of, place_of))
        )
        first = lax.broadcasted_iota(jnp.int32, (8, 128), 0) == 0
        code_ref[core] = jnp.where(first, row, 0.0)


def local_terms(pre, gain_grad, grad, in_proj, items):
    return pl.pallas_call(
        local_kernel,
        out_shape=(
            jax.ShapeDtypeStruct((TOKENS, 3 * WIDTH), F32),
            jax.ShapeDtypeStruct((TOKENS, WIDTH), BF16),
            jax.ShapeDtypeStruct((TOKENS, WIDTH), F32),
            jax.ShapeDtypeStruct((CORES, 8, 128), F32),
        ),
        in_specs=in_vmem(5),
        out_specs=tuple(in_vmem(4)),
        compiler_params=params(),
        cost_estimate=pl.CostEstimate(
            flops=2 * TOKENS * WIDTH * WIDTH,
            bytes_accessed=3 << 20,
            transcendentals=TOKENS * 4 * WIDTH,
        ),
        name="local_terms",
    )(pre, gain_grad, grad, in_proj, items)


def tile_grads(queries, outs, keys, values, weight, live):
    scale = HEAD_DIM ** (-0.5)
    scores = dot(keys, queries, MATMUL_NT) * scale
    attn_grad = dot(values, outs, MATMUL_NT)
    squash = 0.5 + 0.5 * jnp.tanh(scores * 0.5)
    weighted = squash * weight
    if live is not None:
        weighted = jnp.where(live, weighted, 0.0)
    gated = scores * weighted
    attend = gated.astype(BF16)
    score_grad = (attn_grad * (weighted + gated * (1.0 - squash))).astype(BF16)
    return (
        dot(score_grad, keys, MATMUL_TN) * scale,
        dot(score_grad, queries, MATMUL) * scale,
        dot(attend, outs, MATMUL),
    )


def two_of(ref, place, column):
    blocks = (slice(column, column + HEAD_DIM), slice(column + HEAD_DIM, column + 2 * HEAD_DIM))
    if place is None:
        return [ref[:, :, block].reshape(2 * TILE, HEAD_DIM) for block in blocks]
    return [ref[place, :, block] for block in blocks]


def place_of_device():
    ctx = lax.axis_index("ctx")
    x = lax.div(ctx, Y_COUNT)
    y = lax.rem(ctx, Y_COUNT)
    core = lax.rem(lax.axis_index("table"), CORES)
    part = jnp.where(core == 0, lax.div(y, 2), lax.rem(y, 2))
    return (x ^ lax.div(x, 2)) & 1, part, core


def position(index, part, core):
    halves = part * TILE + index
    parities = (index // TOKENS) * TILE + part * TOKENS + index % TOKENS
    return jnp.where(core == 0, halves, parities)


def weight_of(length_ref):
    return jnp.full((1, 1), 1.0, F32) / jnp.full((1, 1), length_ref[0].astype(F32), F32)


def attend_near(length_ref, query_ref, own_ref, flip):
    _, part, core = place_of_device()
    weight = weight_of(length_ref)
    rows = lax.broadcasted_iota(jnp.int32, (2 * TILE, 1), 0)
    rows = jnp.where(rows < TILE, -1, position(rows - TILE, part, core))
    columns = position(lax.broadcasted_iota(jnp.int32, (1, TILE), 1), part ^ flip, core)
    live = rows <= columns
    column = 2 * HEAD_DIM
    low = tile_grads(*two_of(query_ref, 0, 0), *two_of(own_ref, 0, column), weight, live[TILE:])
    high = tile_grads(*two_of(query_ref, 1, 0), *two_of(own_ref, None, column), weight, live)
    return low, high


def attend_own_kernel(length_ref, own_ref, query_ref, key_ref):
    low, high = attend_near(length_ref, own_ref, own_ref, 0)
    query_ref[0] = low[0]
    query_ref[1] = high[0]
    key_ref[0, :, :HEAD_DIM] = low[1] + high[1][:TILE]
    key_ref[0, :, HEAD_DIM:] = low[2] + high[2][:TILE]
    key_ref[1, :, :HEAD_DIM] = high[1][TILE:]
    key_ref[1, :, HEAD_DIM:] = high[2][TILE:]


def attend_queries_kernel(
    length_ref, own_ref, query_far_ref, sums_ref, _, query_ref, key_ref
):
    low, high = attend_near(length_ref, query_far_ref, own_ref, 1)
    query_ref[0] = low[0]
    query_ref[1] = high[0]
    key_ref[0, :, :HEAD_DIM] = sums_ref[0, :, :HEAD_DIM] + (low[1] + high[1][:TILE])
    key_ref[0, :, HEAD_DIM:] = sums_ref[0, :, HEAD_DIM:] + (low[2] + high[2][:TILE])
    key_ref[1, :, :HEAD_DIM] = sums_ref[1, :, :HEAD_DIM] + high[1][TILE:]
    key_ref[1, :, HEAD_DIM:] = sums_ref[1, :, HEAD_DIM:] + high[2][TILE:]


def attend_keys_kernel(
    length_ref,
    own_ref,
    query_far_ref,
    key_far_ref,
    near_own_ref,
    near_far_ref,
    query_own_ref,
    query_send_ref,
    key_send_ref,
    query_acc,
    key_acc,
):
    pair, _, _ = place_of_device()
    weight = weight_of(length_ref)
    last = 1 - pair
    query_own_ref[...] = near_own_ref[...]
    query_acc[...] = near_far_ref[...]
    key_acc[1] = jnp.zeros_like(key_acc[1])
    for query_tile, key_tile in ((1, 0), (last, last)):
        queries, outs = (
            jnp.concatenate(both, axis=0)
            for both in zip(two_of(own_ref, query_tile, 0), two_of(query_far_ref, query_tile, 0))
        )
        query_part, key_part, value_part = tile_grads(
            queries, outs, *two_of(key_far_ref, key_tile, 0), weight, None
        )
        query_own_ref[query_tile] += query_part[:TILE]
        query_acc[query_tile] += query_part[TILE:]
        if key_tile is not last:
            key_acc[0, :, :HEAD_DIM] = key_part
            key_acc[0, :, HEAD_DIM:] = value_part
        else:
            key_acc[last, :, :HEAD_DIM] += key_part
            key_acc[last, :, HEAD_DIM:] += value_part
    query_send_ref[...] = query_acc[...].astype(BF16)
    key_send_ref[...] = key_acc[...].astype(BF16)


def attend_cost(tiles):
    return pl.CostEstimate(
        flops=tiles * 5 * 2 * TILE * TILE * HEAD_DIM,
        bytes_accessed=2 << 20,
        transcendentals=tiles * TILE * TILE,
    )


QUERY_SUMS = jax.ShapeDtypeStruct((2, TILE, HEAD_DIM), F32)
KEY_SUMS = jax.ShapeDtypeStruct((2, TILE, 2 * HEAD_DIM), F32)


def attend_own(length, own):
    return pl.pallas_call(
        attend_own_kernel,
        out_shape=(QUERY_SUMS, KEY_SUMS),
        in_specs=[in_smem()] + in_vmem(1),
        out_specs=tuple(in_vmem(2)),
        compiler_params=params(),
        cost_estimate=attend_cost(3),
        name="attend_own",
    )(length, own)


def attend_queries(length, own, query_far, sums, codes):
    return pl.pallas_call(
        attend_queries_kernel,
        out_shape=(QUERY_SUMS, KEY_SUMS),
        in_specs=[in_smem()] + in_vmem(3) + [pl.BlockSpec(memory_space=pl.ANY)],
        out_specs=tuple(in_vmem(2)),
        compiler_params=params(),
        cost_estimate=attend_cost(3),
        name="attend_queries",
    )(length, own, query_far, sums, codes)


def attend_keys(length, own, query_far, key_far, near_own, near_far):
    return pl.pallas_call(
        attend_keys_kernel,
        out_shape=(
            QUERY_SUMS,
            jax.ShapeDtypeStruct((2, TILE, HEAD_DIM), BF16),
            jax.ShapeDtypeStruct((2, TILE, 2 * HEAD_DIM), BF16),
        ),
        in_specs=[in_smem()] + in_vmem(5),
        out_specs=tuple(in_vmem(3)),
        scratch_shapes=[
            pltpu.VMEM((2, TILE, HEAD_DIM), F32),
            pltpu.VMEM((2, TILE, 2 * HEAD_DIM), F32),
        ],
        compiler_params=params(),
        cost_estimate=attend_cost(4),
        name="attend_keys",
    )(length, own, query_far, key_far, near_own, near_far)


def join_kernel(query_own_ref, query_got_ref, key_own_ref, key_got_ref, out_ref):
    out_ref[:, :, :HEAD_DIM] = (
        key_own_ref[:, :, HEAD_DIM:] + key_got_ref[:, :, HEAD_DIM:].astype(F32)
    ).astype(BF16)
    out_ref[:, :, HEAD_DIM : 2 * HEAD_DIM] = (
        query_own_ref[...] + query_got_ref[...].astype(F32)
    ).astype(BF16)
    out_ref[:, :, 2 * HEAD_DIM :] = (
        key_own_ref[:, :, :HEAD_DIM] + key_got_ref[:, :, :HEAD_DIM].astype(F32)
    ).astype(BF16)


def join_parts(query_own, query_got, key_own, key_got):
    return pl.pallas_call(
        join_kernel,
        out_shape=jax.ShapeDtypeStruct((2, TILE, 3 * HEAD_DIM), BF16),
        in_specs=in_vmem(4),
        out_specs=in_vmem(1)[0],
        compiler_params=params(),
        name="join_parts",
    )(query_own, query_got, key_own, key_got)


def finish_kernel(
    grads_ref,
    slope_ref,
    gate_ref,
    base_ref,
    in_proj_ref,
    slot_ref,
    code_ref,
    proj_ref,
    rows_ref,
    wide_ref,
):
    proj_ref[:, :WIDTH] = gate_ref[...]
    for block in range(3):
        joined = jnp.concatenate(
            [
                grads_ref[head, :, block * HEAD_DIM : (block + 1) * HEAD_DIM].astype(F32)
                for head in range(HEADS)
            ],
            axis=1,
        )
        cols = slice((block + 1) * WIDTH, (block + 2) * WIDTH)
        proj_ref[:, cols] = (joined * slope_ref[:, block * WIDTH : (block + 1) * WIDTH]).astype(
            BF16
        )
    input_grad = base_ref[...] + dot(proj_ref[:, WIDTH:], in_proj_ref[:, WIDTH:], MATMUL_NT)
    high = input_grad.astype(BF16)
    low = (input_grad - high.astype(F32)).astype(BF16)
    order = lax.broadcasted_iota(jnp.int32, (TABLES * CAP, 1), 0)
    within = order % HALF_SLOTS
    slot_of = ((within % FARS) * CORES + order // HALF_SLOTS) * CAP + within // FARS
    picks = (slot_ref[...] == slot_of).astype(F32).astype(BF16)
    summed = dot(picks, high, MATMUL) + dot(picks, low, MATMUL)
    for x in range(X_COUNT):
        for core in range(CORES):
            target = x * CORES + core
            wide_ref[target, :HALF_SLOTS] = summed[
                core * HALF_SLOTS : (core + 1) * HALF_SLOTS, x * QUARTER : (x + 1) * QUARTER
            ]
            wide_ref[target, HALF_SLOTS:] = code_ref[core]
    rows_ref[...] = wide_ref[...].astype(BF16)


def finish(grads, slope, gate, base, in_proj, slots, codes):
    return pl.pallas_call(
        finish_kernel,
        out_shape=(
            pltpu.VMEM((TOKENS, 4 * WIDTH), BF16),
            jax.ShapeDtypeStruct((X_COUNT * CORES, NEAR_ROWS, QUARTER), BF16),
        ),
        in_specs=in_vmem(7),
        out_specs=tuple(in_vmem(2)),
        scratch_shapes=[pltpu.VMEM((X_COUNT * CORES, NEAR_ROWS, QUARTER), F32)],
        compiler_params=params(),
        name="finish",
    )(grads, slope, gate, base, in_proj, slots, codes)


def arrange_kernel(rows_ref, out_ref, wide_ref, packed_ref):
    givers = X_COUNT * CORES
    wide_ref[...] = rows_ref[...].astype(F32)
    for giver in range(givers):
        for level in range(CAP):
            packed_ref[pl.ds(giver * CAP + level, FARS, stride=FAR_ROWS), :] = wide_ref[
                giver, level * FARS : (level + 1) * FARS
            ]
    own = lax.rem(lax.div(lax.axis_index("table"), CORES), 4)
    coded = jnp.concatenate(
        [wide_ref[giver, HALF_SLOTS : HALF_SLOTS + 1] for giver in range(givers)], axis=0
    ).T
    giver = lax.broadcasted_iota(jnp.int32, (givers, 128), 0)
    lane = lax.broadcasted_iota(jnp.int32, (givers, 128), 1)
    for part in range(2):
        row = sum(
            dot(
                coded[
                    part * HALF_SLOTS + level * FARS : part * HALF_SLOTS + (level + 1) * FARS
                ].astype(BF16),
                (lane == own * FAR_SUMS + giver * CAP + level).astype(F32).astype(BF16),
                MATMUL,
            )
            for level in range(CAP)
        )
        packed_ref[pl.ds(FAR_SUMS + part, FARS, stride=FAR_ROWS), :] = row
    for row in range(FAR_SUMS + 2, FAR_ROWS):
        packed_ref[pl.ds(row, FARS, stride=FAR_ROWS), :] = jnp.zeros((FARS, 128), F32)
    out_ref[...] = packed_ref[: FARS * FAR_ROWS].astype(BF16)


def arrange_rows(rows):
    return pl.pallas_call(
        arrange_kernel,
        out_shape=jax.ShapeDtypeStruct((FARS * FAR_ROWS, QUARTER), BF16),
        in_specs=in_vmem(1),
        out_specs=in_vmem(1)[0],
        scratch_shapes=[
            pltpu.VMEM((X_COUNT * CORES, NEAR_ROWS, QUARTER), F32),
            pltpu.VMEM(((FARS + 1) * FAR_ROWS, QUARTER), F32),
        ],
        compiler_params=params(),
        name="arrange_rows",
    )(rows)


def scatter_kernel(rows_ref, proj_ref, out_ref, proj_out, wide_ref, sem):
    copy = pltpu.make_async_copy(proj_ref.at[:HALF], proj_out.at[:HALF], sem)
    copy.start()
    targets = CTX_COUNT * ROWS_DEV
    wide_ref[...] = rows_ref[...].astype(F32)
    rows = wide_ref[:, :FAR_SUMS].reshape(FARS * FAR_SUMS, QUARTER).astype(BF16)
    ids = []
    for first in range(0, FARS, 4):
        coded = sum(wide_ref[far, FAR_SUMS : FAR_SUMS + 8] for far in range(first, first + 4))
        ids.append(coded[:1] * ROWS_DEV + coded[1:2])
    ids = jnp.concatenate(ids, axis=1).astype(jnp.int32)
    target = lax.broadcasted_iota(jnp.int32, (targets, 1), 0)
    hots = (ids == target).astype(F32).astype(BF16)
    out_ref[...] = dot(hots, rows, MATMUL).astype(BF16)
    copy.wait()


def scatter_rows(rows, proj):
    return pl.pallas_call(
        scatter_kernel,
        out_shape=(
            jax.ShapeDtypeStruct((CTX_COUNT * ROWS_DEV, QUARTER), BF16),
            jax.ShapeDtypeStruct((TOKENS, 4 * WIDTH), BF16),
        ),
        in_specs=in_vmem(2),
        out_specs=tuple(in_vmem(1) + in_hbm(1)),
        scratch_shapes=[
            pltpu.VMEM((FARS, FAR_ROWS, QUARTER), F32),
            pltpu.SemaphoreType.DMA(()),
        ],
        compiler_params=params(),
        name="scatter_rows",
    )(rows, proj)


def total_kernel(pieces_ref, proj_ref, _, total_out, proj_out, total_ref, sems):
    copy = pltpu.make_async_copy(proj_ref.at[HALF:], proj_out.at[HALF:], sems.at[0])
    copy.start()
    for x in range(X_COUNT):
        total_ref[:, x * QUARTER : (x + 1) * QUARTER] = sum(
            pieces_ref[x * Y_COUNT + y].astype(F32) for y in range(Y_COUNT)
        )
    total_copy = pltpu.make_async_copy(total_ref, total_out, sems.at[1])
    total_copy.start()
    copy.wait()
    total_copy.wait()


def total_rows(pieces, proj, proj_out):
    return pl.pallas_call(
        total_kernel,
        out_shape=(
            jax.ShapeDtypeStruct((ROWS_DEV, WIDTH), F32),
            jax.ShapeDtypeStruct((TOKENS, 4 * WIDTH), BF16),
        ),
        in_specs=in_vmem(2) + in_hbm(1),
        out_specs=tuple(in_hbm(2)),
        input_output_aliases={2: 1},
        scratch_shapes=[pltpu.VMEM((ROWS_DEV, WIDTH), F32), pltpu.SemaphoreType.DMA((2,))],
        compiler_params=params(),
        name="total_rows",
    )(pieces, proj, proj_out)


def per_device(
    item_inputs,
    attn_saved,
    out_grad,
    seq_lengths,
    token_slot,
    slot_rows,
    in_proj,
    out_proj,
    norm_gain,
):
    parts, pre, gain_grad = project(
        seq_lengths, item_inputs[0], attn_saved[0], out_grad[0], in_proj, out_proj, norm_gain[None]
    )
    own = lax.all_to_all(parts, AXES, 0, 0, axis_index_groups=HEAD_GROUPS)
    own = own.reshape(2, TILE, 4 * HEAD_DIM)
    query_far = lax.ppermute(own[:, :, : 2 * HEAD_DIM], AXES, SWAP_QUERY)
    key_far = lax.ppermute(own[:, :, 2 * HEAD_DIM :], AXES, SWAP_KEY)
    near_own, sums = attend_own(seq_lengths, own)
    slope, gate, base, codes = local_terms(pre, gain_grad, out_grad[0], in_proj, slot_rows)
    near_far, key_own = attend_queries(seq_lengths, own, query_far, sums, codes)
    query_own, query_send, key_send = attend_keys(
        seq_lengths, own, query_far, key_far, near_own, near_far
    )
    query_got = lax.ppermute(query_send, AXES, SWAP_QUERY)
    key_got = lax.ppermute(key_send, AXES, SWAP_KEY)
    joined = join_parts(query_own, query_got, key_own, key_got)
    grads = lax.all_to_all(
        joined.reshape(HEADS, TOKENS, 3 * HEAD_DIM), AXES, 0, 0, axis_index_groups=HEAD_GROUPS
    )
    proj, rows = finish(grads, slope, gate, base, in_proj, token_slot, codes)
    rows = lax.all_to_all(rows, AXES, 0, 0, axis_index_groups=X_CORE_GROUPS)
    rows = arrange_rows(rows).reshape(FARS, FAR_ROWS, QUARTER)
    rows = lax.all_to_all(rows, "table", 0, 0, axis_index_groups=FAR_GROUPS)
    dense, proj_out = scatter_rows(rows, proj)
    pieces = lax.all_to_all(dense.reshape(CTX_COUNT, ROWS_DEV, QUARTER), "ctx", 0, 0)
    table_grad, proj_grad = total_rows(pieces, proj, proj_out)
    return (proj_grad[None], table_grad)


def solution(mesh):
    return jax.shard_map(
        per_device,
        mesh=mesh,
        in_specs=(
            P("table", "ctx", None),
            P("table", "ctx", None),
            P("table", "ctx", None),
            P("table"),
            P("table", "ctx"),
            P("table", "ctx"),
            P(),
            P(),
            P(),
        ),
        out_specs=(P("table", "ctx", None), P(("ctx", "table"), None)),
        check_vma=False,
    )
```
